512 devices in a mesh: grp: 16 (over z), seq: 32 (over y, x, core).
Axes of the slice: x: 4, y: 4, z: 16, core: 2. Of those that a mesh axis runs over, the one named last changes fastest.
Arguments:
- queries: bfloat16 [16, 4096, 1024], P('grp', 'seq'), may hold values from -36 to 36
- keys: bfloat16 [16, 4096, 1024], P('grp', 'seq'), may hold values from -36 to 36
- values: bfloat16 [16, 4096, 1024], P('grp', 'seq'), may hold values from -5 to 5
- grad_attended: bfloat16 [16, 4096, 1024], P('grp', 'seq'), may hold values from -5 to 5
- features: float32 [128, 128], replicated, may hold values from -18 to 18
- chain_lengths: int32 [16, 4], P('grp'), may hold values from 1 to 2048, 4096 in all within a row
Outputs:
- attended: bfloat16 [16, 4096, 1024], P('grp', 'seq')
- grad_queries: bfloat16 [16, 4096, 1024], P('grp', 'seq')
- grad_keys: bfloat16 [16, 4096, 1024], P('grp', 'seq')
- grad_values: bfloat16 [16, 4096, 1024], P('grp', 'seq')
The draws below stay inside these ranges and needn't reach their ends.
Inputs may be any that keep to these rules, and one draw needn't show every extreme that they name: `chain_lengths`: each row lists the lengths of its batch's 4 chains in order of position; they sum to 4096 and the largest is 2048.
All inputs are finite; a program needn't handle non-finite values.
Results may differ from the reference program's by a relative error of at most 0.0034.
Values sent between devices are 32-bit elements; how exact they have to be, the bound alone decides.
No kernel may reach another device: no remote copies, remote signals or barrier semaphores. Data moves between devices by JAX's collectives and lax.ppermute only.
A program may use at most 128 MiB of HBM per device.

```python
import math
import jax
import jax.numpy as jnp
import numpy as np
from jax import lax

H = 8
DH = 128
M = 128
GROUPS = 16
CHAINS = 4
GROUP_TOKENS = 4096
MOST = 2048


def feature_rows(key):
    base = jax.random.normal(jax.random.fold_in(key, 101), (M, DH), jnp.float32)
    return jnp.clip(base, -4.5, 4.5)


def draw_features(key, part):
    return feature_rows(key)


def draw_queries(key, part):
    key = jax.random.fold_in(key, 3)
    shape = (GROUPS, GROUP_TOKENS, H * DH)
    return jnp.clip(jax.random.normal(key, shape, jnp.float32), -4.0, 4.0).astype(jnp.bfloat16)


def draw_keys(key, part):
    key = jax.random.fold_in(key, 5)
    shape = (GROUPS, GROUP_TOKENS, H * DH)
    return jnp.clip(jax.random.normal(key, shape, jnp.float32), -4.0, 4.0).astype(jnp.bfloat16)


def steps_of(key, dims, pieces, least, top_value):
    def one(axis_at, shards_of):
        heights = jax.random.uniform(jax.random.fold_in(jax.random.fold_in(key, 6), axis_at), (shards_of,), jnp.float32, least / len(pieces), top_value / len(pieces))
        return jnp.repeat(jnp.exp(heights), dims[axis_at] // shards_of).reshape((-1,) + (1,) * (len(dims) - axis_at - 1))

    gain = one(*pieces[0])
    for cut in pieces[1:]:
        gain = gain * one(*cut)
    return gain


def profile(number_of, total, limit, lean):
    weights = [(1 << 20) // math.isqrt(standing ** lean) + 1 for standing in range(2, number_of + 1)]
    surplus, given = total - limit - (number_of - 1), [1] * (number_of - 1)
    while surplus > 0:
        movable = [i for i in range(number_of - 1) if given[i] < limit]
        pool, budget = sum([weights[i] for i in movable]), surplus
        for i in movable:
            more = min(limit - given[i], max(1, budget * weights[i] // pool), surplus)
            given[i] = given[i] + more
            surplus = surplus - more
    return np.array([limit] + given)


def uneven_parts(rng, number_of, total, bound, slope):
    if number_of == 2:
        one = jax.random.randint(rng, (), max(1, total - bound), min(bound, total - 1) + 1)
        return jnp.stack([one, total - one])
    tallies = jnp.asarray(profile(number_of, total, bound, slope), jnp.int32)
    twos = (number_of - 1) // 2
    source_of, sink = tallies[1:1 + 2 * twos:2], tallies[2:2 + 2 * twos:2]
    margin = jnp.minimum(source_of - 1, bound - sink)
    passed = jax.random.randint(jax.random.fold_in(rng, 1), (twos,), 0, 1 << 20) % (margin + 1)
    tallies = tallies.at[1:1 + 2 * twos:2].set(source_of - passed).at[2:2 + 2 * twos:2].set(sink + passed)
    return tallies[jax.random.permutation(jax.random.fold_in(rng, 2), number_of)]


def bell_draw(own_key, extent, width, reach, cuts=(), kind=jnp.bfloat16):
    factor_of = steps_of(own_key, extent, cuts, -0.22, 0.18) if cuts else 1.0
    array = jax.random.normal(own_key, extent, jnp.float32) * width * factor_of
    return jnp.minimum(jnp.maximum(array, -reach), reach).astype(kind)


def setup_inputs(seed: int = 0) -> dict:
    streams_of = jax.random.split(jax.random.key(seed), 7)
    queries = draw_queries(jax.random.fold_in(streams_of[6], 71), 0)
    keys = draw_keys(jax.random.fold_in(streams_of[6], 71), 0)
    values = bell_draw(streams_of[2], (GROUPS, GROUP_TOKENS, H * DH), 1.0, 5.0, ((0, 16), (1, 32)))
    grad_attended = bell_draw(streams_of[3], (GROUPS, GROUP_TOKENS, H * DH), 1.0, 5.0, ((0, 16), (1, 32)))
    features = draw_features(jax.random.fold_in(streams_of[6], 71), 0)
    chain_lengths = jax.vmap(lambda own: uneven_parts(own, CHAINS, GROUP_TOKENS, MOST, 2))(jax.random.split(streams_of[5], GROUPS)).reshape((GROUPS, CHAINS)).astype(jnp.int32)
    return dict(queries=queries, keys=keys, values=values, grad_attended=grad_attended, features=features, chain_lengths=chain_lengths)


exact_precision = lax.Precision.HIGHEST
epsilon = 1e-06

def feature_logits(rows, features):
    scaled = rows.reshape(rows.shape[0], H, DH) * DH ** (-0.25)
    logits = jnp.einsum('phd,md->phm', scaled, features, precision=exact_precision)
    return logits - 0.5 * lax.optimization_barrier(jnp.sum(scaled * scaled, axis=2, keepdims=True))

def reference(queries, keys, values, grad_attended, features, chain_lengths):
    ratio = M ** (-0.5)

    def group_peak(block):
        return lax.optimization_barrier(jnp.max(feature_logits(block.astype(jnp.float32), features), axis=(0, 2)))
    peak = lax.stop_gradient(lax.optimization_barrier(jnp.max(lax.map(group_peak, keys), axis=0)))

    def one_group(items):
        query_block, key_block, value_block, grad_block, lengths = items
        chain_ends = jnp.cumsum(lengths).astype(jnp.int32)
        chain_starts = (chain_ends - lengths).astype(jnp.int32)

        def forward(query_rows, key_rows, value_matrix_rows):
            query_logits = feature_logits(query_rows, features)
            row_peak = lax.stop_gradient(lax.optimization_barrier(jnp.max(query_logits, axis=2, keepdims=True)))
            query_feature_maps = (jnp.exp(query_logits - row_peak) + epsilon) * ratio
            key_feature_maps = (jnp.exp(feature_logits(key_rows, features) - peak[None, :, None]) + epsilon) * ratio
            value_heads = value_matrix_rows.reshape(GROUP_TOKENS, H, DH)

            def chain_step(total, item):
                start, length = item
                corner = jnp.minimum(start, GROUP_TOKENS - MOST).astype(jnp.int32)
                offsets = corner + jnp.arange(MOST, dtype=jnp.int32)
                inside = ((offsets >= start) & (offsets < start + length)).astype(jnp.float32)[:, None, None]
                key_slice_view = lax.dynamic_slice_in_dim(key_feature_maps, corner, MOST, 0) * inside
                value_slice_view = lax.dynamic_slice_in_dim(value_heads, corner, MOST, 0)
                query_slice_view = lax.dynamic_slice_in_dim(query_feature_maps, corner, MOST, 0)
                running_state = jnp.einsum('iyn,iyu->ynu', key_slice_view, value_slice_view, precision=exact_precision)
                summed = lax.optimization_barrier(jnp.sum(key_slice_view, axis=0))
                numerator_value = jnp.einsum('wki,kij->wkj', query_slice_view, running_state, precision=exact_precision)
                denom = jnp.einsum('phm,hm->ph', query_slice_view, summed, precision=exact_precision)
                piece = numerator_value / denom[:, :, None] * inside
                current = lax.dynamic_slice_in_dim(total, corner, MOST, 0)
                return (lax.dynamic_update_slice_in_dim(total, current + piece, corner, 0), 0)
            start_total = jnp.zeros((GROUP_TOKENS, H, DH), jnp.float32)
            total, unused = lax.scan(chain_step, start_total, (chain_starts, lengths))
            return total.reshape(GROUP_TOKENS, H * DH)
        exact, pullback = jax.vjp(forward, query_block.astype(jnp.float32), key_block.astype(jnp.float32), value_block.astype(jnp.float32))
        grads = pullback(grad_block.astype(jnp.float32))
        return (exact.astype(jnp.bfloat16), grads[0].astype(jnp.bfloat16), grads[1].astype(jnp.bfloat16), grads[2].astype(jnp.bfloat16))
    outs = lax.map(one_group, (queries, keys, values, grad_attended, chain_lengths))
    return (outs[0], outs[1], outs[2], outs[3])
```

```python
import functools

import jax
import jax.numpy as jnp
from jax import lax
from jax.experimental import pallas as pl
from jax.experimental.pallas import tpu as pltpu
from jax.sharding import PartitionSpec as P

H = 8
D = 128
M = 128
CHAINS = 4
EPS = 1e-06
SCALE = D ** (-0.25)
RATIO = M ** (-0.5)
F32 = jnp.float32
BF16 = jnp.bfloat16
NN = (((1,), (0,)), ((), ()))
NT = (((1,), (1,)), ((), ()))
TN = (((0,), (0,)), ((), ()))


def dot(a, b, dims):
    return lax.dot_general(a, b, dims, preferred_element_type=F32)


def split(x):
    hi = x.astype(BF16)
    return hi, (x - hi.astype(F32)).astype(BF16)


def split3(x):
    hi = x.astype(BF16)
    rest = x - hi.astype(F32)
    mid = rest.astype(BF16)
    return hi, mid, (rest - mid.astype(F32)).astype(BF16)


def dot3(a, b, dims):
    (ah, al), (bh, bl) = a, b
    return dot(ah, bh, dims) + (dot(ah, bl, dims) + dot(al, bh, dims))


def head(h):
    return slice(h * D, (h + 1) * D)


def logits_of(x, parts):
    f1, f2, f3 = parts
    z = dot(x, f1, NT) + (dot(x, f2, NT) + dot(x, f3, NT))
    wide = x.astype(F32)
    return SCALE * z - (0.5 * SCALE * SCALE) * jnp.sum(wide * wide, axis=1, keepdims=True)


class Chains:
    def __init__(self, lens, place, rows):
        self.rows = rows
        self.first_row = place[0] * rows
        l0, l1, l2 = lens[0, 0], lens[0, 1], lens[0, 2]
        self.starts = (jnp.int32(0), l0, l0 + l1, l0 + l1 + l2)
        self.lens = lens

    def count_ended(self, position):
        c = jnp.int32(0)
        for s in self.starts[1:]:
            c = c + (position >= s).astype(jnp.int32)
        return c

    def present(self):
        return self.count_ended(self.first_row), self.count_ended(self.first_row + self.rows - 1) + 1

    def start_of(self, c):
        s = self.starts
        return jnp.where(c == 0, s[0], jnp.where(c == 1, s[1], jnp.where(c == 2, s[2], s[3])))

    def mask(self, c, axis=0, shape=None):
        shape = (self.rows, D) if shape is None else shape
        low = self.start_of(c) - self.first_row
        at = lax.broadcasted_iota(jnp.int32, shape, axis)
        return (at >= low) & (at < low + self.lens[0, c])


def key_kernel(lens, place, k_ref, f_ref, kl_ref, pay_ref):
    rows = k_ref.shape[0]
    chains = Chains(lens, place, rows)
    parts = split3(f_ref[...])
    masks = [chains.mask(c) for c in range(CHAINS)]
    for h in range(H):
        kl = logits_of(k_ref[:, head(h)], parts)
        kl_ref[:, head(h)] = kl
        peak = jnp.max(kl, axis=(0, 1), keepdims=True)
        raised = jnp.exp(kl - peak)
        for c in range(CHAINS):
            at = c * H + h
            pay_ref[at : at + 1, :] = jnp.sum(
                jnp.where(masks[c], raised, 0.0), axis=0, keepdims=True
            )
        at = CHAINS * H + h
        pay_ref[at : at + 1, :] = jnp.broadcast_to(peak, (1, D))


def state_kernel(lens, place, kl_ref, v_ref, gp_ref, s_ref):
    rows = v_ref.shape[0]
    chains = Chains(lens, place, rows)
    s_ref[...] = jnp.zeros_like(s_ref)
    low, high = chains.present()

    def one(c, carry):
        mask = chains.mask(c)
        for h in range(H):
            raised = jnp.where(mask, jnp.exp(kl_ref[:, head(h)] - gp_ref[h : h + 1, :]), 0.0)
            hi, lo = split(raised)
            v = v_ref[:, head(h)]
            s_ref[c * H + h, :M, :] = dot(hi, v, TN) + dot(lo, v, TN)
        return carry

    lax.fori_loop(low, high, one, 0)
    row = lax.broadcasted_iota(jnp.int32, (8, rows), 0)
    hot = jnp.zeros((8, rows), F32)
    for c in range(CHAINS):
        inside = chains.mask(c, 1, (8, rows)) & (row == c)
        hot = jnp.where(inside, 1.0, hot)
    sums = dot(hot.astype(BF16), v_ref[...], NN)
    for h in range(H):
        for c in range(CHAINS):
            s_ref[c * H + h, M : M + 1, :] = sums[c : c + 1, head(h)]


def query_kernel(q_ref, f_ref, all_ref, gp_ref, qr_ref, te_ref):
    parts = split3(f_ref[...])
    for h in range(H):
        ql = logits_of(q_ref[:, head(h)], parts)
        qr_ref[:, head(h)] = jnp.exp(ql - jnp.max(ql, axis=1, keepdims=True)) * RATIO
    gp = gp_ref[...]

    def one(d, sums):
        share = jnp.exp(all_ref[d, CHAINS * H :, :] - gp)
        return tuple(sums[c] + share * all_ref[d, c * H : (c + 1) * H, :] for c in range(CHAINS))

    zero = jnp.zeros((H, D), F32)
    sums = lax.fori_loop(0, all_ref.shape[0], one, (zero,) * CHAINS)
    for c in range(CHAINS):
        te_ref[c * H : (c + 1) * H, :] = sums[c]


def back_kernel(lens, place, qr_ref, g_ref, te_ref, gp_ref, peak_ref, b_ref, t_ref, inv_ref):
    rows = g_ref.shape[0]
    chains = Chains(lens, place, rows)
    share = jnp.exp(gp_ref[...] - peak_ref[...])
    for c in range(CHAINS):
        count = lens[0, c].astype(F32)
        t_ref[c * H : (c + 1) * H, :] = RATIO * (share * te_ref[c * H : (c + 1) * H, :] + EPS * count)
    b_ref[...] = jnp.zeros_like(b_ref)
    low, high = chains.present()

    def one(c, carry):
        mask = chains.mask(c)
        for h in range(H):
            qf = qr_ref[:, head(h)] + EPS * RATIO
            total = t_ref[pl.ds(c * H + h, 1), :]
            inv = 1.0 / jnp.sum(qf * total, axis=1, keepdims=True)
            hi, lo = split(jnp.where(mask, qf * inv, 0.0))
            g = g_ref[:, head(h)]
            b_ref[c * H + h] = dot(hi, g, TN) + dot(lo, g, TN)
            inv_ref[:, head(h)] = jnp.where(mask, inv, inv_ref[:, head(h)])
        return carry

    lax.fori_loop(low, high, one, 0)


def query_out_kernel(
    lens, place, qr_ref, q_ref, g_ref, f_ref, s_ref, t_ref, inv_ref, gp_ref, peak_ref,
    out_ref, gq_ref, bt_ref, num_ref, gs_ref, tr_ref,
):
    rows = g_ref.shape[0]
    chains = Chains(lens, place, rows)
    share = jnp.exp(gp_ref[...] - peak_ref[...])
    low, high = chains.present()

    def one(c, carry):
        mask = chains.mask(c)
        for h in range(H):
            at = head(h)
            value_sum = s_ref[c * H + h, M : M + 1, :]
            state = RATIO * (share[h : h + 1, :] * s_ref[c * H + h, :M, :] + EPS * value_sum)
            state = split(state)
            num = dot3(split(qr_ref[:, at] + EPS * RATIO), state, NN)
            g = g_ref[:, at]
            gs = dot(g, state[0], NT) + dot(g, state[1], NT)
            num_ref[:, at] = jnp.where(mask, num, num_ref[:, at])
            gs_ref[:, at] = jnp.where(mask, gs, gs_ref[:, at])
            tr_ref[:, at] = jnp.where(mask, t_ref[pl.ds(c * H + h, 1), :], tr_ref[:, at])
        return carry

    lax.fori_loop(low, high, one, 0)
    masks = [chains.mask(c) for c in range(CHAINS)]
    feats = split(f_ref[...])
    for h in range(H):
        at = head(h)
        inv = inv_ref[:, at]
        exact = num_ref[:, at] * inv
        out_ref[:, at] = exact.astype(BF16)
        grad_denom = -jnp.sum(g_ref[:, at].astype(F32) * exact, axis=1, keepdims=True) * inv
        raised = qr_ref[:, at]
        weighted = (raised + EPS * RATIO) * grad_denom
        for c in range(CHAINS):
            bt_ref[c * H + h : c * H + h + 1, :] = jnp.sum(
                jnp.where(masks[c], weighted, 0.0), axis=0, keepdims=True
            )
        grad_logits = (gs_ref[:, at] * inv + grad_denom * tr_ref[:, at]) * raised
        back = dot3(split(grad_logits), feats, NN)
        back = back - jnp.sum(grad_logits, axis=1, keepdims=True) * (SCALE * q_ref[:, at].astype(F32))
        gq_ref[:, at] = (back * SCALE).astype(BF16)


def key_out_kernel(
    lens, place, kl_ref, k_ref, v_ref, f_ref, b_ref, all_ref, peak_ref,
    gk_ref, gv_ref, dk_ref, dv_ref, bt_ref,
):
    rows = v_ref.shape[0]
    chains = Chains(lens, place, rows)
    bt_ref[...] = jnp.sum(all_ref[...], axis=0)
    low, high = chains.present()

    def one(c, carry):
        mask = chains.mask(c)
        for h in range(H):
            at = head(h)
            state = split(b_ref[c * H + h])
            feats = jnp.exp(kl_ref[:, at] - peak_ref[h : h + 1, :]) * RATIO + EPS * RATIO
            dv = dot3(split(feats), state, NN)
            v = v_ref[:, at]
            dk = dot(v, state[0], NT) + dot(v, state[1], NT) + bt_ref[pl.ds(c * H + h, 1), :]
            dv_ref[:, at] = jnp.where(mask, dv, dv_ref[:, at])
            dk_ref[:, at] = jnp.where(mask, dk, dk_ref[:, at])
        return carry

    lax.fori_loop(low, high, one, 0)
    feats = split(f_ref[...])
    for h in range(H):
        at = head(h)
        gv_ref[:, at] = dv_ref[:, at].astype(BF16)
        grad_logits = dk_ref[:, at] * (jnp.exp(kl_ref[:, at] - peak_ref[h : h + 1, :]) * RATIO)
        back = dot3(split(grad_logits), feats, NN)
        back = back - jnp.sum(grad_logits, axis=1, keepdims=True) * (SCALE * k_ref[:, at].astype(F32))
        gk_ref[:, at] = (back * SCALE).astype(BF16)


def call(kernel, shapes, args, scalars=0, scratch=(), flops=10**8):
    vmem = pl.BlockSpec(memory_space=pltpu.VMEM)
    smem = pl.BlockSpec(memory_space=pltpu.SMEM)
    size = sum(a.size * a.dtype.itemsize for a in args)
    return pl.pallas_call(
        kernel,
        out_shape=shapes,
        in_specs=[smem] * scalars + [vmem] * (len(args) - scalars),
        out_specs=[vmem] * len(shapes),
        scratch_shapes=list(scratch),
        compiler_params=pltpu.CompilerParams(vmem_limit_bytes=40 * 2**20),
        cost_estimate=pl.CostEstimate(flops=flops, bytes_accessed=size, transcendentals=10**5),
    )(*args)


def max_over(x, axis):
    count = lax.axis_size(axis)
    span = 1
    while span < count:
        steps = range(span, min(4 * span, count), span)
        others = [
            lax.ppermute(x, axis, [(i, (i + s) % count) for i in range(count)]) for s in steps
        ]
        for other in others:
            x = jnp.maximum(x, other)
        span *= 4
    return x


def on_device(queries, keys, values, grad_attended, features, chain_lengths):
    rows, width = queries.shape[1:]
    q, k, v, g = (a.reshape(rows, width) for a in (queries, keys, values, grad_attended))
    place = lax.axis_index("seq").astype(jnp.int32).reshape(1)
    where = (chain_lengths, place)
    lots = CHAINS * H
    wide = jax.ShapeDtypeStruct((rows, width), F32)
    narrow = jax.ShapeDtypeStruct((rows, width), BF16)
    small = jax.ShapeDtypeStruct((lots, D), F32)
    logits, payload = call(
        key_kernel, [wide, jax.ShapeDtypeStruct((lots + H, D), F32)], (*where, k, features), 2
    )
    gathered = lax.all_gather(payload, "seq")
    group_peak = jnp.max(gathered[:, lots:, :], axis=0)
    (states,) = call(
        state_kernel, [jax.ShapeDtypeStruct((lots, M + 8, D), F32)], (*where, logits, v, group_peak), 2
    )
    states = lax.psum_scatter(states, "seq", scatter_dimension=0, tiled=True)
    states = lax.all_gather(states, "seq", tiled=True)
    peak = max_over(group_peak, "grp")
    raised, sums = call(query_kernel, [wide, small], (q, features, gathered, group_peak))
    backs, totals, inverse = call(
        back_kernel,
        [jax.ShapeDtypeStruct((lots, M, D), F32), small, wide],
        (*where, raised, g, sums, group_peak, peak),
        2,
    )
    backs = lax.psum(backs, "seq")
    scratch = pltpu.VMEM((rows, width), F32)
    attended, grad_queries, back_totals = call(
        query_out_kernel,
        [narrow, narrow, small],
        (*where, raised, q, g, features, states, totals, inverse, group_peak, peak),
        2,
        [scratch] * 3,
    )
    back_totals = lax.all_gather(back_totals, "seq")
    grad_keys, grad_values = call(
        key_out_kernel,
        [narrow, narrow],
        (*where, logits, k, v, features, backs, back_totals, peak),
        2,
        [scratch] * 2 + [pltpu.VMEM((lots, D), F32)],
    )
    return tuple(a.reshape(1, rows, width) for a in (attended, grad_queries, grad_keys, grad_values))


def solution(mesh):
    rows = P("grp", "seq", None)
    return jax.shard_map(
        on_device,
        mesh=mesh,
        in_specs=(rows, rows, rows, rows, P(), P("grp", None)),
        out_specs=(rows, rows, rows, rows),
        check_vma=False,
    )
```

```python
import jax
import jax.numpy as jnp
from jax import lax
from jax.experimental import pallas as pl
from jax.experimental.pallas import tpu as pltpu
from jax.sharding import Mesh
from jax.sharding import PartitionSpec as P

H = 8
D = 128
M = 128
CHAINS = 4
EPS = 1e-06
SCALE = D ** (-0.25)
RATIO = M ** (-0.5)
F32 = jnp.float32
BF16 = jnp.bfloat16
NN = (((1,), (0,)), ((), ()))
NT = (((1,), (1,)), ((), ()))
TN = (((0,), (0,)), ((), ()))
K, V, Q, G = range(4)
OUT, GQ, GK, GV = range(4)


def dot(a, b, dims):
    return lax.dot_general(a, b, dims, preferred_element_type=F32)


def split(x):
    hi = x.astype(BF16)
    return hi, (x - hi.astype(F32)).astype(BF16)


def split3(x):
    hi = x.astype(BF16)
    rest = x - hi.astype(F32)
    mid = rest.astype(BF16)
    return hi, mid, (rest - mid.astype(F32)).astype(BF16)


def dot3(a, b, dims):
    (ah, al), (bh, bl) = a, b
    return dot(ah, bh, dims) + (dot(ah, bl, dims) + dot(al, bh, dims))


def head(h):
    return slice(h * D, (h + 1) * D)


def logits_of(x, parts):
    f1, f2, f3 = parts
    y = x.astype(BF16)
    z = dot(y, f1, NT) + (dot(y, f2, NT) + dot(y, f3, NT))
    return SCALE * z - (0.5 * SCALE * SCALE) * jnp.sum(x * x, axis=1, keepdims=True)


class Chains:
    def __init__(self, lens, place, blocks, rows):
        self.rows = rows
        self.span = blocks * rows
        self.me = place[0]
        l0, l1, l2 = lens[0, 0], lens[0, 1], lens[0, 2]
        self.starts = (jnp.int32(0), l0, l0 + l1, l0 + l1 + l2)
        self.lens = lens

    def count_ended(self, position):
        c = jnp.int32(0)
        for s in self.starts[1:]:
            c = c + (position >= s).astype(jnp.int32)
        return c

    def ends_of(self, which):
        return self.count_ended(which * self.span), self.count_ended((which + 1) * self.span - 1)

    def start_of(self, c):
        s = self.starts
        return jnp.where(c == 0, s[0], jnp.where(c == 1, s[1], jnp.where(c == 2, s[2], s[3])))

    def mask(self, c, block):
        low = self.start_of(c) - (self.me * self.span + block * self.rows)
        at = lax.broadcasted_iota(jnp.int32, (self.rows, D), 0)
        return (at >= low) & (at < low + self.lens[0, c])


def pack_kernel(k_ref, v_ref, q_ref, g_ref, out_ref):
    for h in range(H):
        for i, ref in enumerate((k_ref, v_ref, q_ref, g_ref)):
            out_ref[h, i] = ref[:, head(h)].astype(F32)


def logit_kernel(lens, place, all_ref, f_ref, kl_ref, qr_ref, pay_ref):
    blocks, _, rows, _ = all_ref.shape
    chains = Chains(lens, place, blocks, rows)
    parts = split3(f_ref[...])
    for b in range(blocks):
        kl_ref[b] = logits_of(all_ref[b, K], parts)
    peak = jnp.max(jnp.max(kl_ref[...], axis=0), axis=(0, 1), keepdims=True)
    pay_ref[...] = jnp.broadcast_to(peak, pay_ref.shape)
    low, high = chains.ends_of(chains.me)

    pay_ref[0:CHAINS, :] = jnp.zeros((CHAINS, M), F32)

    def one(c, carry):
        total = jnp.zeros((rows, M), F32)
        for b in range(blocks):
            total = total + jnp.where(chains.mask(c, b), jnp.exp(kl_ref[b] - peak), 0.0)
        pay_ref[pl.ds(c, 1), :] = jnp.sum(total, axis=0, keepdims=True)
        return carry

    lax.fori_loop(low, high + 1, one, 0)
    for b in range(blocks):
        ql = logits_of(all_ref[b, Q], parts)
        qr_ref[b] = jnp.exp(ql - jnp.max(ql, axis=1, keepdims=True)) * RATIO


def state_kernel(
    lens, place, all_ref, kl_ref, qr_ref, pay_ref,
    kr_ref, inv_ref, t_ref, s_ref, b_ref, s_send, b_send,
):
    blocks, _, rows, _ = all_ref.shape
    chains = Chains(lens, place, blocks, rows)
    lots = pay_ref.shape[1]
    peaks = pay_ref[:, :, CHAINS : CHAINS + 1, :]
    peak = jnp.max(peaks, axis=(0, 1)).reshape(1, M)
    total = jnp.zeros((CHAINS, M), F32)
    for r in range(lots):
        mine = pay_ref[place[1], r]
        total = total + jnp.exp(mine[CHAINS : CHAINS + 1, :] - peak) * mine[:CHAINS, :]
    for c in range(CHAINS):
        count = lens[0, c].astype(F32)
        t_ref[c : c + 1, :] = RATIO * (total[c : c + 1, :] + EPS * count)
    for b in range(blocks):
        kr_ref[b] = jnp.exp(kl_ref[b] - peak) * RATIO
    s_ref[...] = jnp.zeros_like(s_ref)
    b_ref[...] = jnp.zeros_like(b_ref)
    low, high = chains.ends_of(chains.me)

    def one(c, carry):
        state = jnp.zeros((M, D), F32)
        back = jnp.zeros((M, D), F32)
        weights = t_ref[pl.ds(c, 1), :]
        for b in range(blocks):
            mask = chains.mask(c, b)
            hi, lo = split(jnp.where(mask, kr_ref[b] + EPS * RATIO, 0.0))
            v = all_ref[b, V].astype(BF16)
            state = state + (dot(hi, v, TN) + dot(lo, v, TN))
            qf = qr_ref[b] + EPS * RATIO
            inv = 1.0 / jnp.sum(qf * weights, axis=1, keepdims=True)
            hi, lo = split(jnp.where(mask, qf * inv, 0.0))
            g = all_ref[b, G].astype(BF16)
            back = back + (dot(hi, g, TN) + dot(lo, g, TN))
            inv_ref[b] = jnp.where(mask, inv, inv_ref[b])
        s_ref[c] = state
        b_ref[c] = back
        return carry

    lax.fori_loop(low, high + 1, one, 0)
    other = (high != low).astype(F32)
    s_send[0] = s_ref[low]
    b_send[0] = b_ref[low]
    s_send[1] = s_ref[high] * other
    b_send[1] = b_ref[high] * other


def add_rows(chains, full_ref, own_ref, sent_ref):
    full_ref[...] = own_ref[...]
    for r in range(sent_ref.shape[0]):
        low, high = chains.ends_of(r)

        @pl.when(chains.me != r)
        def _():
            full_ref[low] += sent_ref[r, 0]
            full_ref[high] += sent_ref[r, 1]


def middle_kernel(
    lens, place, all_ref, f_ref, qr_ref, kr_ref, inv_ref, t_ref, s_ref, b_ref, s_sent, b_sent,
    res_ref, dk_ref, bt_ref, s_full, b_full, num_ref, gs_ref, tr_ref,
):
    blocks, _, rows, _ = all_ref.shape
    chains = Chains(lens, place, blocks, rows)
    add_rows(chains, s_full, s_ref, s_sent)
    add_rows(chains, b_full, b_ref, b_sent)
    low, high = chains.ends_of(chains.me)

    def one(c, carry):
        state = split(s_full[c])
        back = split(b_full[c])
        for b in range(blocks):
            mask = chains.mask(c, b)
            num = dot3(split(qr_ref[b] + EPS * RATIO), state, NN)
            num_ref[b] = jnp.where(mask, num, num_ref[b])
            g = all_ref[b, G].astype(BF16)
            gs = dot(g, state[0], NT) + dot(g, state[1], NT)
            gs_ref[b] = jnp.where(mask, gs, gs_ref[b])
            tr_ref[b] = jnp.where(mask, t_ref[pl.ds(c, 1), :], tr_ref[b])
            dv = dot3(split(kr_ref[b] + EPS * RATIO), back, NN)
            res_ref[b, GV] = jnp.where(mask, dv, res_ref[b, GV])
            v = all_ref[b, V].astype(BF16)
            dk = dot(v, back[0], NT) + dot(v, back[1], NT)
            dk_ref[b] = jnp.where(mask, dk, dk_ref[b])
        return carry

    lax.fori_loop(low, high + 1, one, 0)
    feats = split(f_ref[...])
    for b in range(blocks):
        inv = inv_ref[b]
        exact = num_ref[b] * inv
        res_ref[b, OUT] = exact
        res_ref[b, GK] = exact
        grad_denom = -jnp.sum(all_ref[b, G] * exact, axis=1, keepdims=True) * inv
        raised = qr_ref[b]
        num_ref[b] = (raised + EPS * RATIO) * grad_denom
        grad_logits = (gs_ref[b] * inv + grad_denom * tr_ref[b]) * raised
        back = dot3(split(grad_logits), feats, NN)
        back = back - jnp.sum(grad_logits, axis=1, keepdims=True) * (SCALE * all_ref[b, Q])
        res_ref[b, GQ] = back * SCALE
    bt_ref[...] = jnp.zeros_like(bt_ref)

    def two(c, carry):
        total = jnp.zeros((rows, M), F32)
        for b in range(blocks):
            total = total + jnp.where(chains.mask(c, b), num_ref[b], 0.0)
        bt_ref[pl.ds(c, 1), :] = jnp.sum(total, axis=0, keepdims=True)
        return carry

    lax.fori_loop(low, high + 1, two, 0)


def key_kernel(lens, place, all_ref, f_ref, kr_ref, dk_ref, res_in, bt_ref, res_ref, sum_ref, add_ref):
    blocks, _, rows, _ = all_ref.shape
    chains = Chains(lens, place, blocks, rows)
    sum_ref[...] = jnp.sum(bt_ref[...], axis=0)
    low, high = chains.ends_of(chains.me)

    def one(c, carry):
        for b in range(blocks):
            add_ref[b] = jnp.where(chains.mask(c, b), sum_ref[pl.ds(c, 1), :], add_ref[b])
        return carry

    lax.fori_loop(low, high + 1, one, 0)
    feats = split(f_ref[...])
    for b in range(blocks):
        for i in (OUT, GQ, GV):
            res_ref[b, i] = res_in[b, i]
        grad_logits = (dk_ref[b] + add_ref[b]) * kr_ref[b]
        back = dot3(split(grad_logits), feats, NN)
        back = back - jnp.sum(grad_logits, axis=1, keepdims=True) * (SCALE * all_ref[b, K])
        res_ref[b, GK] = back * SCALE


def unpack_kernel(res_ref, out_ref, gq_ref, gk_ref, gv_ref):
    for h in range(H):
        for i, ref in ((OUT, out_ref), (GQ, gq_ref), (GK, gk_ref), (GV, gv_ref)):
            ref[:, head(h)] = res_ref[h, i].astype(BF16)


def call(kernel, shapes, args, scalars=0, scratch=()):
    vmem = pl.BlockSpec(memory_space=pltpu.VMEM)
    smem = pl.BlockSpec(memory_space=pltpu.SMEM)
    return pl.pallas_call(
        kernel,
        out_shape=shapes,
        in_specs=[smem] * scalars + [vmem] * (len(args) - scalars),
        out_specs=[vmem] * len(shapes),
        scratch_shapes=list(scratch),
        compiler_params=pltpu.CompilerParams(vmem_limit_bytes=40 * 2**20),
    )(*args)


def f32(*shape):
    return jax.ShapeDtypeStruct(shape, F32)


def on_device(queries, keys, values, grad_attended, features, chain_lengths):
    rows, width = queries.shape[1:]
    q, k, v, g = (a.reshape(rows, width) for a in (queries, keys, values, grad_attended))
    place = jnp.stack([lax.axis_index("row"), lax.axis_index("grp")]).astype(jnp.int32)
    where = (chain_lengths, place)
    blocks = lax.axis_size("col")
    wide = (blocks, rows, D)
    (packed,) = call(pack_kernel, [f32(H, 4, rows, D)], (k, v, q, g))
    own = lax.all_to_all(packed, "col", 0, 0, tiled=True)
    logits, raised, payload = call(
        logit_kernel, [f32(*wide), f32(*wide), f32(2 * CHAINS, M)], (*where, own, features), 2
    )
    payload = lax.all_gather(payload, ("grp", "row"))
    payload = payload.reshape(lax.axis_size("grp"), lax.axis_size("row"), 2 * CHAINS, M)
    lots = (CHAINS, M, D)
    key_raised, inverse, totals, states, backs, state_ends, back_ends = call(
        state_kernel,
        [f32(*wide), f32(*wide), f32(CHAINS, M), f32(*lots), f32(*lots), f32(2, M, D), f32(2, M, D)],
        (*where, own, logits, raised, payload),
        2,
    )
    state_ends = lax.all_gather(state_ends, "row")
    back_ends = lax.all_gather(back_ends, "row")
    results, grad_feats, back_totals = call(
        middle_kernel,
        [f32(blocks, 4, rows, D), f32(*wide), f32(2 * CHAINS, M)],
        (*where, own, features, raised, key_raised, inverse, totals, states, backs, state_ends, back_ends),
        2,
        [pltpu.VMEM(lots, F32)] * 2 + [pltpu.VMEM(wide, F32)] * 3,
    )
    back_totals = lax.all_gather(back_totals, "row")
    (results,) = call(
        key_kernel,
        [f32(blocks, 4, rows, D)],
        (*where, own, features, key_raised, grad_feats, results, back_totals),
        2,
        [pltpu.VMEM((2 * CHAINS, M), F32), pltpu.VMEM(wide, F32)],
    )
    results = lax.all_to_all(results, "col", 0, 0, tiled=True)
    outs = call(unpack_kernel, [jax.ShapeDtypeStruct((rows, width), BF16)] * 4, (results,))
    return tuple(a.reshape(1, rows, width) for a in outs)


def solution(mesh):
    groups, seq = mesh.devices.shape
    fine = Mesh(mesh.devices.reshape(groups, seq // H, H), ("grp", "row", "col"))
    rows = P("grp", ("row", "col"), None)
    return jax.shard_map(
        on_device,
        mesh=fine,
        in_specs=(rows, rows, rows, rows, P(), P("grp", None)),
        out_specs=(rows, rows, rows, rows),
        check_vma=False,
    )
```

```python
import jax
import jax.numpy as jnp
from jax import lax
from jax.experimental import pallas as pl
from jax.experimental.pallas import tpu as pltpu
from jax.sharding import Mesh
from jax.sharding import PartitionSpec as P

H = 8
D = 128
M = 128
CHAINS = 4
EPS = 1e-06
SCALE = D ** (-0.25)
RATIO = M ** (-0.5)
F32 = jnp.float32
BF16 = jnp.bfloat16
NN = (((1,), (0,)), ((), ()))
NT = (((1,), (1,)), ((), ()))
TN = (((0,), (0,)), ((), ()))
K, V, Q, G = range(4)
OUT, GQ, GV = range(3)


def dot(a, b, dims):
    return lax.dot_general(a, b, dims, preferred_element_type=F32)


def split(x):
    hi = x.astype(BF16)
    return hi, (x - hi.astype(F32)).astype(BF16)


def split3(x):
    hi = x.astype(BF16)
    rest = x - hi.astype(F32)
    mid = rest.astype(BF16)
    return hi, mid, (rest - mid.astype(F32)).astype(BF16)


def dot3(a, b, dims):
    (ah, al), (bh, bl) = a, b
    return dot(ah, bh, dims) + (dot(ah, bl, dims) + dot(al, bh, dims))


def head(h):
    return slice(h * D, (h + 1) * D)


def logits_of(x, parts):
    f1, f2, f3 = parts
    y = x.astype(BF16)
    z = dot(y, f1, NT) + (dot(y, f2, NT) + dot(y, f3, NT))
    return SCALE * z - (0.5 * SCALE * SCALE) * jnp.sum(x * x, axis=1, keepdims=True)


class Chains:
    def __init__(self, lens, place, blocks, rows):
        self.rows = rows
        self.span = blocks * rows
        self.me = place[0]
        l0, l1, l2 = lens[0, 0], lens[0, 1], lens[0, 2]
        self.starts = (jnp.int32(0), l0, l0 + l1, l0 + l1 + l2)
        self.lens = lens

    def count_ended(self, position):
        c = jnp.int32(0)
        for s in self.starts[1:]:
            c = c + (position >= s).astype(jnp.int32)
        return c

    def ends_of(self, which):
        return self.count_ended(which * self.span), self.count_ended((which + 1) * self.span - 1)

    def start_of(self, c):
        s = self.starts
        return jnp.where(c == 0, s[0], jnp.where(c == 1, s[1], jnp.where(c == 2, s[2], s[3])))

    def mask(self, c, block):
        low = self.start_of(c) - (self.me * self.span + block * self.rows)
        at = lax.broadcasted_iota(jnp.int32, (self.rows, D), 0)
        return (at >= low) & (at < low + self.lens[0, c])


def pack_kernel(f_ref, k_hbm, v_hbm, q_hbm, g_hbm, out_hbm, peak_ref, rows_ref, wide_ref, in_sem, out_sem):
    sources = (k_hbm, v_hbm, q_hbm, g_hbm)
    loads = [pltpu.make_async_copy(r, rows_ref.at[i], in_sem.at[i]) for i, r in enumerate(sources)]
    for load in loads:
        load.start()
    for load in loads:
        load.wait()
    stores = [pltpu.make_async_copy(wide_ref.at[h], out_hbm.at[h], out_sem.at[h]) for h in range(H)]
    for h in range(H):
        for i in range(4):
            wide_ref[h, i] = rows_ref[i, :, head(h)].astype(F32)
        stores[h].start()
    parts = split3(f_ref[...])
    for h in range(H):
        logits = logits_of(rows_ref[K, :, head(h)].astype(F32), parts)
        peak = jnp.broadcast_to(jnp.max(logits, axis=(0, 1), keepdims=True), (1, M))
        peak_ref[0, h : h + 1, :] = peak
    for r in range(1, peak_ref.shape[0]):
        peak_ref[r] = peak_ref[0]
    for store in stores:
        store.wait()


def logit_kernel(lens, place, all_ref, f_ref, z_ref, kl_ref, qr_ref, pay_ref):
    blocks, _, rows, _ = all_ref.shape
    chains = Chains(lens, place, blocks, rows)
    parts = split3(f_ref[...])
    for b in range(blocks):
        kl_ref[b] = logits_of(all_ref[b, K], parts)
    peak = jnp.max(jnp.max(kl_ref[...], axis=0), axis=(0, 1), keepdims=True)
    low, high = chains.ends_of(chains.me)
    pay_ref[0] = jnp.zeros((2 * CHAINS, M), F32)
    pay_ref[0, CHAINS : CHAINS + 1, :] = jnp.broadcast_to(peak, (1, M))

    def one(c, carry):
        total = jnp.zeros((rows, M), F32)
        for b in range(blocks):
            total = total + jnp.where(chains.mask(c, b), jnp.exp(kl_ref[b] - peak), 0.0)
        pay_ref[0, pl.ds(c, 1), :] = jnp.sum(total, axis=0, keepdims=True)
        return carry

    lax.fori_loop(low, high + 1, one, 0)
    peaks = jnp.max(z_ref[...], axis=0)
    for i in range(1, pay_ref.shape[0]):
        h = i % H
        pay_ref[i] = pay_ref[0]
        pay_ref[i, CHAINS + 1 : CHAINS + 2, :] = peaks[h : h + 1, :]
    pay_ref[0, CHAINS + 1 : CHAINS + 2, :] = peaks[0:1, :]
    for b in range(blocks):
        ql = logits_of(all_ref[b, Q], parts)
        qr_ref[b] = jnp.exp(ql - jnp.max(ql, axis=1, keepdims=True)) * RATIO


def state_kernel(
    lens, place, all_ref, kl_ref, qr_ref, pay_ref,
    kr_ref, inv_ref, t_ref, s_ref, b_ref, send_ref,
):
    blocks, _, rows, _ = all_ref.shape
    chains = Chains(lens, place, blocks, rows)
    everyone = pay_ref.shape[0]
    peak = jnp.max(pay_ref[...], axis=0)[CHAINS + 1 : CHAINS + 2, :]
    total = jnp.zeros((CHAINS, M), F32)
    for r in range(everyone // H):
        mine = pay_ref[r * H + place[1]]
        total = total + jnp.exp(mine[CHAINS : CHAINS + 1, :] - peak) * mine[:CHAINS, :]
    for c in range(CHAINS):
        count = lens[0, c].astype(F32)
        t_ref[c : c + 1, :] = RATIO * (total[c : c + 1, :] + EPS * count)
    for b in range(blocks):
        kr_ref[b] = jnp.exp(kl_ref[b] - peak) * RATIO
    s_ref[...] = jnp.zeros_like(s_ref)
    b_ref[...] = jnp.zeros_like(b_ref)
    low, high = chains.ends_of(chains.me)

    def one(c, carry):
        state = jnp.zeros((M, D), F32)
        back = jnp.zeros((M, D), F32)
        weights = t_ref[pl.ds(c, 1), :]
        for b in range(blocks):
            mask = chains.mask(c, b)
            hi, lo = split(jnp.where(mask, kr_ref[b] + EPS * RATIO, 0.0))
            v = all_ref[b, V].astype(BF16)
            state = state + (dot(hi, v, TN) + dot(lo, v, TN))
            qf = qr_ref[b] + EPS * RATIO
            inv = 1.0 / jnp.sum(qf * weights, axis=1, keepdims=True)
            hi, lo = split(jnp.where(mask, qf * inv, 0.0))
            g = all_ref[b, G].astype(BF16)
            back = back + (dot(hi, g, TN) + dot(lo, g, TN))
            inv_ref[b] = jnp.where(mask, inv, inv_ref[b])
        s_ref[c] = state
        b_ref[c] = back
        return carry

    lax.fori_loop(low, high + 1, one, 0)
    other = (high != low).astype(F32)
    for r in range(send_ref.shape[0]):
        for i, ref in ((0, s_ref), (1, b_ref)):
            send_ref[r, i, 0] = ref[low]
            send_ref[r, i, 1] = ref[high] * other


def add_rows(chains, full_ref, own_ref, sent_ref, which):
    full_ref[...] = own_ref[...]
    for r in range(sent_ref.shape[0]):
        low, high = chains.ends_of(r)

        @pl.when(chains.me != r)
        def _():
            full_ref[low] += sent_ref[r, which, 0]
            full_ref[high] += sent_ref[r, which, 1]


def middle_kernel(
    lens, place, all_ref, f_ref, qr_ref, kr_ref, inv_ref, t_ref, s_ref, b_ref, sent_ref,
    res_ref, dk_ref, bt_ref, s_full, b_full, num_ref, gs_ref, tr_ref,
):
    blocks, _, rows, _ = all_ref.shape
    chains = Chains(lens, place, blocks, rows)
    add_rows(chains, s_full, s_ref, sent_ref, 0)
    add_rows(chains, b_full, b_ref, sent_ref, 1)
    low, high = chains.ends_of(chains.me)

    def one(c, carry):
        state = split(s_full[c])
        back = split(b_full[c])
        for b in range(blocks):
            mask = chains.mask(c, b)
            num = dot3(split(qr_ref[b] + EPS * RATIO), state, NN)
            num_ref[b] = jnp.where(mask, num, num_ref[b])
            g = all_ref[b, G].astype(BF16)
            gs = dot(g, state[0], NT) + dot(g, state[1], NT)
            gs_ref[b] = jnp.where(mask, gs, gs_ref[b])
            tr_ref[b] = jnp.where(mask, t_ref[pl.ds(c, 1), :], tr_ref[b])
            dv = dot3(split(kr_ref[b] + EPS * RATIO), back, NN)
            res_ref[b, GV] = jnp.where(mask, dv, res_ref[b, GV])
            v = all_ref[b, V].astype(BF16)
            dk = dot(v, back[0], NT) + dot(v, back[1], NT)
            dk_ref[b] = jnp.where(mask, dk, dk_ref[b])
        return carry

    lax.fori_loop(low, high + 1, one, 0)
    feats = split(f_ref[...])
    for b in range(blocks):
        inv = inv_ref[b]
        exact = num_ref[b] * inv
        res_ref[b, OUT] = exact
        grad_denom = -jnp.sum(all_ref[b, G] * exact, axis=1, keepdims=True) * inv
        raised = qr_ref[b]
        num_ref[b] = (raised + EPS * RATIO) * grad_denom
        grad_logits = (gs_ref[b] * inv + grad_denom * tr_ref[b]) * raised
        back = dot3(split(grad_logits), feats, NN)
        back = back - jnp.sum(grad_logits, axis=1, keepdims=True) * (SCALE * all_ref[b, Q])
        res_ref[b, GQ] = back * SCALE
    bt_ref[0] = jnp.zeros(bt_ref.shape[1:], F32)

    def two(c, carry):
        total = jnp.zeros((rows, M), F32)
        for b in range(blocks):
            total = total + jnp.where(chains.mask(c, b), num_ref[b], 0.0)
        bt_ref[0, pl.ds(c, 1), :] = jnp.sum(total, axis=0, keepdims=True)
        return carry

    lax.fori_loop(low, high + 1, two, 0)
    for r in range(1, bt_ref.shape[0]):
        bt_ref[r] = bt_ref[0]


def key_kernel(lens, place, all_ref, f_ref, kr_ref, dk_ref, bt_ref, res_ref, sum_ref, add_ref):
    blocks, _, rows, _ = all_ref.shape
    chains = Chains(lens, place, blocks, rows)
    sum_ref[...] = jnp.sum(bt_ref[...], axis=0)
    low, high = chains.ends_of(chains.me)

    def one(c, carry):
        for b in range(blocks):
            add_ref[b] = jnp.where(chains.mask(c, b), sum_ref[pl.ds(c, 1), :], add_ref[b])
        return carry

    lax.fori_loop(low, high + 1, one, 0)
    feats = split(f_ref[...])
    for b in range(blocks):
        grad_logits = (dk_ref[b] + add_ref[b]) * kr_ref[b]
        back = dot3(split(grad_logits), feats, NN)
        back = back - jnp.sum(grad_logits, axis=1, keepdims=True) * (SCALE * all_ref[b, K])
        res_ref[b] = back * SCALE


def unpack_kernel(res_ref, key_ref, out_ref, gq_ref, gk_ref, gv_ref):
    for h in range(H):
        for i, ref in ((OUT, out_ref), (GQ, gq_ref), (GV, gv_ref)):
            ref[:, head(h)] = res_ref[h, i].astype(BF16)
        gk_ref[:, head(h)] = key_ref[h].astype(BF16)


def call(kernel, shapes, args, scalars=0, scratch=()):
    vmem = pl.BlockSpec(memory_space=pltpu.VMEM)
    smem = pl.BlockSpec(memory_space=pltpu.SMEM)
    return pl.pallas_call(
        kernel,
        out_shape=shapes,
        in_specs=[smem] * scalars + [vmem] * (len(args) - scalars),
        out_specs=[vmem] * len(shapes),
        scratch_shapes=list(scratch),
        compiler_params=pltpu.CompilerParams(vmem_limit_bytes=40 * 2**20),
    )(*args)


def f32(*shape):
    return jax.ShapeDtypeStruct(shape, F32)


def on_device(queries, keys, values, grad_attended, features, chain_lengths):
    rows, width = queries.shape[1:]
    q, k, v, g = (a.reshape(rows, width) for a in (queries, keys, values, grad_attended))
    place = jnp.stack([lax.axis_index("row"), lax.axis_index("col")]).astype(jnp.int32)
    where = (chain_lengths, place)
    groups, lines, blocks = (lax.axis_size(a) for a in ("grp", "row", "col"))
    wide = (blocks, rows, D)
    hbm = pl.BlockSpec(memory_space=pltpu.HBM)
    vmem = pl.BlockSpec(memory_space=pltpu.VMEM)
    packed, peaks = pl.pallas_call(
        pack_kernel,
        out_shape=[f32(H, 4, rows, D), f32(groups, H, M)],
        in_specs=[vmem] + [hbm] * 4,
        out_specs=[hbm, vmem],
        scratch_shapes=[
            pltpu.VMEM((4, rows, width), BF16),
            pltpu.VMEM((H, 4, rows, D), F32),
            pltpu.SemaphoreType.DMA((4,)),
            pltpu.SemaphoreType.DMA((H,)),
        ],
        compiler_params=pltpu.CompilerParams(vmem_limit_bytes=40 * 2**20),
    )(features, k, v, q, g)
    own = lax.all_to_all(packed, "col", 0, 0, tiled=True)
    peaks = lax.all_to_all(peaks, "grp", 0, 0, tiled=True)
    logits, raised, payload = call(
        logit_kernel,
        [f32(*wide), f32(*wide), f32(lines * blocks, 2 * CHAINS, M)],
        (*where, own, features, peaks),
        2,
    )
    payload = lax.all_to_all(payload, ("row", "col"), 0, 0, tiled=True)
    lots = (CHAINS, M, D)
    key_raised, inverse, totals, states, backs, ends = call(
        state_kernel,
        [f32(*wide), f32(*wide), f32(CHAINS, M), f32(*lots), f32(*lots), f32(lines, 2, 2, M, D)],
        (*where, own, logits, raised, payload),
        2,
    )
    ends = lax.all_to_all(ends, "row", 0, 0, tiled=True)
    results, grad_feats, back_totals = call(
        middle_kernel,
        [f32(blocks, 3, rows, D), f32(*wide), f32(lines, 2 * CHAINS, M)],
        (*where, own, features, raised, key_raised, inverse, totals, states, backs, ends),
        2,
        [pltpu.VMEM(lots, F32)] * 2 + [pltpu.VMEM(wide, F32)] * 3,
    )
    results = lax.all_to_all(results, "col", 0, 0, tiled=True)
    back_totals = lax.all_to_all(back_totals, "row", 0, 0, tiled=True)
    (grad_keys,) = call(
        key_kernel,
        [f32(*wide)],
        (*where, own, features, key_raised, grad_feats, back_totals),
        2,
        [pltpu.VMEM((2 * CHAINS, M), F32), pltpu.VMEM(wide, F32)],
    )
    grad_keys = lax.all_to_all(grad_keys, "col", 0, 0, tiled=True)
    outs = call(
        unpack_kernel, [jax.ShapeDtypeStruct((rows, width), BF16)] * 4, (results, grad_keys)
    )
    return tuple(a.reshape(1, rows, width) for a in outs)


def solution(mesh):
    groups, seq = mesh.devices.shape
    fine = Mesh(mesh.devices.reshape(groups, seq // H, H), ("grp", "row", "col"))
    rows = P("grp", ("row", "col"), None)
    return jax.shard_map(
        on_device,
        mesh=fine,
        in_specs=(rows, rows, rows, rows, P(), P("grp", None)),
        out_specs=(rows, rows, rows, rows),
        check_vma=False,
    )
```

```python
import jax
import jax.numpy as jnp
from jax import lax
from jax.experimental import pallas as pl
from jax.experimental.pallas import tpu as pltpu
from jax.sharding import Mesh
from jax.sharding import PartitionSpec as P

H = 8
D = 128
M = 128
CHAINS = 4
EPS = 1e-06
SCALE = D ** (-0.25)
RATIO = M ** (-0.5)
F32 = jnp.float32
BF16 = jnp.bfloat16
NN = (((1,), (0,)), ((), ()))
NT = (((1,), (1,)), ((), ()))
TN = (((0,), (0,)), ((), ()))
K, V, Q, G = range(4)
OUT, GQ = range(2)
GK, GV = range(2)


def dot(a, b, dims):
    return lax.dot_general(a, b, dims, preferred_element_type=F32)


def split(x):
    hi = x.astype(BF16)
    return hi, (x - hi.astype(F32)).astype(BF16)


def split3(x):
    hi = x.astype(BF16)
    rest = x - hi.astype(F32)
    mid = rest.astype(BF16)
    return hi, mid, (rest - mid.astype(F32)).astype(BF16)


def dot3(a, b, dims):
    (ah, al), (bh, bl) = a, b
    return dot(ah, bh, dims) + (dot(ah, bl, dims) + dot(al, bh, dims))


def head(h):
    return slice(h * D, (h + 1) * D)


def logits_of(x, parts):
    f1, f2, f3 = parts
    y = x.astype(BF16)
    z = dot(y, f1, NT) + (dot(y, f2, NT) + dot(y, f3, NT))
    return SCALE * z - (0.5 * SCALE * SCALE) * jnp.sum(x * x, axis=1, keepdims=True)


class Chains:
    def __init__(self, lens, place, blocks, rows):
        self.rows = rows
        self.span = blocks * rows
        self.me = place[0]
        l0, l1, l2 = lens[0, 0], lens[0, 1], lens[0, 2]
        self.starts = (jnp.int32(0), l0, l0 + l1, l0 + l1 + l2)
        self.lens = lens

    def count_ended(self, position):
        c = jnp.int32(0)
        for s in self.starts[1:]:
            c = c + (position >= s).astype(jnp.int32)
        return c

    def ends_of(self, which):
        return self.count_ended(which * self.span), self.count_ended((which + 1) * self.span - 1)

    def start_of(self, c):
        s = self.starts
        return jnp.where(c == 0, s[0], jnp.where(c == 1, s[1], jnp.where(c == 2, s[2], s[3])))

    def mask(self, c, block):
        low = self.start_of(c) - (self.me * self.span + block * self.rows)
        at = lax.broadcasted_iota(jnp.int32, (self.rows, D), 0)
        return (at >= low) & (at < low + self.lens[0, c])


def pack_kernel(f_ref, k_hbm, v_hbm, q_hbm, g_hbm, out_hbm, peak_ref, rows_ref, wide_ref, in_sem, out_sem):
    sources = (k_hbm, v_hbm, q_hbm, g_hbm)
    loads = [pltpu.make_async_copy(r, rows_ref.at[i], in_sem.at[i]) for i, r in enumerate(sources)]
    for load in loads:
        load.start()
    for load in loads:
        load.wait()
    stores = [pltpu.make_async_copy(wide_ref.at[h], out_hbm.at[h], out_sem.at[h]) for h in range(H)]
    for h in range(H):
        for i in range(4):
            wide_ref[h, i] = rows_ref[i, :, head(h)].astype(F32)
        stores[h].start()
    parts = split3(f_ref[...])
    for h in range(H):
        logits = logits_of(rows_ref[K, :, head(h)].astype(F32), parts)
        peak = jnp.broadcast_to(jnp.max(logits, axis=(0, 1), keepdims=True), (1, M))
        peak_ref[h : h + 1, :] = peak
    for store in stores:
        store.wait()


def logit_kernel(lens, place, all_ref, f_ref, kl_ref, qr_ref, base_ref):
    blocks, _, rows, _ = all_ref.shape
    chains = Chains(lens, place, blocks, rows)
    parts = split3(f_ref[...])
    for b in range(blocks):
        kl_ref[b] = logits_of(all_ref[b, K], parts)
    peak = jnp.max(jnp.max(kl_ref[...], axis=0), axis=(0, 1), keepdims=True)
    low, high = chains.ends_of(chains.me)
    base_ref[...] = jnp.zeros_like(base_ref)
    base_ref[CHAINS : CHAINS + 1, :] = jnp.broadcast_to(peak, (1, M))

    def one(c, carry):
        total = jnp.zeros((rows, M), F32)
        for b in range(blocks):
            total = total + jnp.where(chains.mask(c, b), jnp.exp(kl_ref[b] - peak), 0.0)
        base_ref[pl.ds(c, 1), :] = jnp.sum(total, axis=0, keepdims=True)
        return carry

    lax.fori_loop(low, high + 1, one, 0)
    for b in range(blocks):
        ql = logits_of(all_ref[b, Q], parts)
        qr_ref[b] = jnp.exp(ql - jnp.max(ql, axis=1, keepdims=True)) * RATIO


def payload_kernel(base_ref, peak_ref, pay_ref):
    row = lax.broadcasted_iota(jnp.int32, base_ref.shape, 0)
    for i in range(pay_ref.shape[0]):
        h = i % H
        pay_ref[i] = jnp.where(row == CHAINS + 1, peak_ref[h : h + 1, :], base_ref[...])


def state_kernel(
    lens, place, all_ref, kl_ref, qr_ref, pay_ref,
    kr_ref, inv_ref, t_ref, s_ref, b_ref, s_send, b_send,
):
    blocks, _, rows, _ = all_ref.shape
    chains = Chains(lens, place, blocks, rows)
    everyone = pay_ref.shape[0]
    peak = jnp.max(pay_ref[...], axis=0)[CHAINS + 1 : CHAINS + 2, :]
    total = jnp.zeros((CHAINS, M), F32)
    for r in range(everyone // H):
        mine = pay_ref[r * H + place[1]]
        total = total + jnp.exp(mine[CHAINS : CHAINS + 1, :] - peak) * mine[:CHAINS, :]
    for c in range(CHAINS):
        count = lens[0, c].astype(F32)
        t_ref[c : c + 1, :] = RATIO * (total[c : c + 1, :] + EPS * count)
    for b in range(blocks):
        kr_ref[b] = jnp.exp(kl_ref[b] - peak) * RATIO
    s_ref[...] = jnp.zeros_like(s_ref)
    b_ref[...] = jnp.zeros_like(b_ref)
    low, high = chains.ends_of(chains.me)

    def one(c, carry):
        state = jnp.zeros((M, D), F32)
        back = jnp.zeros((M, D), F32)
        weights = t_ref[pl.ds(c, 1), :]
        for b in range(blocks):
            mask = chains.mask(c, b)
            hi, lo = split(jnp.where(mask, kr_ref[b] + EPS * RATIO, 0.0))
            v = all_ref[b, V].astype(BF16)
            state = state + (dot(hi, v, TN) + dot(lo, v, TN))
            qf = qr_ref[b] + EPS * RATIO
            inv = 1.0 / jnp.sum(qf * weights, axis=1, keepdims=True)
            hi, lo = split(jnp.where(mask, qf * inv, 0.0))
            g = all_ref[b, G].astype(BF16)
            back = back + (dot(hi, g, TN) + dot(lo, g, TN))
            inv_ref[b] = jnp.where(mask, inv, inv_ref[b])
        s_ref[c] = state
        b_ref[c] = back
        return carry

    lax.fori_loop(low, high + 1, one, 0)
    other = (high != low).astype(F32)
    for ref, send in ((s_ref, s_send), (b_ref, b_send)):
        send[0] = ref[low]
        send[1] = ref[high] * other


def add_rows(chains, full_ref, own_ref, sent_ref):
    full_ref[...] = own_ref[...]
    for r in range(sent_ref.shape[0]):
        low, high = chains.ends_of(r)

        @pl.when(chains.me != r)
        def _():
            full_ref[low] += sent_ref[r, :M, :]
            full_ref[high] += sent_ref[r, M : 2 * M, :]


def query_kernel(
    lens, place, all_ref, f_ref, qr_ref, inv_ref, t_ref, s_ref, s_sent, b_send,
    res_ref, back_ref, full_ref, num_ref, gs_ref, tr_ref,
):
    blocks, _, rows, _ = all_ref.shape
    chains = Chains(lens, place, blocks, rows)
    add_rows(chains, full_ref, s_ref, s_sent)
    low, high = chains.ends_of(chains.me)

    def one(c, carry):
        state = split(full_ref[c])
        for b in range(blocks):
            mask = chains.mask(c, b)
            num = dot3(split(qr_ref[b] + EPS * RATIO), state, NN)
            num_ref[b] = jnp.where(mask, num, num_ref[b])
            g = all_ref[b, G].astype(BF16)
            gs = dot(g, state[0], NT) + dot(g, state[1], NT)
            gs_ref[b] = jnp.where(mask, gs, gs_ref[b])
            tr_ref[b] = jnp.where(mask, t_ref[pl.ds(c, 1), :], tr_ref[b])
        return carry

    lax.fori_loop(low, high + 1, one, 0)
    feats = split(f_ref[...])
    for b in range(blocks):
        inv = inv_ref[b]
        exact = num_ref[b] * inv
        res_ref[b, OUT] = exact
        grad_denom = -jnp.sum(all_ref[b, G] * exact, axis=1, keepdims=True) * inv
        raised = qr_ref[b]
        num_ref[b] = (raised + EPS * RATIO) * grad_denom
        grad_logits = (gs_ref[b] * inv + grad_denom * tr_ref[b]) * raised
        back = dot3(split(grad_logits), feats, NN)
        back = back - jnp.sum(grad_logits, axis=1, keepdims=True) * (SCALE * all_ref[b, Q])
        res_ref[b, GQ] = back * SCALE
    back_ref[0:M, :] = b_send[0]
    back_ref[M : 2 * M, :] = b_send[1]
    back_ref[2 * M :, :] = jnp.zeros((2 * CHAINS, M), F32)

    def two(c, carry):
        total = jnp.zeros((rows, M), F32)
        for b in range(blocks):
            total = total + jnp.where(chains.mask(c, b), num_ref[b], 0.0)
        back_ref[pl.ds(2 * M + c, 1), :] = jnp.sum(total, axis=0, keepdims=True)
        return carry

    lax.fori_loop(low, high + 1, two, 0)


def key_kernel(
    lens, place, all_ref, f_ref, kr_ref, b_ref, sent_ref, res_ref, full_ref, sum_ref, dk_ref,
):
    blocks, _, rows, _ = all_ref.shape
    chains = Chains(lens, place, blocks, rows)
    add_rows(chains, full_ref, b_ref, sent_ref)
    sum_ref[...] = jnp.sum(sent_ref[:, 2 * M :, :], axis=0)
    low, high = chains.ends_of(chains.me)

    def one(c, carry):
        back = split(full_ref[c])
        total = sum_ref[pl.ds(c, 1), :]
        for b in range(blocks):
            mask = chains.mask(c, b)
            dv = dot3(split(kr_ref[b] + EPS * RATIO), back, NN)
            res_ref[b, GV] = jnp.where(mask, dv, res_ref[b, GV])
            v = all_ref[b, V].astype(BF16)
            dk = dot(v, back[0], NT) + dot(v, back[1], NT) + total
            dk_ref[b] = jnp.where(mask, dk, dk_ref[b])
        return carry

    lax.fori_loop(low, high + 1, one, 0)
    feats = split(f_ref[...])
    for b in range(blocks):
        grad_logits = dk_ref[b] * kr_ref[b]
        back = dot3(split(grad_logits), feats, NN)
        back = back - jnp.sum(grad_logits, axis=1, keepdims=True) * (SCALE * all_ref[b, K])
        res_ref[b, GK] = back * SCALE


def unpack_kernel(first_ref, second_ref, out_ref, gq_ref, gk_ref, gv_ref):
    for h in range(H):
        out_ref[:, head(h)] = first_ref[h, OUT].astype(BF16)
        gq_ref[:, head(h)] = first_ref[h, GQ].astype(BF16)
        gk_ref[:, head(h)] = second_ref[h, GK].astype(BF16)
        gv_ref[:, head(h)] = second_ref[h, GV].astype(BF16)


def call(kernel, shapes, args, scalars=0, scratch=()):
    vmem = pl.BlockSpec(memory_space=pltpu.VMEM)
    smem = pl.BlockSpec(memory_space=pltpu.SMEM)
    return pl.pallas_call(
        kernel,
        out_shape=shapes,
        in_specs=[smem] * scalars + [vmem] * (len(args) - scalars),
        out_specs=[vmem] * len(shapes),
        scratch_shapes=list(scratch),
        compiler_params=pltpu.CompilerParams(vmem_limit_bytes=40 * 2**20),
    )(*args)


def f32(*shape):
    return jax.ShapeDtypeStruct(shape, F32)


def max_over(x, axis):
    count = lax.axis_size(axis)
    reach = 0
    while 2 * reach + 1 < count:
        step = min(2 * reach + 1, count // 2 - reach)
        up = lax.ppermute(x, axis, [(i, (i + step) % count) for i in range(count)])
        down = lax.ppermute(x, axis, [(i, (i - step) % count) for i in range(count)])
        x = jnp.maximum(x, jnp.maximum(up, down))
        reach += step
    return x


def on_device(queries, keys, values, grad_attended, features, chain_lengths):
    rows, width = queries.shape[1:]
    q, k, v, g = (a.reshape(rows, width) for a in (queries, keys, values, grad_attended))
    place = jnp.stack([lax.axis_index("row"), lax.axis_index("col")]).astype(jnp.int32)
    where = (chain_lengths, place)
    lines, blocks = (lax.axis_size(a) for a in ("row", "col"))
    wide = (blocks, rows, D)
    hbm = pl.BlockSpec(memory_space=pltpu.HBM)
    vmem = pl.BlockSpec(memory_space=pltpu.VMEM)
    packed, peaks = pl.pallas_call(
        pack_kernel,
        out_shape=[f32(H, 4, rows, D), f32(H, M)],
        in_specs=[vmem] + [hbm] * 4,
        out_specs=[hbm, vmem],
        scratch_shapes=[
            pltpu.VMEM((4, rows, width), BF16),
            pltpu.VMEM((H, 4, rows, D), F32),
            pltpu.SemaphoreType.DMA((4,)),
            pltpu.SemaphoreType.DMA((H,)),
        ],
        compiler_params=pltpu.CompilerParams(vmem_limit_bytes=60 * 2**20),
    )(features, k, v, q, g)
    own = lax.all_to_all(packed, "col", 0, 0, tiled=True)
    peaks = max_over(peaks, "grp")
    logits, raised, base = call(
        logit_kernel, [f32(*wide), f32(*wide), f32(2 * CHAINS, M)], (*where, own, features), 2
    )
    (payload,) = call(payload_kernel, [f32(lines * blocks, 2 * CHAINS, M)], (base, peaks))
    payload = lax.all_to_all(payload, ("row", "col"), 0, 0, tiled=True)
    lots = (CHAINS, M, D)
    key_raised, inverse, totals, states, backs, state_ends, back_ends = call(
        state_kernel,
        [f32(*wide), f32(*wide), f32(CHAINS, M), f32(*lots), f32(*lots), f32(2, M, D), f32(2, M, D)],
        (*where, own, logits, raised, payload),
        2,
    )
    state_ends = lax.all_gather(state_ends.reshape(2 * M, D), "row")
    first, back_ends = call(
        query_kernel,
        [f32(blocks, 2, rows, D), f32(2 * M + 2 * CHAINS, D)],
        (*where, own, features, raised, inverse, totals, states, state_ends, back_ends),
        2,
        [pltpu.VMEM(lots, F32)] + [pltpu.VMEM(wide, F32)] * 3,
    )
    first = lax.all_to_all(first, "col", 0, 0, tiled=True)
    back_ends = lax.all_gather(back_ends, "row")
    (second,) = call(
        key_kernel,
        [f32(blocks, 2, rows, D)],
        (*where, own, features, key_raised, backs, back_ends),
        2,
        [pltpu.VMEM(lots, F32), pltpu.VMEM((2 * CHAINS, M), F32), pltpu.VMEM(wide, F32)],
    )
    second = lax.all_to_all(second, "col", 0, 0, tiled=True)
    outs = call(unpack_kernel, [jax.ShapeDtypeStruct((rows, width), BF16)] * 4, (first, second))
    return tuple(a.reshape(1, rows, width) for a in outs)


def solution(mesh):
    groups, seq = mesh.devices.shape
    fine = Mesh(mesh.devices.reshape(groups, seq // H, H), ("grp", "row", "col"))
    rows = P("grp", ("row", "col"), None)
    return jax.shard_map(
        on_device,
        mesh=fine,
        in_specs=(rows, rows, rows, rows, P(), P("grp", None)),
        out_specs=(rows, rows, rows, rows),
        check_vma=False,
    )
```

```python
import jax
import jax.numpy as jnp
from jax import lax
from jax.experimental import pallas as pl
from jax.experimental.pallas import tpu as pltpu
from jax.sharding import Mesh
from jax.sharding import PartitionSpec as P

H = 8
D = 128
M = 128
CHAINS = 4
EPS = 1e-06
SCALE = D ** (-0.25)
RATIO = M ** (-0.5)
F32 = jnp.float32
BF16 = jnp.bfloat16
NN = (((1,), (0,)), ((), ()))
NT = (((1,), (1,)), ((), ()))
TN = (((0,), (0,)), ((), ()))
K, V, Q, G = range(4)
OUT, GQ = range(2)
GK, GV = range(2)


def dot(a, b, dims):
    return lax.dot_general(a, b, dims, preferred_element_type=F32)


def split(x):
    hi = x.astype(BF16)
    return hi, (x - hi.astype(F32)).astype(BF16)


def split3(x):
    hi = x.astype(BF16)
    rest = x - hi.astype(F32)
    mid = rest.astype(BF16)
    return hi, mid, (rest - mid.astype(F32)).astype(BF16)


def dot3(a, b, dims):
    (ah, al), (bh, bl) = a, b
    return dot(ah, bh, dims) + (dot(ah, bl, dims) + dot(al, bh, dims))


def head(h):
    return slice(h * D, (h + 1) * D)


def logits_of(x, parts):
    f1, f2, f3 = parts
    y = x.astype(BF16)
    z = dot(y, f1, NT) + (dot(y, f2, NT) + dot(y, f3, NT))
    return SCALE * z - (0.5 * SCALE * SCALE) * jnp.sum(x * x, axis=1, keepdims=True)


class Chains:
    def __init__(self, lens, me, blocks, rows):
        self.rows = rows
        self.span = blocks * rows
        self.me = me
        l0, l1, l2 = lens[0, 0], lens[0, 1], lens[0, 2]
        self.starts = (jnp.int32(0), l0, l0 + l1, l0 + l1 + l2)
        self.lens = lens

    def count_ended(self, position):
        c = jnp.int32(0)
        for s in self.starts[1:]:
            c = c + (position >= s).astype(jnp.int32)
        return c

    def ends_of(self, which):
        return self.count_ended(which * self.span), self.count_ended((which + 1) * self.span - 1)

    def start_of(self, c):
        s = self.starts
        return jnp.where(c == 0, s[0], jnp.where(c == 1, s[1], jnp.where(c == 2, s[2], s[3])))

    def mask(self, c, block):
        low = self.start_of(c) - (self.me * self.span + block * self.rows)
        at = lax.broadcasted_iota(jnp.int32, (self.rows, D), 0)
        return (at >= low) & (at < low + self.lens[0, c])


def pack_kernel(k_hbm, v_hbm, q_hbm, g_hbm, out_hbm, rows_ref, wide_ref, in_sem, out_sem):
    sources = (k_hbm, v_hbm, q_hbm, g_hbm)
    loads = [pltpu.make_async_copy(r, rows_ref.at[i], in_sem.at[i]) for i, r in enumerate(sources)]
    for load in loads:
        load.start()
    for load in loads:
        load.wait()
    stores = [pltpu.make_async_copy(wide_ref.at[h], out_hbm.at[h], out_sem.at[h]) for h in range(H)]
    for h in range(H):
        for i in range(4):
            wide_ref[h, i] = rows_ref[i, :, head(h)].astype(F32)
        stores[h].start()
    for store in stores:
        store.wait()


def total_kernel(lens, place, k_ref, f_ref, pay_ref, kl_ref):
    rows = k_ref.shape[0]
    chains = Chains(lens, place[0] * H + place[1], 1, rows)
    parts = split3(f_ref[...])
    pay_ref[: CHAINS * H, :] = jnp.zeros((CHAINS * H, M), F32)
    for h in range(H):
        logits = logits_of(k_ref[:, head(h)].astype(F32), parts)
        peak = jnp.max(logits, axis=(0, 1), keepdims=True)
        kl_ref[h] = jnp.exp(logits - peak)
        pay_ref[CHAINS * H + h : CHAINS * H + h + 1, :] = jnp.broadcast_to(peak, (1, M))
    low, high = chains.ends_of(chains.me)

    def one(c, carry):
        mask = chains.mask(c, 0)
        for h in range(H):
            total = jnp.sum(jnp.where(mask, kl_ref[h], 0.0), axis=0, keepdims=True)
            pay_ref[pl.ds(c * H + h, 1), :] = total
        return carry

    lax.fori_loop(low, high + 1, one, 0)


def state_kernel(
    lens, place, all_ref, f_ref, pay_ref,
    er_ref, qr_ref, tot_ref, z_ref, s_ref, send_ref, sums_ref,
):
    blocks, _, rows, _ = all_ref.shape
    chains = Chains(lens, place[0], blocks, rows)
    peaks = jnp.max(pay_ref[:, CHAINS * H :, :], axis=0)
    sums = [jnp.zeros((H, M), F32) for _ in range(CHAINS)]
    for d in range(pay_ref.shape[0]):
        share = jnp.exp(pay_ref[d, CHAINS * H :, :] - peaks)
        for c in range(CHAINS):
            sums[c] = sums[c] + share * pay_ref[d, c * H : (c + 1) * H, :]
    for c in range(CHAINS):
        sums_ref[c * H : (c + 1) * H, :] = sums[c]
    sums_ref[CHAINS * H :, :] = peaks
    tot_ref[...] = jnp.zeros_like(tot_ref)
    for c in range(CHAINS + 1):
        tot_ref[c : c + 1, :] = sums_ref[pl.ds(c * H + place[1], 1), :]
    peak = tot_ref[CHAINS : CHAINS + 1, :]
    for i in range(z_ref.shape[0]):
        z_ref[i] = jnp.broadcast_to(peak, z_ref.shape[1:])
    parts = split3(f_ref[...])
    for b in range(blocks):
        er_ref[b] = jnp.exp(logits_of(all_ref[b, K], parts) - peak)
        ql = logits_of(all_ref[b, Q], parts)
        qr_ref[b] = jnp.exp(ql - jnp.max(ql, axis=1, keepdims=True)) * RATIO
    s_ref[...] = jnp.zeros_like(s_ref)
    low, high = chains.ends_of(chains.me)

    def one(c, carry):
        state = jnp.zeros((M, D), F32)
        total = jnp.zeros((rows, D), F32)
        for b in range(blocks):
            mask = chains.mask(c, b)
            hi, lo = split(jnp.where(mask, er_ref[b], 0.0))
            v = all_ref[b, V]
            total = total + jnp.where(mask, v, 0.0)
            v = v.astype(BF16)
            state = state + (dot(hi, v, TN) + dot(lo, v, TN))
        s_ref[c, :M, :] = state
        s_ref[c, M : M + 1, :] = jnp.sum(total, axis=0, keepdims=True)
        return carry

    lax.fori_loop(low, high + 1, one, 0)
    send_ref[0] = s_ref[low]
    send_ref[1] = s_ref[high] * (high != low).astype(F32)


def query_kernel(
    lens, place, all_ref, f_ref, er_ref, qr_ref, tot_ref, z_ref, s_ref, s1_ref, s2_ref, s3_ref,
    res_ref, send_ref, bt_ref, b_ref, share_ref, full_ref, num_ref, gs_ref, inv_ref, tr_ref, t_ref,
):
    blocks, _, rows, _ = all_ref.shape
    chains = Chains(lens, place[0], blocks, rows)
    peak = jnp.max(jnp.max(z_ref[...], axis=0), axis=0, keepdims=True)
    share = jnp.exp(tot_ref[CHAINS : CHAINS + 1, :] - peak)
    share_ref[...] = jnp.broadcast_to(RATIO * share, share_ref.shape)
    for c in range(CHAINS):
        count = lens[0, c].astype(F32)
        t_ref[c : c + 1, :] = RATIO * (share * tot_ref[c : c + 1, :] + EPS * count)
    full_ref[...] = s_ref[...]
    for step, sent_ref in ((1, s1_ref), (2, s2_ref), (3, s3_ref)):
        ends = chains.ends_of(lax.rem(chains.me + (4 - step), 4))
        for i, c in enumerate(ends):
            full_ref[c] += sent_ref[i]
    b_ref[...] = jnp.zeros_like(b_ref)
    low, high = chains.ends_of(chains.me)

    def one(c, carry):
        state = RATIO * (share * full_ref[c, :M, :] + EPS * full_ref[c, M : M + 1, :])
        state = split(state)
        weights = t_ref[pl.ds(c, 1), :]
        back = jnp.zeros((M, D), F32)
        for b in range(blocks):
            mask = chains.mask(c, b)
            qf = qr_ref[b] + EPS * RATIO
            inv = 1.0 / jnp.sum(qf * weights, axis=1, keepdims=True)
            inv_ref[b] = jnp.where(mask, inv, inv_ref[b])
            tr_ref[b] = jnp.where(mask, weights, tr_ref[b])
            num = dot3(split(qf), state, NN)
            num_ref[b] = jnp.where(mask, num, num_ref[b])
            g = all_ref[b, G].astype(BF16)
            gs = dot(g, state[0], NT) + dot(g, state[1], NT)
            gs_ref[b] = jnp.where(mask, gs, gs_ref[b])
            hi, lo = split(jnp.where(mask, qf * inv, 0.0))
            back = back + (dot(hi, g, TN) + dot(lo, g, TN))
        b_ref[c] = back
        return carry

    lax.fori_loop(low, high + 1, one, 0)
    feats = split(f_ref[...])
    for b in range(blocks):
        inv = inv_ref[b]
        exact = num_ref[b] * inv
        res_ref[b, OUT] = exact
        grad_denom = -jnp.sum(all_ref[b, G] * exact, axis=1, keepdims=True) * inv
        raised = qr_ref[b]
        num_ref[b] = (raised + EPS * RATIO) * grad_denom
        grad_logits = (gs_ref[b] * inv + grad_denom * tr_ref[b]) * raised
        back = dot3(split(grad_logits), feats, NN)
        back = back - jnp.sum(grad_logits, axis=1, keepdims=True) * (SCALE * all_ref[b, Q])
        res_ref[b, GQ] = back * SCALE
    bt_ref[...] = jnp.zeros_like(bt_ref)

    def two(c, carry):
        total = jnp.zeros((rows, M), F32)
        for b in range(blocks):
            total = total + jnp.where(chains.mask(c, b), num_ref[b], 0.0)
        bt_ref[pl.ds(c, 1), :] = jnp.sum(total, axis=0, keepdims=True)
        return carry

    lax.fori_loop(low, high + 1, two, 0)
    send_ref[0:M, :] = b_ref[low]
    send_ref[M : 2 * M, :] = b_ref[high] * (high != low).astype(F32)
    send_ref[2 * M :, :] = bt_ref[...]


def key_kernel(
    lens, place, all_ref, f_ref, er_ref, share_ref, b_ref, sent_ref,
    res_ref, full_ref, sum_ref, dk_ref,
):
    blocks, _, rows, _ = all_ref.shape
    chains = Chains(lens, place[0], blocks, rows)
    full_ref[...] = b_ref[...]
    for r in range(sent_ref.shape[0]):
        low, high = chains.ends_of(r)

        @pl.when(chains.me != r)
        def _():
            full_ref[low] += sent_ref[r, :M, :]
            full_ref[high] += sent_ref[r, M : 2 * M, :]

    sum_ref[...] = jnp.sum(sent_ref[:, 2 * M :, :], axis=0)
    share = share_ref[0:1, :]
    low, high = chains.ends_of(chains.me)

    def one(c, carry):
        back = split(full_ref[c])
        total = sum_ref[pl.ds(c, 1), :]
        for b in range(blocks):
            mask = chains.mask(c, b)
            dv = dot3(split(er_ref[b] * share + EPS * RATIO), back, NN)
            res_ref[b, GV] = jnp.where(mask, dv, res_ref[b, GV])
            v = all_ref[b, V].astype(BF16)
            dk = dot(v, back[0], NT) + dot(v, back[1], NT) + total
            dk_ref[b] = jnp.where(mask, dk, dk_ref[b])
        return carry

    lax.fori_loop(low, high + 1, one, 0)
    feats = split(f_ref[...])
    for b in range(blocks):
        grad_logits = dk_ref[b] * (er_ref[b] * share)
        back = dot3(split(grad_logits), feats, NN)
        back = back - jnp.sum(grad_logits, axis=1, keepdims=True) * (SCALE * all_ref[b, K])
        res_ref[b, GK] = back * SCALE


def unpack_kernel(res_ref, *outs):
    for h in range(H):
        for i, out in enumerate(outs):
            out[:, head(h)] = res_ref[h, i].astype(BF16)


def call(kernel, shapes, args, scalars=0, scratch=()):
    vmem = pl.BlockSpec(memory_space=pltpu.VMEM)
    smem = pl.BlockSpec(memory_space=pltpu.SMEM)
    return pl.pallas_call(
        kernel,
        out_shape=shapes,
        in_specs=[smem] * scalars + [vmem] * (len(args) - scalars),
        out_specs=[vmem] * len(shapes),
        scratch_shapes=list(scratch),
        compiler_params=pltpu.CompilerParams(vmem_limit_bytes=40 * 2**20),
    )(*args)


def f32(*shape):
    return jax.ShapeDtypeStruct(shape, F32)


def on_device(queries, keys, values, grad_attended, features, chain_lengths):
    rows, width = queries.shape[1:]
    q, k, v, g = (a.reshape(rows, width) for a in (queries, keys, values, grad_attended))
    place = jnp.stack([lax.axis_index("row"), lax.axis_index("col")]).astype(jnp.int32)
    where = (chain_lengths, place)
    groups, lines, blocks = (lax.axis_size(a) for a in ("grp", "row", "col"))
    wide = (blocks, rows, D)
    hbm = pl.BlockSpec(memory_space=pltpu.HBM)
    packed = pl.pallas_call(
        pack_kernel,
        out_shape=f32(H, 4, rows, D),
        in_specs=[hbm] * 4,
        out_specs=hbm,
        scratch_shapes=[
            pltpu.VMEM((4, rows, width), BF16),
            pltpu.VMEM((H, 4, rows, D), F32),
            pltpu.SemaphoreType.DMA((4,)),
            pltpu.SemaphoreType.DMA((H,)),
        ],
        compiler_params=pltpu.CompilerParams(vmem_limit_bytes=60 * 2**20),
    )(k, v, q, g)
    own = lax.all_to_all(packed, "col", 0, 0, tiled=True)
    small = f32(2 * CHAINS, M)
    lots = ((CHAINS + 1) * H, M)
    (payload,) = call(
        total_kernel, [f32(*lots)], (*where, k, features), 2, [pltpu.VMEM((H, rows, M), F32)]
    )
    payload = lax.all_gather(payload, ("row", "col"))
    states = (CHAINS, M + 8, D)
    key_raised, raised, totals, peaks, own_states, ends = call(
        state_kernel,
        [f32(*wide), f32(*wide), small, f32(groups, 8, M), f32(*states), f32(2, M + 8, D)],
        (*where, own, features, payload),
        2,
        [pltpu.VMEM(lots, F32)],
    )
    sent = [
        lax.ppermute(ends, "row", [(i, (i + step) % lines) for i in range(lines)])
        for step in range(1, lines)
    ]
    peaks = lax.all_to_all(peaks, "grp", 0, 0, tiled=True)
    first, back_ends, _, backs, share = call(
        query_kernel,
        [f32(blocks, 2, rows, D), f32(2 * M + 2 * CHAINS, D), small, f32(CHAINS, M, D), small],
        (*where, own, features, key_raised, raised, totals, peaks, own_states, *sent),
        2,
        [pltpu.VMEM(states, F32)] + [pltpu.VMEM(wide, F32)] * 4 + [pltpu.VMEM((2 * CHAINS, M), F32)],
    )
    first = lax.all_to_all(first, "col", 0, 0, tiled=True)
    back_ends = lax.all_gather(back_ends, "row")
    (second,) = call(
        key_kernel,
        [f32(blocks, 2, rows, D)],
        (*where, own, features, key_raised, share, backs, back_ends),
        2,
        [pltpu.VMEM((CHAINS, M, D), F32), pltpu.VMEM((2 * CHAINS, M), F32), pltpu.VMEM(wide, F32)],
    )
    second = lax.all_to_all(second, "col", 0, 0, tiled=True)
    narrow = [jax.ShapeDtypeStruct((rows, width), BF16)] * 2
    outs = (*call(unpack_kernel, narrow, (first,)), *call(unpack_kernel, narrow, (second,)))
    return tuple(a.reshape(1, rows, width) for a in outs)


def solution(mesh):
    groups, seq = mesh.devices.shape
    fine = Mesh(mesh.devices.reshape(groups, seq // H, H), ("grp", "row", "col"))
    rows = P("grp", ("row", "col"), None)
    return jax.shard_map(
        on_device,
        mesh=fine,
        in_specs=(rows, rows, rows, rows, P(), P("grp", None)),
        out_specs=(rows, rows, rows, rows),
        check_vma=False,
    )
```

```python
import jax
import jax.numpy as jnp
from jax import lax
from jax.experimental import pallas as pl
from jax.experimental.pallas import tpu as pltpu
from jax.sharding import Mesh
from jax.sharding import PartitionSpec as P

H = 8
D = 128
M = 128
CHAINS = 4
EPS = 1e-06
SCALE = D ** (-0.25)
RATIO = M ** (-0.5)
F32 = jnp.float32
BF16 = jnp.bfloat16
NN = (((1,), (0,)), ((), ()))
NT = (((1,), (1,)), ((), ()))
TN = (((0,), (0,)), ((), ()))
K, V, Q, G = range(4)
OUT, GQ = range(2)
GK, GV = range(2)
VALUES, TOTALS, PEAK = M, M + 1, M + 2


def dot(a, b, dims):
    return lax.dot_general(a, b, dims, preferred_element_type=F32)


def split(x):
    hi = x.astype(BF16)
    return hi, (x - hi.astype(F32)).astype(BF16)


def split3(x):
    hi = x.astype(BF16)
    rest = x - hi.astype(F32)
    mid = rest.astype(BF16)
    return hi, mid, (rest - mid.astype(F32)).astype(BF16)


def dot3(a, b, dims):
    (ah, al), (bh, bl) = a, b
    return dot(ah, bh, dims) + (dot(ah, bl, dims) + dot(al, bh, dims))


def head(h):
    return slice(h * D, (h + 1) * D)


def logits_of(x, parts):
    f1, f2, f3 = parts
    y = x.astype(BF16)
    z = dot(y, f1, NT) + (dot(y, f2, NT) + dot(y, f3, NT))
    return SCALE * z - (0.5 * SCALE * SCALE) * jnp.sum(x * x, axis=1, keepdims=True)


class Chains:
    def __init__(self, lens, me, blocks, rows):
        self.rows = rows
        self.span = blocks * rows
        self.me = me
        l0, l1, l2 = lens[0, 0], lens[0, 1], lens[0, 2]
        self.starts = (jnp.int32(0), l0, l0 + l1, l0 + l1 + l2)
        self.lens = lens

    def count_ended(self, position):
        c = jnp.int32(0)
        for s in self.starts[1:]:
            c = c + (position >= s).astype(jnp.int32)
        return c

    def ends_of(self, which):
        return self.count_ended(which * self.span), self.count_ended((which + 1) * self.span - 1)

    def start_of(self, c):
        s = self.starts
        return jnp.where(c == 0, s[0], jnp.where(c == 1, s[1], jnp.where(c == 2, s[2], s[3])))

    def mask(self, c, block):
        low = self.start_of(c) - (self.me * self.span + block * self.rows)
        at = lax.broadcasted_iota(jnp.int32, (self.rows, D), 0)
        return (at >= low) & (at < low + self.lens[0, c])


def pack_kernel(k_hbm, v_hbm, q_hbm, g_hbm, out_hbm, rows_ref, wide_ref, in_sem, out_sem):
    sources = (k_hbm, v_hbm, q_hbm, g_hbm)
    loads = [pltpu.make_async_copy(r, rows_ref.at[i], in_sem.at[i]) for i, r in enumerate(sources)]
    for load in loads:
        load.start()
    for load in loads:
        load.wait()
    stores = [pltpu.make_async_copy(wide_ref.at[h], out_hbm.at[h], out_sem.at[h]) for h in range(H)]
    for h in range(H):
        for i in range(4):
            wide_ref[h, i] = rows_ref[i, :, head(h)].astype(F32)
        stores[h].start()
    for store in stores:
        store.wait()


def state_kernel(
    lens, place, all_ref, f_ref, z_hbm, s_ref, send_hbm, er_ref, send_ref, z_ref, sem, z_sem
):
    blocks, _, rows, _ = all_ref.shape
    chains = Chains(lens, place[0], blocks, rows)
    parts = split3(f_ref[...])
    peak = jnp.full((1, 1), -jnp.inf, F32)
    for b in range(blocks):
        logits = logits_of(all_ref[b, K], parts)
        er_ref[b] = logits
        peak = jnp.maximum(peak, jnp.max(logits, axis=(0, 1), keepdims=True))
    for b in range(blocks):
        er_ref[b] = jnp.exp(er_ref[b] - peak)
    for i in range(z_ref.shape[0]):
        z_ref[i] = jnp.broadcast_to(peak, z_ref.shape[1:])
    z_store = pltpu.make_async_copy(z_ref, z_hbm, z_sem)
    z_store.start()
    s_ref[...] = jnp.zeros_like(s_ref)
    for c in range(CHAINS):
        s_ref[c, PEAK : PEAK + 1, :] = jnp.broadcast_to(peak, (1, D))
    low, high = chains.ends_of(chains.me)

    def one(c, carry):
        state = jnp.zeros((M, D), F32)
        values = jnp.zeros((rows, D), F32)
        totals = jnp.zeros((rows, M), F32)
        for b in range(blocks):
            mask = chains.mask(c, b)
            raised = jnp.where(mask, er_ref[b], 0.0)
            totals = totals + raised
            hi, lo = split(raised)
            v = all_ref[b, V]
            values = values + jnp.where(mask, v, 0.0)
            v = v.astype(BF16)
            state = state + (dot(hi, v, TN) + dot(lo, v, TN))
        s_ref[c, :M, :] = state
        s_ref[c, VALUES : VALUES + 1, :] = jnp.sum(values, axis=0, keepdims=True)
        s_ref[c, TOTALS : TOTALS + 1, :] = jnp.sum(totals, axis=0, keepdims=True)
        return carry

    lax.fori_loop(low, high + 1, one, 0)
    send_ref[0] = s_ref[low]
    send_ref[1] = s_ref[high] * (high != low).astype(F32)
    store = pltpu.make_async_copy(send_ref, send_hbm, sem)
    store.start()
    z_store.wait()
    store.wait()


def query_kernel(
    lens, place, all_ref, f_ref, z_ref, s_ref, sent_ref,
    res_hbm, send_hbm, b_ref, peak_ref,
    qr_ref, full_ref, num_ref, gs_ref, inv_ref, tr_ref, t_ref, bt_ref, res_ref, send_ref, res_sem, send_sem,
):
    blocks, _, rows, _ = all_ref.shape
    chains = Chains(lens, place[0], blocks, rows)
    parts = split3(f_ref[...])
    for b in range(blocks):
        ql = logits_of(all_ref[b, Q], parts)
        qr_ref[b] = jnp.exp(ql - jnp.max(ql, axis=1, keepdims=True)) * RATIO
    peak = jnp.max(jnp.max(z_ref[...], axis=0), axis=0, keepdims=True)
    peak_ref[...] = jnp.broadcast_to(peak, peak_ref.shape)
    row = lax.broadcasted_iota(jnp.int32, (M + 8, D), 0)
    share = jnp.where(row == VALUES, 1.0, jnp.exp(s_ref[0, PEAK : PEAK + 1, :] - peak))
    for c in range(CHAINS):
        full_ref[c] = s_ref[c] * share
    for r in range(sent_ref.shape[0]):
        ends = chains.ends_of(r)

        @pl.when(chains.me != r)
        def _():
            share = jnp.where(row == VALUES, 1.0, jnp.exp(sent_ref[r, 0, PEAK : PEAK + 1, :] - peak))
            for i, c in enumerate(ends):
                full_ref[c] += sent_ref[r, i] * share

    for c in range(CHAINS):
        count = lens[0, c].astype(F32)
        t_ref[c : c + 1, :] = RATIO * (full_ref[c, TOTALS : TOTALS + 1, :] + EPS * count)
    b_ref[...] = jnp.zeros_like(b_ref)
    low, high = chains.ends_of(chains.me)

    def one(c, carry):
        state = RATIO * (full_ref[c, :M, :] + EPS * full_ref[c, VALUES : VALUES + 1, :])
        state = split(state)
        weights = t_ref[pl.ds(c, 1), :]
        back = jnp.zeros((M, D), F32)
        for b in range(blocks):
            mask = chains.mask(c, b)
            qf = qr_ref[b] + EPS * RATIO
            inv = 1.0 / jnp.sum(qf * weights, axis=1, keepdims=True)
            inv_ref[b] = jnp.where(mask, inv, inv_ref[b])
            tr_ref[b] = jnp.where(mask, weights, tr_ref[b])
            num = dot3(split(qf), state, NN)
            num_ref[b] = jnp.where(mask, num, num_ref[b])
            g = all_ref[b, G].astype(BF16)
            gs = dot(g, state[0], NT) + dot(g, state[1], NT)
            gs_ref[b] = jnp.where(mask, gs, gs_ref[b])
            hi, lo = split(jnp.where(mask, qf * inv, 0.0))
            back = back + (dot(hi, g, TN) + dot(lo, g, TN))
        b_ref[c] = back
        return carry

    lax.fori_loop(low, high + 1, one, 0)
    feats = parts[:2]
    stores = [pltpu.make_async_copy(res_ref.at[b], res_hbm.at[b], res_sem.at[b]) for b in range(blocks)]
    for b in range(blocks):
        inv = inv_ref[b]
        exact = num_ref[b] * inv
        res_ref[b, OUT] = exact
        grad_denom = -jnp.sum(all_ref[b, G] * exact, axis=1, keepdims=True) * inv
        raised = qr_ref[b]
        num_ref[b] = (raised + EPS * RATIO) * grad_denom
        grad_logits = (gs_ref[b] * inv + grad_denom * tr_ref[b]) * raised
        back = dot3(split(grad_logits), feats, NN)
        back = back - jnp.sum(grad_logits, axis=1, keepdims=True) * (SCALE * all_ref[b, Q])
        res_ref[b, GQ] = back * SCALE
        stores[b].start()
    bt_ref[...] = jnp.zeros_like(bt_ref)

    def two(c, carry):
        total = jnp.zeros((rows, M), F32)
        for b in range(blocks):
            total = total + jnp.where(chains.mask(c, b), num_ref[b], 0.0)
        bt_ref[pl.ds(c, 1), :] = jnp.sum(total, axis=0, keepdims=True)
        return carry

    lax.fori_loop(low, high + 1, two, 0)
    send_ref[0:M, :] = b_ref[low]
    send_ref[M : 2 * M, :] = b_ref[high] * (high != low).astype(F32)
    send_ref[2 * M :, :] = bt_ref[...]
    store = pltpu.make_async_copy(send_ref, send_hbm, send_sem)
    store.start()
    for one_store in stores:
        one_store.wait()
    store.wait()


def key_kernel(
    lens, place, all_ref, f_ref, peak_ref, b_ref, sent_ref,
    res_hbm, kr_ref, full_ref, sum_ref, dk_ref, res_ref, res_sem,
):
    blocks, _, rows, _ = all_ref.shape
    chains = Chains(lens, place[0], blocks, rows)
    parts = split3(f_ref[...])
    peak = peak_ref[0:1, :]
    for b in range(blocks):
        kr_ref[b] = jnp.exp(logits_of(all_ref[b, K], parts) - peak) * RATIO
    full_ref[...] = b_ref[...]
    for r in range(sent_ref.shape[0]):
        low, high = chains.ends_of(r)

        @pl.when(chains.me != r)
        def _():
            full_ref[low] += sent_ref[r, :M, :]
            full_ref[high] += sent_ref[r, M : 2 * M, :]

    sum_ref[...] = jnp.sum(sent_ref[:, 2 * M :, :], axis=0)
    low, high = chains.ends_of(chains.me)

    def one(c, carry):
        back = split(full_ref[c])
        total = sum_ref[pl.ds(c, 1), :]
        for b in range(blocks):
            mask = chains.mask(c, b)
            dv = dot3(split(kr_ref[b] + EPS * RATIO), back, NN)
            res_ref[b, GV] = jnp.where(mask, dv, res_ref[b, GV])
            v = all_ref[b, V].astype(BF16)
            dk = dot(v, back[0], NT) + dot(v, back[1], NT) + total
            dk_ref[b] = jnp.where(mask, dk, dk_ref[b])
        return carry

    lax.fori_loop(low, high + 1, one, 0)
    feats = parts[:2]
    stores = [pltpu.make_async_copy(res_ref.at[b], res_hbm.at[b], res_sem.at[b]) for b in range(blocks)]
    for b in range(blocks):
        grad_logits = dk_ref[b] * kr_ref[b]
        back = dot3(split(grad_logits), feats, NN)
        back = back - jnp.sum(grad_logits, axis=1, keepdims=True) * (SCALE * all_ref[b, K])
        res_ref[b, GK] = back * SCALE
        stores[b].start()
    for store in stores:
        store.wait()


def unpack_kernel(res_ref, *outs):
    for h in range(H):
        for i, out in enumerate(outs):
            out[:, head(h)] = res_ref[h, i].astype(BF16)


def is_hbm(shape):
    return getattr(shape, "memory_space", None) is pltpu.HBM


def call(kernel, shapes, args, scalars=0, scratch=()):
    vmem = pl.BlockSpec(memory_space=pltpu.VMEM)
    smem = pl.BlockSpec(memory_space=pltpu.SMEM)
    hbm = pl.BlockSpec(memory_space=pltpu.HBM)
    return pl.pallas_call(
        kernel,
        out_shape=shapes,
        in_specs=[smem] * scalars + [vmem] * (len(args) - scalars),
        out_specs=[hbm if is_hbm(a) else vmem for a in shapes],
        scratch_shapes=list(scratch),
        compiler_params=pltpu.CompilerParams(vmem_limit_bytes=40 * 2**20),
    )(*args)


def f32(*shape):
    return jax.ShapeDtypeStruct(shape, F32)


def on_device(queries, keys, values, grad_attended, features, chain_lengths):
    rows, width = queries.shape[1:]
    q, k, v, g = (a.reshape(rows, width) for a in (queries, keys, values, grad_attended))
    place = jnp.stack([lax.axis_index("row"), lax.axis_index("col")]).astype(jnp.int32)
    where = (chain_lengths, place)
    groups, lines, blocks = (lax.axis_size(a) for a in ("grp", "row", "col"))
    wide = (blocks, rows, D)
    hbm = pl.BlockSpec(memory_space=pltpu.HBM)
    packed = pl.pallas_call(
        pack_kernel,
        out_shape=f32(H, 4, rows, D),
        in_specs=[hbm] * 4,
        out_specs=hbm,
        scratch_shapes=[
            pltpu.VMEM((4, rows, width), BF16),
            pltpu.VMEM((H, 4, rows, D), F32),
            pltpu.SemaphoreType.DMA((4,)),
            pltpu.SemaphoreType.DMA((H,)),
        ],
        compiler_params=pltpu.CompilerParams(vmem_limit_bytes=60 * 2**20),
    )(k, v, q, g)
    own = lax.all_to_all(packed, "col", 0, 0, tiled=True)
    states = (CHAINS, M + 8, D)
    peers = (groups * lines, 8, M)
    dma = pltpu.SemaphoreType.DMA
    peaks, own_states, ends = call(
        state_kernel,
        [pltpu.HBM(peers, F32), f32(*states), pltpu.HBM((2, M + 8, D), F32)],
        (*where, own, features),
        2,
        [pltpu.VMEM(wide, F32), pltpu.VMEM((2, M + 8, D), F32), pltpu.VMEM(peers, F32), dma, dma],
    )
    peaks = lax.all_to_all(peaks, ("grp", "row"), 0, 0, tiled=True)
    ends = lax.all_gather(ends, "row")
    pair = (blocks, 2, rows, D)
    back = (2 * M + 2 * CHAINS, D)
    small = (2 * CHAINS, M)
    first, back_ends, backs, peak = call(
        query_kernel,
        [pltpu.HBM(pair, F32), pltpu.HBM(back, F32), f32(CHAINS, M, D), f32(*small)],
        (*where, own, features, peaks, own_states, ends),
        2,
        [pltpu.VMEM(wide, F32), pltpu.VMEM(states, F32)]
        + [pltpu.VMEM(wide, F32)] * 4
        + [pltpu.VMEM(small, F32)] * 2
        + [pltpu.VMEM(pair, F32), pltpu.VMEM(back, F32), dma((blocks,)), dma],
    )
    first = lax.all_to_all(first, "col", 0, 0, tiled=True)
    back_ends = lax.all_gather(back_ends, "row")
    (second,) = call(
        key_kernel,
        [pltpu.HBM(pair, F32)],
        (*where, own, features, peak, backs, back_ends),
        2,
        [pltpu.VMEM(wide, F32), pltpu.VMEM((CHAINS, M, D), F32), pltpu.VMEM(small, F32)]
        + [pltpu.VMEM(wide, F32), pltpu.VMEM(pair, F32), dma((blocks,))],
    )
    second = lax.all_to_all(second, "col", 0, 0, tiled=True)
    narrow = [jax.ShapeDtypeStruct((rows, width), BF16)] * 2
    outs = (*call(unpack_kernel, narrow, (first,)), *call(unpack_kernel, narrow, (second,)))
    return tuple(a.reshape(1, rows, width) for a in outs)


def solution(mesh):
    groups, seq = mesh.devices.shape
    fine = Mesh(mesh.devices.reshape(groups, seq // H, H), ("grp", "row", "col"))
    rows = P("grp", ("row", "col"), None)
    return jax.shard_map(
        on_device,
        mesh=fine,
        in_specs=(rows, rows, rows, rows, P(), P("grp", None)),
        out_specs=(rows, rows, rows, rows),
        check_vma=False,
    )
```

```python
import jax
import jax.numpy as jnp
from jax import lax
from jax.experimental import pallas as pl
from jax.experimental.pallas import tpu as pltpu
from jax.sharding import Mesh
from jax.sharding import PartitionSpec as P

H = 8
D = 128
M = 128
CHAINS = 4
EPS = 1e-06
SCALE = D ** (-0.25)
RATIO = M ** (-0.5)
F32 = jnp.float32
BF16 = jnp.bfloat16
NN = (((1,), (0,)), ((), ()))
NT = (((1,), (1,)), ((), ()))
TN = (((0,), (0,)), ((), ()))
K, V, Q, G = range(4)
OUT, GQ = range(2)
GK, GV = range(2)
VALUES, TOTALS, PEAK = M, M + 1, M + 2


def dot(a, b, dims):
    return lax.dot_general(a, b, dims, preferred_element_type=F32)


def split(x):
    hi = x.astype(BF16)
    return hi, (x - hi.astype(F32)).astype(BF16)


def split3(x):
    hi = x.astype(BF16)
    rest = x - hi.astype(F32)
    mid = rest.astype(BF16)
    return hi, mid, (rest - mid.astype(F32)).astype(BF16)


def dot3(a, b, dims):
    (ah, al), (bh, bl) = a, b
    return dot(ah, bh, dims) + (dot(ah, bl, dims) + dot(al, bh, dims))


def head(h):
    return slice(h * D, (h + 1) * D)


def logits_of(x, parts):
    f1, f2, f3 = parts
    y = x.astype(BF16)
    z = dot(y, f1, NT) + (dot(y, f2, NT) + dot(y, f3, NT))
    return SCALE * z - (0.5 * SCALE * SCALE) * jnp.sum(x * x, axis=1, keepdims=True)


class Chains:
    def __init__(self, lens, me, blocks, rows):
        self.rows = rows
        self.span = blocks * rows
        self.me = me
        l0, l1, l2 = lens[0, 0], lens[0, 1], lens[0, 2]
        self.starts = (jnp.int32(0), l0, l0 + l1, l0 + l1 + l2)
        self.lens = lens

    def count_ended(self, position):
        c = jnp.int32(0)
        for s in self.starts[1:]:
            c = c + (position >= s).astype(jnp.int32)
        return c

    def ends_of(self, which):
        return self.count_ended(which * self.span), self.count_ended((which + 1) * self.span - 1)

    def start_of(self, c):
        s = self.starts
        return jnp.where(c == 0, s[0], jnp.where(c == 1, s[1], jnp.where(c == 2, s[2], s[3])))

    def mask(self, c, block):
        low = self.start_of(c) - (self.me * self.span + block * self.rows)
        at = lax.broadcasted_iota(jnp.int32, (self.rows, D), 0)
        return (at >= low) & (at < low + self.lens[0, c])


def pack_kernel(k_hbm, v_hbm, q_hbm, g_hbm, out_hbm, rows_ref, wide_ref, in_sem, out_sem):
    sources = (k_hbm, v_hbm, q_hbm, g_hbm)
    loads = [pltpu.make_async_copy(r, rows_ref.at[i], in_sem.at[i]) for i, r in enumerate(sources)]
    for load in loads:
        load.start()
    for load in loads:
        load.wait()
    stores = [pltpu.make_async_copy(wide_ref.at[h], out_hbm.at[h], out_sem.at[h]) for h in range(H)]
    for h in range(H):
        for i in range(4):
            wide_ref[h, i] = rows_ref[i, :, head(h)].astype(F32)
        stores[h].start()
    for store in stores:
        store.wait()


def peak_kernel(k_ref, f_ref, peak_ref):
    parts = split3(f_ref[...])
    for h in range(H):
        logits = logits_of(k_ref[:, head(h)].astype(F32), parts)
        peak = jnp.max(logits, axis=(0, 1), keepdims=True)
        peak_ref[h : h + 1, :] = jnp.broadcast_to(peak, (1, M))


def state_kernel(
    lens, place, all_ref, f_ref, lines_ref, z_hbm, s_ref, send_hbm, er_ref, send_ref, z_ref, sem, z_sem
):
    blocks, _, rows, _ = all_ref.shape
    chains = Chains(lens, place[0], blocks, rows)
    parts = split3(f_ref[...])
    peak = jnp.full((1, 1), -jnp.inf, F32)
    for b in range(blocks):
        logits = logits_of(all_ref[b, K], parts)
        er_ref[b] = logits
        peak = jnp.maximum(peak, jnp.max(logits, axis=(0, 1), keepdims=True))
    for b in range(blocks):
        er_ref[b] = jnp.exp(er_ref[b] - peak)
    for i in range(z_ref.shape[0]):
        h = i % H
        z_ref[i] = jnp.broadcast_to(lines_ref[h : h + 1, :], z_ref.shape[1:])
    z_store = pltpu.make_async_copy(z_ref, z_hbm, z_sem)
    z_store.start()
    s_ref[...] = jnp.zeros_like(s_ref)
    for c in range(CHAINS):
        s_ref[c, PEAK : PEAK + 1, :] = jnp.broadcast_to(peak, (1, D))
    low, high = chains.ends_of(chains.me)

    def one(c, carry):
        state = jnp.zeros((M, D), F32)
        values = jnp.zeros((rows, D), F32)
        totals = jnp.zeros((rows, M), F32)
        for b in range(blocks):
            mask = chains.mask(c, b)
            raised = jnp.where(mask, er_ref[b], 0.0)
            totals = totals + raised
            hi, lo = split(raised)
            v = all_ref[b, V]
            values = values + jnp.where(mask, v, 0.0)
            v = v.astype(BF16)
            state = state + (dot(hi, v, TN) + dot(lo, v, TN))
        s_ref[c, :M, :] = state
        s_ref[c, VALUES : VALUES + 1, :] = jnp.sum(values, axis=0, keepdims=True)
        s_ref[c, TOTALS : TOTALS + 1, :] = jnp.sum(totals, axis=0, keepdims=True)
        return carry

    lax.fori_loop(low, high + 1, one, 0)
    send_ref[0] = s_ref[low]
    send_ref[1] = s_ref[high] * (high != low).astype(F32)
    store = pltpu.make_async_copy(send_ref, send_hbm, sem)
    store.start()
    z_store.wait()
    store.wait()


def query_kernel(
    lens, place, all_ref, f_ref, z_ref, s_ref, sent_ref,
    res_hbm, send_hbm, b_ref, peak_ref,
    qr_ref, full_ref, num_ref, gs_ref, inv_ref, tr_ref, t_ref, bt_ref, res_ref, send_ref, res_sem, send_sem,
):
    blocks, _, rows, _ = all_ref.shape
    chains = Chains(lens, place[0], blocks, rows)
    parts = split3(f_ref[...])
    for b in range(blocks):
        ql = logits_of(all_ref[b, Q], parts)
        qr_ref[b] = jnp.exp(ql - jnp.max(ql, axis=1, keepdims=True)) * RATIO
    peak = jnp.max(jnp.max(z_ref[...], axis=0), axis=0, keepdims=True)
    peak_ref[...] = jnp.broadcast_to(peak, peak_ref.shape)
    row = lax.broadcasted_iota(jnp.int32, (M + 8, D), 0)
    share = jnp.where(row == VALUES, 1.0, jnp.exp(s_ref[0, PEAK : PEAK + 1, :] - peak))
    for c in range(CHAINS):
        full_ref[c] = s_ref[c] * share
    for r in range(sent_ref.shape[0]):
        ends = chains.ends_of(r)

        @pl.when(chains.me != r)
        def _():
            share = jnp.where(row == VALUES, 1.0, jnp.exp(sent_ref[r, 0, PEAK : PEAK + 1, :] - peak))
            for i, c in enumerate(ends):
                full_ref[c] += sent_ref[r, i] * share

    for c in range(CHAINS):
        count = lens[0, c].astype(F32)
        t_ref[c : c + 1, :] = RATIO * (full_ref[c, TOTALS : TOTALS + 1, :] + EPS * count)
    b_ref[...] = jnp.zeros_like(b_ref)
    low, high = chains.ends_of(chains.me)

    def one(c, carry):
        state = RATIO * (full_ref[c, :M, :] + EPS * full_ref[c, VALUES : VALUES + 1, :])
        state = split(state)
        weights = t_ref[pl.ds(c, 1), :]
        back = jnp.zeros((M, D), F32)
        for b in range(blocks):
            mask = chains.mask(c, b)
            qf = qr_ref[b] + EPS * RATIO
            inv = 1.0 / jnp.sum(qf * weights, axis=1, keepdims=True)
            inv_ref[b] = jnp.where(mask, inv, inv_ref[b])
            tr_ref[b] = jnp.where(mask, weights, tr_ref[b])
            num = dot3(split(qf), state, NN)
            num_ref[b] = jnp.where(mask, num, num_ref[b])
            g = all_ref[b, G].astype(BF16)
            gs = dot(g, state[0], NT) + dot(g, state[1], NT)
            gs_ref[b] = jnp.where(mask, gs, gs_ref[b])
            hi, lo = split(jnp.where(mask, qf * inv, 0.0))
            back = back + (dot(hi, g, TN) + dot(lo, g, TN))
        b_ref[c] = back
        return carry

    lax.fori_loop(low, high + 1, one, 0)
    feats = parts[:2]
    stores = [pltpu.make_async_copy(res_ref.at[b], res_hbm.at[b], res_sem.at[b]) for b in range(blocks)]
    for b in range(blocks):
        inv = inv_ref[b]
        exact = num_ref[b] * inv
        res_ref[b, OUT] = exact
        grad_denom = -jnp.sum(all_ref[b, G] * exact, axis=1, keepdims=True) * inv
        raised = qr_ref[b]
        num_ref[b] = (raised + EPS * RATIO) * grad_denom
        grad_logits = (gs_ref[b] * inv + grad_denom * tr_ref[b]) * raised
        back = dot3(split(grad_logits), feats, NN)
        back = back - jnp.sum(grad_logits, axis=1, keepdims=True) * (SCALE * all_ref[b, Q])
        res_ref[b, GQ] = back * SCALE
        stores[b].start()
    bt_ref[...] = jnp.zeros_like(bt_ref)

    def two(c, carry):
        total = jnp.zeros((rows, M), F32)
        for b in range(blocks):
            total = total + jnp.where(chains.mask(c, b), num_ref[b], 0.0)
        bt_ref[pl.ds(c, 1), :] = jnp.sum(total, axis=0, keepdims=True)
        return carry

    lax.fori_loop(low, high + 1, two, 0)
    send_ref[0:M, :] = b_ref[low]
    send_ref[M : 2 * M, :] = b_ref[high] * (high != low).astype(F32)
    send_ref[2 * M :, :] = bt_ref[...]
    store = pltpu.make_async_copy(send_ref, send_hbm, send_sem)
    store.start()
    for one_store in stores:
        one_store.wait()
    store.wait()


def key_kernel(
    lens, place, all_ref, f_ref, peak_ref, b_ref, sent_ref,
    res_hbm, kr_ref, full_ref, sum_ref, dk_ref, res_ref, res_sem,
):
    blocks, _, rows, _ = all_ref.shape
    chains = Chains(lens, place[0], blocks, rows)
    parts = split3(f_ref[...])
    peak = peak_ref[0:1, :]
    for b in range(blocks):
        kr_ref[b] = jnp.exp(logits_of(all_ref[b, K], parts) - peak) * RATIO
    full_ref[...] = b_ref[...]
    for r in range(sent_ref.shape[0]):
        low, high = chains.ends_of(r)

        @pl.when(chains.me != r)
        def _():
            full_ref[low] += sent_ref[r, :M, :]
            full_ref[high] += sent_ref[r, M : 2 * M, :]

    sum_ref[...] = jnp.sum(sent_ref[:, 2 * M :, :], axis=0)
    low, high = chains.ends_of(chains.me)

    def one(c, carry):
        back = split(full_ref[c])
        total = sum_ref[pl.ds(c, 1), :]
        for b in range(blocks):
            mask = chains.mask(c, b)
            dv = dot3(split(kr_ref[b] + EPS * RATIO), back, NN)
            res_ref[b, GV] = jnp.where(mask, dv, res_ref[b, GV])
            v = all_ref[b, V].astype(BF16)
            dk = dot(v, back[0], NT) + dot(v, back[1], NT) + total
            dk_ref[b] = jnp.where(mask, dk, dk_ref[b])
        return carry

    lax.fori_loop(low, high + 1, one, 0)
    feats = parts[:2]
    stores = [pltpu.make_async_copy(res_ref.at[b], res_hbm.at[b], res_sem.at[b]) for b in range(blocks)]
    for b in range(blocks):
        grad_logits = dk_ref[b] * kr_ref[b]
        back = dot3(split(grad_logits), feats, NN)
        back = back - jnp.sum(grad_logits, axis=1, keepdims=True) * (SCALE * all_ref[b, K])
        res_ref[b, GK] = back * SCALE
        stores[b].start()
    for store in stores:
        store.wait()


def unpack_kernel(res_ref, *outs):
    for h in range(H):
        for i, out in enumerate(outs):
            out[:, head(h)] = res_ref[h, i].astype(BF16)


def is_hbm(shape):
    return getattr(shape, "memory_space", None) is pltpu.HBM


def call(kernel, shapes, args, scalars=0, scratch=(), limit=40):
    vmem = pl.BlockSpec(memory_space=pltpu.VMEM)
    smem = pl.BlockSpec(memory_space=pltpu.SMEM)
    hbm = pl.BlockSpec(memory_space=pltpu.HBM)
    return pl.pallas_call(
        kernel,
        out_shape=shapes,
        in_specs=[smem] * scalars + [vmem] * (len(args) - scalars),
        out_specs=[hbm if is_hbm(a) else vmem for a in shapes],
        scratch_shapes=list(scratch),
        compiler_params=pltpu.CompilerParams(vmem_limit_bytes=limit * 2**20),
    )(*args)


def f32(*shape):
    return jax.ShapeDtypeStruct(shape, F32)


def max_over(x, axis):
    count = lax.axis_size(axis)
    reach = 0
    while 2 * reach + 1 < count:
        step = min(2 * reach + 1, count // 2 - reach)
        up = lax.ppermute(x, axis, [(i, (i + step) % count) for i in range(count)])
        down = lax.ppermute(x, axis, [(i, (i - step) % count) for i in range(count)])
        x = jnp.maximum(x, jnp.maximum(up, down))
        reach += step
    return x


def on_device(queries, keys, values, grad_attended, features, chain_lengths):
    rows, width = queries.shape[1:]
    q, k, v, g = (a.reshape(rows, width) for a in (queries, keys, values, grad_attended))
    place = jnp.stack([lax.axis_index("row"), lax.axis_index("col")]).astype(jnp.int32)
    where = (chain_lengths, place)
    lines, blocks = (lax.axis_size(a) for a in ("row", "col"))
    wide = (blocks, rows, D)
    hbm = pl.BlockSpec(memory_space=pltpu.HBM)
    (peaks,) = call(peak_kernel, [f32(H, M)], (k, features), limit=60)
    peaks = max_over(peaks, "grp")
    packed = pl.pallas_call(
        pack_kernel,
        out_shape=f32(H, 4, rows, D),
        in_specs=[hbm] * 4,
        out_specs=hbm,
        scratch_shapes=[
            pltpu.VMEM((4, rows, width), BF16),
            pltpu.VMEM((H, 4, rows, D), F32),
            pltpu.SemaphoreType.DMA((4,)),
            pltpu.SemaphoreType.DMA((H,)),
        ],
        compiler_params=pltpu.CompilerParams(vmem_limit_bytes=60 * 2**20),
    )(k, v, q, g)
    own = lax.all_to_all(packed, "col", 0, 0, tiled=True)
    states = (CHAINS, M + 8, D)
    peers = (lines * blocks, 8, M)
    dma = pltpu.SemaphoreType.DMA
    peaks, own_states, ends = call(
        state_kernel,
        [pltpu.HBM(peers, F32), pltpu.VMEM(states, F32), pltpu.HBM((2, M + 8, D), F32)],
        (*where, own, features, peaks),
        2,
        [pltpu.VMEM(wide, F32), pltpu.VMEM((2, M + 8, D), F32), pltpu.VMEM(peers, F32), dma, dma],
    )
    peaks = lax.all_to_all(peaks, ("row", "col"), 0, 0, tiled=True)
    ends = lax.all_gather(ends, "row")
    pair = (blocks, 2, rows, D)
    back = (2 * M + 2 * CHAINS, D)
    small = (2 * CHAINS, M)
    first, back_ends, backs, peak = call(
        query_kernel,
        [pltpu.HBM(pair, F32), pltpu.HBM(back, F32), pltpu.VMEM((CHAINS, M, D), F32), f32(*small)],
        (*where, own, features, peaks, own_states, ends),
        2,
        [pltpu.VMEM(wide, F32), pltpu.VMEM(states, F32)]
        + [pltpu.VMEM(wide, F32)] * 4
        + [pltpu.VMEM(small, F32)] * 2
        + [pltpu.VMEM(pair, F32), pltpu.VMEM(back, F32), dma((blocks,)), dma],
    )
    first = lax.all_to_all(first, "col", 0, 0, tiled=True)
    back_ends = lax.all_gather(back_ends, "row")
    (second,) = call(
        key_kernel,
        [pltpu.HBM(pair, F32)],
        (*where, own, features, peak, backs, back_ends),
        2,
        [pltpu.VMEM(wide, F32), pltpu.VMEM((CHAINS, M, D), F32), pltpu.VMEM(small, F32)]
        + [pltpu.VMEM(wide, F32), pltpu.VMEM(pair, F32), dma((blocks,))],
    )
    second = lax.all_to_all(second, "col", 0, 0, tiled=True)
    narrow = [jax.ShapeDtypeStruct((rows, width), BF16)] * 2
    outs = (*call(unpack_kernel, narrow, (first,)), *call(unpack_kernel, narrow, (second,)))
    return tuple(a.reshape(1, rows, width) for a in outs)


def solution(mesh):
    groups, seq = mesh.devices.shape
    fine = Mesh(mesh.devices.reshape(groups, seq // H, H), ("grp", "row", "col"))
    rows = P("grp", ("row", "col"), None)
    return jax.shard_map(
        on_device,
        mesh=fine,
        in_specs=(rows, rows, rows, rows, P(), P("grp", None)),
        out_specs=(rows, rows, rows, rows),
        check_vma=False,
    )
```

```python
import jax
import jax.numpy as jnp
from jax import lax
from jax.experimental import pallas as pl
from jax.experimental.pallas import tpu as pltpu
from jax.sharding import Mesh
from jax.sharding import PartitionSpec as P

H = 8
D = 128
M = 128
CHAINS = 4
EPS = 1e-06
SCALE = D ** (-0.25)
RATIO = M ** (-0.5)
F32 = jnp.float32
BF16 = jnp.bfloat16
NN = (((1,), (0,)), ((), ()))
NT = (((1,), (1,)), ((), ()))
TN = (((0,), (0,)), ((), ()))
K, V = range(2)
Q, G = range(2)
OUT, GQ = range(2)
GK, GV = range(2)
VALUES, TOTALS, PEAK = M, M + 1, M + 2


def dot(a, b, dims):
    return lax.dot_general(a, b, dims, preferred_element_type=F32)


def split(x):
    hi = x.astype(BF16)
    return hi, (x - hi.astype(F32)).astype(BF16)


def split3(x):
    hi = x.astype(BF16)
    rest = x - hi.astype(F32)
    mid = rest.astype(BF16)
    return hi, mid, (rest - mid.astype(F32)).astype(BF16)


def dot3(a, b, dims):
    (ah, al), (bh, bl) = a, b
    return dot(ah, bh, dims) + (dot(ah, bl, dims) + dot(al, bh, dims))


def head(h):
    return slice(h * D, (h + 1) * D)


def logits_of(x, parts):
    f1, f2, f3 = parts
    y = x.astype(BF16)
    z = dot(y, f1, NT) + (dot(y, f2, NT) + dot(y, f3, NT))
    return SCALE * z - (0.5 * SCALE * SCALE) * jnp.sum(x * x, axis=1, keepdims=True)


class Chains:
    def __init__(self, lens, me, blocks, rows):
        self.rows = rows
        self.span = blocks * rows
        self.me = me
        l0, l1, l2 = lens[0, 0], lens[0, 1], lens[0, 2]
        self.starts = (jnp.int32(0), l0, l0 + l1, l0 + l1 + l2)
        self.lens = lens

    def count_ended(self, position):
        c = jnp.int32(0)
        for s in self.starts[1:]:
            c = c + (position >= s).astype(jnp.int32)
        return c

    def ends_of(self, which):
        return self.count_ended(which * self.span), self.count_ended((which + 1) * self.span - 1)

    def start_of(self, c):
        s = self.starts
        return jnp.where(c == 0, s[0], jnp.where(c == 1, s[1], jnp.where(c == 2, s[2], s[3])))

    def mask(self, c, block):
        low = self.start_of(c) - (self.me * self.span + block * self.rows)
        at = lax.broadcasted_iota(jnp.int32, (self.rows, D), 0)
        return (at >= low) & (at < low + self.lens[0, c])


def pack_kernel(first_hbm, second_hbm, out_hbm, rows_ref, wide_ref, in_sem, out_sem):
    sources = (first_hbm, second_hbm)
    loads = [pltpu.make_async_copy(r, rows_ref.at[i], in_sem.at[i]) for i, r in enumerate(sources)]
    for load in loads:
        load.start()
    for load in loads:
        load.wait()
    stores = [pltpu.make_async_copy(wide_ref.at[h], out_hbm.at[h], out_sem.at[h]) for h in range(H)]
    for h in range(H):
        for i in range(2):
            wide_ref[h, i] = rows_ref[i, :, head(h)].astype(F32)
        stores[h].start()
    for store in stores:
        store.wait()


def state_kernel(lens, place, all_ref, f_ref, s_ref, send_hbm, er_ref, send_ref, sem):
    blocks, _, rows, _ = all_ref.shape
    chains = Chains(lens, place[0], blocks, rows)
    parts = split3(f_ref[...])
    peak = jnp.full((1, 1), -jnp.inf, F32)
    for b in range(blocks):
        logits = logits_of(all_ref[b, K], parts)
        er_ref[b] = logits
        peak = jnp.maximum(peak, jnp.max(logits, axis=(0, 1), keepdims=True))
    for b in range(blocks):
        er_ref[b] = jnp.exp(er_ref[b] - peak)
    s_ref[...] = jnp.zeros_like(s_ref)
    for c in range(CHAINS):
        s_ref[c, PEAK : PEAK + 1, :] = jnp.broadcast_to(peak, (1, D))
    low, high = chains.ends_of(chains.me)

    def one(c, carry):
        state = jnp.zeros((M, D), F32)
        values = jnp.zeros((rows, D), F32)
        totals = jnp.zeros((rows, M), F32)
        for b in range(blocks):
            mask = chains.mask(c, b)
            raised = jnp.where(mask, er_ref[b], 0.0)
            totals = totals + raised
            hi, lo = split(raised)
            v = all_ref[b, V]
            values = values + jnp.where(mask, v, 0.0)
            v = v.astype(BF16)
            state = state + (dot(hi, v, TN) + dot(lo, v, TN))
        s_ref[c, :M, :] = state
        s_ref[c, VALUES : VALUES + 1, :] = jnp.sum(values, axis=0, keepdims=True)
        s_ref[c, TOTALS : TOTALS + 1, :] = jnp.sum(totals, axis=0, keepdims=True)
        return carry

    lax.fori_loop(low, high + 1, one, 0)
    send_ref[0] = s_ref[low]
    send_ref[1] = s_ref[high] * (high != low).astype(F32)
    store = pltpu.make_async_copy(send_ref, send_hbm, sem)
    store.start()
    store.wait()


def peak_kernel(sent_ref, wait_ref, z_hbm, z_ref, sem):
    peak = jnp.max(sent_ref[:, 0, PEAK : PEAK + 1, :], axis=0)
    for i in range(z_ref.shape[0]):
        z_ref[i] = jnp.broadcast_to(peak, z_ref.shape[1:])
    store = pltpu.make_async_copy(z_ref, z_hbm, sem)
    store.start()
    store.wait()


def ahead_kernel(lens, place, all_ref, f_ref, s_ref, sent_ref, full_ref, qr_ref, num_ref, gs_ref):
    blocks, _, rows, _ = all_ref.shape
    chains = Chains(lens, place[0], blocks, rows)
    parts = split3(f_ref[...])
    for b in range(blocks):
        ql = logits_of(all_ref[b, Q], parts)
        qr_ref[b] = jnp.exp(ql - jnp.max(ql, axis=1, keepdims=True)) * RATIO
    peak = jnp.max(sent_ref[:, 0, PEAK : PEAK + 1, :], axis=0)
    row = lax.broadcasted_iota(jnp.int32, (M + 8, D), 0)
    share = jnp.where(row == VALUES, 1.0, jnp.exp(s_ref[0, PEAK : PEAK + 1, :] - peak))
    for c in range(CHAINS):
        full_ref[c] = s_ref[c] * share
    for r in range(sent_ref.shape[0]):
        ends = chains.ends_of(r)

        @pl.when(chains.me != r)
        def _():
            share = jnp.where(row == VALUES, 1.0, jnp.exp(sent_ref[r, 0, PEAK : PEAK + 1, :] - peak))
            for i, c in enumerate(ends):
                full_ref[c] += sent_ref[r, i] * share

    for c in range(CHAINS):
        full_ref[c, PEAK : PEAK + 1, :] = peak
    low, high = chains.ends_of(chains.me)

    def one(c, carry):
        state = split(full_ref[c, :M, :])
        for b in range(blocks):
            mask = chains.mask(c, b)
            num = dot3(split(qr_ref[b] + EPS * RATIO), state, NN)
            num_ref[b] = jnp.where(mask, num, num_ref[b])
            g = all_ref[b, G].astype(BF16)
            gs = dot(g, state[0], NT) + dot(g, state[1], NT)
            gs_ref[b] = jnp.where(mask, gs, gs_ref[b])
        return carry

    lax.fori_loop(low, high + 1, one, 0)


def query_kernel(
    lens, place, all_ref, f_ref, z_ref, full_ref, qr_ref, num_in, gs_in,
    res_hbm, send_hbm, b_ref, peak_ref,
    num_ref, gs_ref, inv_ref, tr_ref, t_ref, bt_ref, res_ref, send_ref, res_sem, send_sem,
):
    blocks, _, rows, _ = all_ref.shape
    chains = Chains(lens, place[0], blocks, rows)
    parts = split(f_ref[...])
    peak = jnp.max(jnp.max(z_ref[...], axis=0), axis=0, keepdims=True)
    peak_ref[...] = jnp.broadcast_to(peak, peak_ref.shape)
    share = RATIO * jnp.exp(full_ref[0, PEAK : PEAK + 1, :] - peak)
    for c in range(CHAINS):
        count = lens[0, c].astype(F32)
        t_ref[c : c + 1, :] = share * full_ref[c, TOTALS : TOTALS + 1, :] + EPS * RATIO * count
    b_ref[...] = jnp.zeros_like(b_ref)
    low, high = chains.ends_of(chains.me)

    def one(c, carry):
        weights = t_ref[pl.ds(c, 1), :]
        values = EPS * RATIO * full_ref[c, VALUES : VALUES + 1, :]
        back = jnp.zeros((M, D), F32)
        for b in range(blocks):
            mask = chains.mask(c, b)
            qf = qr_ref[b] + EPS * RATIO
            inv = 1.0 / jnp.sum(qf * weights, axis=1, keepdims=True)
            inv_ref[b] = jnp.where(mask, inv, inv_ref[b])
            tr_ref[b] = jnp.where(mask, weights, tr_ref[b])
            num = share * num_in[b] + jnp.sum(qf, axis=1, keepdims=True) * values
            num_ref[b] = jnp.where(mask, num, num_ref[b])
            g = all_ref[b, G]
            gs = share * gs_in[b] + jnp.sum(g * values, axis=1, keepdims=True)
            gs_ref[b] = jnp.where(mask, gs, gs_ref[b])
            hi, lo = split(jnp.where(mask, qf * inv, 0.0))
            g = g.astype(BF16)
            back = back + (dot(hi, g, TN) + dot(lo, g, TN))
        b_ref[c] = back
        return carry

    lax.fori_loop(low, high + 1, one, 0)
    feats = parts
    stores = [pltpu.make_async_copy(res_ref.at[b], res_hbm.at[b], res_sem.at[b]) for b in range(blocks)]
    for b in range(blocks):
        inv = inv_ref[b]
        exact = num_ref[b] * inv
        res_ref[b, OUT] = exact
        grad_denom = -jnp.sum(all_ref[b, G] * exact, axis=1, keepdims=True) * inv
        raised = qr_ref[b]
        num_ref[b] = (raised + EPS * RATIO) * grad_denom
        grad_logits = (gs_ref[b] * inv + grad_denom * tr_ref[b]) * raised
        back = dot3(split(grad_logits), feats, NN)
        back = back - jnp.sum(grad_logits, axis=1, keepdims=True) * (SCALE * all_ref[b, Q])
        res_ref[b, GQ] = back * SCALE
        stores[b].start()
    bt_ref[...] = jnp.zeros_like(bt_ref)

    def two(c, carry):
        total = jnp.zeros((rows, M), F32)
        for b in range(blocks):
            total = total + jnp.where(chains.mask(c, b), num_ref[b], 0.0)
        bt_ref[pl.ds(c, 1), :] = jnp.sum(total, axis=0, keepdims=True)
        return carry

    lax.fori_loop(low, high + 1, two, 0)
    send_ref[0:M, :] = b_ref[low]
    send_ref[M : 2 * M, :] = b_ref[high] * (high != low).astype(F32)
    send_ref[2 * M :, :] = bt_ref[...]
    store = pltpu.make_async_copy(send_ref, send_hbm, send_sem)
    store.start()
    for one_store in stores:
        one_store.wait()
    store.wait()


def key_kernel(
    lens, place, all_ref, f_ref, peak_ref, b_ref, sent_ref,
    res_hbm, kr_ref, full_ref, sum_ref, dk_ref, res_ref, res_sem,
):
    blocks, _, rows, _ = all_ref.shape
    chains = Chains(lens, place[0], blocks, rows)
    parts = split3(f_ref[...])
    peak = peak_ref[0:1, :]
    for b in range(blocks):
        kr_ref[b] = jnp.exp(logits_of(all_ref[b, K], parts) - peak) * RATIO
    full_ref[...] = b_ref[...]
    for r in range(sent_ref.shape[0]):
        low, high = chains.ends_of(r)

        @pl.when(chains.me != r)
        def _():
            full_ref[low] += sent_ref[r, :M, :]
            full_ref[high] += sent_ref[r, M : 2 * M, :]

    sum_ref[...] = jnp.sum(sent_ref[:, 2 * M :, :], axis=0)
    low, high = chains.ends_of(chains.me)

    def one(c, carry):
        back = split(full_ref[c])
        total = sum_ref[pl.ds(c, 1), :]
        for b in range(blocks):
            mask = chains.mask(c, b)
            dv = dot3(split(kr_ref[b] + EPS * RATIO), back, NN)
            res_ref[b, GV] = jnp.where(mask, dv, res_ref[b, GV])
            v = all_ref[b, V].astype(BF16)
            dk = dot(v, back[0], NT) + dot(v, back[1], NT) + total
            dk_ref[b] = jnp.where(mask, dk, dk_ref[b])
        return carry

    lax.fori_loop(low, high + 1, one, 0)
    feats = parts[:2]
    stores = [pltpu.make_async_copy(res_ref.at[b], res_hbm.at[b], res_sem.at[b]) for b in range(blocks)]
    for b in range(blocks):
        grad_logits = dk_ref[b] * kr_ref[b]
        back = dot3(split(grad_logits), feats, NN)
        back = back - jnp.sum(grad_logits, axis=1, keepdims=True) * (SCALE * all_ref[b, K])
        res_ref[b, GK] = back * SCALE
        stores[b].start()
    for store in stores:
        store.wait()


def unpack_kernel(res_ref, *outs):
    for h in range(H):
        for i, out in enumerate(outs):
            out[:, head(h)] = res_ref[h, i].astype(BF16)


def is_hbm(shape):
    return getattr(shape, "memory_space", None) is pltpu.HBM


def call(kernel, shapes, args, scalars=0, scratch=()):
    vmem = pl.BlockSpec(memory_space=pltpu.VMEM)
    smem = pl.BlockSpec(memory_space=pltpu.SMEM)
    hbm = pl.BlockSpec(memory_space=pltpu.HBM)
    return pl.pallas_call(
        kernel,
        out_shape=shapes,
        in_specs=[smem] * scalars + [vmem] * (len(args) - scalars),
        out_specs=[hbm if is_hbm(a) else vmem for a in shapes],
        scratch_shapes=list(scratch),
        compiler_params=pltpu.CompilerParams(vmem_limit_bytes=40 * 2**20),
    )(*args)


def f32(*shape):
    return jax.ShapeDtypeStruct(shape, F32)


def on_device(queries, keys, values, grad_attended, features, chain_lengths):
    rows, width = queries.shape[1:]
    q, k, v, g = (a.reshape(rows, width) for a in (queries, keys, values, grad_attended))
    place = jnp.stack([lax.axis_index("row"), lax.axis_index("col")]).astype(jnp.int32)
    where = (chain_lengths, place)
    groups, lines, blocks = (lax.axis_size(a) for a in ("grp", "row", "col"))
    wide = (blocks, rows, D)
    hbm = pl.BlockSpec(memory_space=pltpu.HBM)
    dma = pltpu.SemaphoreType.DMA
    pair = (blocks, 2, rows, D)

    def exchanged(*two):
        packed = pl.pallas_call(
            pack_kernel,
            out_shape=pltpu.HBM((H, 2, rows, D), F32),
            in_specs=[hbm] * 2,
            out_specs=hbm,
            scratch_shapes=[
                pltpu.VMEM((2, rows, width), BF16), pltpu.VMEM((H, 2, rows, D), F32), dma((2,)), dma((H,)),
            ],
            compiler_params=pltpu.CompilerParams(vmem_limit_bytes=60 * 2**20),
        )(*two)
        return lax.all_to_all(packed, "col", 0, 0, tiled=True)

    key_rows, query_rows = exchanged(k, v), exchanged(q, g)
    states = (CHAINS, M + 8, D)
    own_states, ends = call(
        state_kernel,
        [pltpu.VMEM(states, F32), pltpu.HBM((2, M + 8, D), F32)],
        (*where, key_rows, features),
        2,
        [pltpu.VMEM(wide, F32), pltpu.VMEM((2, M + 8, D), F32), dma],
    )
    ends = lax.all_gather(ends, "row")
    peers = (groups, 8, M)
    peaks = pl.pallas_call(
        peak_kernel,
        out_shape=pltpu.HBM(peers, F32),
        in_specs=[pl.BlockSpec(memory_space=pltpu.VMEM), pl.BlockSpec(memory_space=pl.ANY)],
        out_specs=hbm,
        scratch_shapes=[pltpu.VMEM(peers, F32), dma],
    )(ends, query_rows)
    peaks = lax.all_to_all(peaks, "grp", 0, 0, tiled=True)
    full_states, raised, products, grad_products = call(
        ahead_kernel,
        [f32(*states), f32(*wide), f32(*wide), f32(*wide)],
        (*where, query_rows, features, own_states, ends),
        2,
    )
    back = (2 * M + 2 * CHAINS, D)
    small = (2 * CHAINS, M)
    first, back_ends, backs, peak = call(
        query_kernel,
        [pltpu.HBM(pair, F32), pltpu.HBM(back, F32), pltpu.VMEM((CHAINS, M, D), F32), f32(*small)],
        (*where, query_rows, features, peaks, full_states, raised, products, grad_products),
        2,
        [pltpu.VMEM(wide, F32)] * 4
        + [pltpu.VMEM(small, F32)] * 2
        + [pltpu.VMEM(pair, F32), pltpu.VMEM(back, F32), dma((blocks,)), dma],
    )
    first = lax.all_to_all(first, "col", 0, 0, tiled=True)
    back_ends = lax.all_gather(back_ends, "row")
    (second,) = call(
        key_kernel,
        [pltpu.HBM(pair, F32)],
        (*where, key_rows, features, peak, backs, back_ends),
        2,
        [pltpu.VMEM(wide, F32), pltpu.VMEM((CHAINS, M, D), F32), pltpu.VMEM(small, F32)]
        + [pltpu.VMEM(wide, F32), pltpu.VMEM(pair, F32), dma((blocks,))],
    )
    second = lax.all_to_all(second, "col", 0, 0, tiled=True)
    narrow = [jax.ShapeDtypeStruct((rows, width), BF16)] * 2
    outs = (*call(unpack_kernel, narrow, (first,)), *call(unpack_kernel, narrow, (second,)))
    return tuple(a.reshape(1, rows, width) for a in outs)


def solution(mesh):
    groups, seq = mesh.devices.shape
    fine = Mesh(mesh.devices.reshape(groups, seq // H, H), ("grp", "row", "col"))
    rows = P("grp", ("row", "col"), None)
    return jax.shard_map(
        on_device,
        mesh=fine,
        in_specs=(rows, rows, rows, rows, P(), P("grp", None)),
        out_specs=(rows, rows, rows, rows),
        check_vma=False,
    )
```

```python
import jax
import jax.numpy as jnp
from jax import lax
from jax.experimental import pallas as pl
from jax.experimental.pallas import tpu as pltpu
from jax.sharding import Mesh
from jax.sharding import PartitionSpec as P

H = 8
D = 128
M = 128
CHAINS = 4
EPS = 1e-06
SCALE = D ** (-0.25)
RATIO = M ** (-0.5)
F32 = jnp.float32
BF16 = jnp.bfloat16
NN = (((1,), (0,)), ((), ()))
NT = (((1,), (1,)), ((), ()))
TN = (((0,), (0,)), ((), ()))
K, V = range(2)
Q, G = range(2)
OUT, GQ = range(2)
GK, GV = range(2)
VALUES, TOTALS, PEAK = M, M + 1, M + 2


def dot(a, b, dims):
    return lax.dot_general(a, b, dims, preferred_element_type=F32)


def split(x):
    hi = x.astype(BF16)
    return hi, (x - hi.astype(F32)).astype(BF16)


def split3(x):
    hi = x.astype(BF16)
    rest = x - hi.astype(F32)
    mid = rest.astype(BF16)
    return hi, mid, (rest - mid.astype(F32)).astype(BF16)


def dot3(a, b, dims):
    (ah, al), (bh, bl) = a, b
    return dot(ah, bh, dims) + (dot(ah, bl, dims) + dot(al, bh, dims))


def head(h):
    return slice(h * D, (h + 1) * D)


def logits_of(x, parts):
    f1, f2, f3 = parts
    y = x.astype(BF16)
    z = dot(y, f1, NT) + (dot(y, f2, NT) + dot(y, f3, NT))
    return SCALE * z - (0.5 * SCALE * SCALE) * jnp.sum(x * x, axis=1, keepdims=True)


class Chains:
    def __init__(self, lens, me, blocks, rows):
        self.rows = rows
        self.span = blocks * rows
        self.me = me
        l0, l1, l2 = lens[0, 0], lens[0, 1], lens[0, 2]
        self.starts = (jnp.int32(0), l0, l0 + l1, l0 + l1 + l2)
        self.lens = lens

    def count_ended(self, position):
        c = jnp.int32(0)
        for s in self.starts[1:]:
            c = c + (position >= s).astype(jnp.int32)
        return c

    def ends_of(self, which):
        return self.count_ended(which * self.span), self.count_ended((which + 1) * self.span - 1)

    def start_of(self, c):
        s = self.starts
        return jnp.where(c == 0, s[0], jnp.where(c == 1, s[1], jnp.where(c == 2, s[2], s[3])))

    def mask(self, c, block):
        low = self.start_of(c) - (self.me * self.span + block * self.rows)
        at = lax.broadcasted_iota(jnp.int32, (self.rows, D), 0)
        return (at >= low) & (at < low + self.lens[0, c])


def pack_kernel(first_hbm, second_hbm, out_hbm, rows_ref, wide_ref, in_sem, out_sem):
    sources = (first_hbm, second_hbm)
    loads = [pltpu.make_async_copy(r, rows_ref.at[i], in_sem.at[i]) for i, r in enumerate(sources)]
    for load in loads:
        load.start()
    for load in loads:
        load.wait()
    stores = [pltpu.make_async_copy(wide_ref.at[h], out_hbm.at[h], out_sem.at[h]) for h in range(H)]
    for h in range(H):
        for i in range(2):
            wide_ref[h, i] = rows_ref[i, :, head(h)].astype(F32)
        stores[h].start()
    for store in stores:
        store.wait()


def state_kernel(lens, place, all_ref, f_ref, s_ref, send_hbm, er_ref, send_ref, sem):
    blocks, _, rows, _ = all_ref.shape
    chains = Chains(lens, place[0], blocks, rows)
    parts = split3(f_ref[...])
    peak = jnp.full((1, 1), -jnp.inf, F32)
    for b in range(blocks):
        logits = logits_of(all_ref[b, K], parts)
        er_ref[b] = logits
        peak = jnp.maximum(peak, jnp.max(logits, axis=(0, 1), keepdims=True))
    for b in range(blocks):
        er_ref[b] = jnp.exp(er_ref[b] - peak)
    s_ref[...] = jnp.zeros_like(s_ref)
    for c in range(CHAINS):
        s_ref[c, PEAK : PEAK + 1, :] = jnp.broadcast_to(peak, (1, D))
    low, high = chains.ends_of(chains.me)

    def one(c, carry):
        state = jnp.zeros((M, D), F32)
        values = jnp.zeros((rows, D), F32)
        totals = jnp.zeros((rows, M), F32)
        for b in range(blocks):
            mask = chains.mask(c, b)
            raised = jnp.where(mask, er_ref[b], 0.0)
            totals = totals + raised
            hi, lo = split(raised)
            v = all_ref[b, V]
            values = values + jnp.where(mask, v, 0.0)
            v = v.astype(BF16)
            state = state + (dot(hi, v, TN) + dot(lo, v, TN))
        s_ref[c, :M, :] = state
        s_ref[c, VALUES : VALUES + 1, :] = jnp.sum(values, axis=0, keepdims=True)
        s_ref[c, TOTALS : TOTALS + 1, :] = jnp.sum(totals, axis=0, keepdims=True)
        return carry

    lax.fori_loop(low, high + 1, one, 0)
    send_ref[0] = s_ref[low]
    send_ref[1] = s_ref[high] * (high != low).astype(F32)
    store = pltpu.make_async_copy(send_ref, send_hbm, sem)
    store.start()
    store.wait()


def peak_kernel(sent_hbm, wait_ref, z_hbm, tile_ref, z_ref, sems):
    load = pltpu.make_async_copy(sent_hbm.at[:, 0, pl.ds(M, 8), :], tile_ref, sems.at[0])
    load.start()
    load.wait()
    peak = jnp.max(tile_ref[:, PEAK - M : PEAK - M + 1, :], axis=0)
    for i in range(z_ref.shape[0]):
        z_ref[i] = jnp.broadcast_to(peak, z_ref.shape[1:])
    store = pltpu.make_async_copy(z_ref, z_hbm, sems.at[1])
    store.start()
    store.wait()


def ahead_kernel(
    sent_hbm, lens, place, key_ref, all_ref, f_ref, s_ref,
    full_ref, qr_ref, num_ref, gs_ref, num_eps_ref, gs_eps_ref, er_ref, sent_ref, sem,
):
    load = pltpu.make_async_copy(sent_hbm, sent_ref, sem)
    load.start()
    blocks, _, rows, _ = all_ref.shape
    chains = Chains(lens, place[0], blocks, rows)
    parts = split3(f_ref[...])
    for b in range(blocks):
        ql = logits_of(all_ref[b, Q], parts)
        qr_ref[b] = jnp.exp(ql - jnp.max(ql, axis=1, keepdims=True)) * RATIO
    load.wait()
    peak = jnp.max(sent_ref[:, 0, PEAK : PEAK + 1, :], axis=0)
    for b in range(blocks):
        er_ref[b] = jnp.exp(logits_of(key_ref[b, K], parts) - peak)
    row = lax.broadcasted_iota(jnp.int32, (M + 8, D), 0)
    share = jnp.where(row == VALUES, 1.0, jnp.exp(s_ref[0, PEAK : PEAK + 1, :] - peak))
    for c in range(CHAINS):
        full_ref[c] = s_ref[c] * share
    for r in range(sent_ref.shape[0]):
        ends = chains.ends_of(r)

        @pl.when(chains.me != r)
        def _():
            share = jnp.where(row == VALUES, 1.0, jnp.exp(sent_ref[r, 0, PEAK : PEAK + 1, :] - peak))
            for i, c in enumerate(ends):
                full_ref[c] += sent_ref[r, i] * share

    for c in range(CHAINS):
        full_ref[c, PEAK : PEAK + 1, :] = peak
    low, high = chains.ends_of(chains.me)

    def one(c, carry):
        state = split(full_ref[c, :M, :])
        values = EPS * RATIO * full_ref[c, VALUES : VALUES + 1, :]
        for b in range(blocks):
            mask = chains.mask(c, b)
            qf = qr_ref[b] + EPS * RATIO
            num = dot3(split(qf), state, NN)
            num_ref[b] = jnp.where(mask, num, num_ref[b])
            num_eps = jnp.sum(qf, axis=1, keepdims=True) * values
            num_eps_ref[b] = jnp.where(mask, num_eps, num_eps_ref[b])
            g = all_ref[b, G]
            gs_eps = jnp.sum(g * values, axis=1, keepdims=True)
            gs_eps_ref[b] = jnp.where(mask, gs_eps, gs_eps_ref[b])
            g = g.astype(BF16)
            gs = dot(g, state[0], NT) + dot(g, state[1], NT)
            gs_ref[b] = jnp.where(mask, gs, gs_ref[b])
        return carry

    lax.fori_loop(low, high + 1, one, 0)


def query_kernel(
    lens, place, all_ref, f_ref, z_ref, full_ref, qr_ref, num_ref, gs_ref, num_eps_ref, gs_eps_ref,
    res_hbm, send_hbm, b_ref, share_ref,
    bt_rows, inv_ref, tr_ref, t_ref, bt_ref, res_ref, send_ref, res_sem, send_sem,
):
    blocks, _, rows, _ = all_ref.shape
    chains = Chains(lens, place[0], blocks, rows)
    parts = split(f_ref[...])
    peak = jnp.max(jnp.max(z_ref[...], axis=0), axis=0, keepdims=True)
    share = RATIO * jnp.exp(full_ref[0, PEAK : PEAK + 1, :] - peak)
    share_ref[...] = jnp.broadcast_to(share, share_ref.shape)
    for c in range(CHAINS):
        count = lens[0, c].astype(F32)
        t_ref[c : c + 1, :] = share * full_ref[c, TOTALS : TOTALS + 1, :] + EPS * RATIO * count
    b_ref[...] = jnp.zeros_like(b_ref)
    low, high = chains.ends_of(chains.me)

    def one(c, carry):
        weights = t_ref[pl.ds(c, 1), :]
        back = jnp.zeros((M, D), F32)
        for b in range(blocks):
            mask = chains.mask(c, b)
            qf = qr_ref[b] + EPS * RATIO
            inv = 1.0 / jnp.sum(qf * weights, axis=1, keepdims=True)
            inv_ref[b] = jnp.where(mask, inv, inv_ref[b])
            tr_ref[b] = jnp.where(mask, weights, tr_ref[b])
            hi, lo = split(jnp.where(mask, qf * inv, 0.0))
            g = all_ref[b, G].astype(BF16)
            back = back + (dot(hi, g, TN) + dot(lo, g, TN))
        b_ref[c] = back
        return carry

    lax.fori_loop(low, high + 1, one, 0)
    feats = parts
    stores = [pltpu.make_async_copy(res_ref.at[b], res_hbm.at[b], res_sem.at[b]) for b in range(blocks)]
    for b in range(blocks):
        inv = inv_ref[b]
        exact = (share * num_ref[b] + num_eps_ref[b]) * inv
        res_ref[b, OUT] = exact
        grad_denom = -jnp.sum(all_ref[b, G] * exact, axis=1, keepdims=True) * inv
        raised = qr_ref[b]
        bt_rows[b] = (raised + EPS * RATIO) * grad_denom
        gs = share * gs_ref[b] + gs_eps_ref[b]
        grad_logits = (gs * inv + grad_denom * tr_ref[b]) * raised
        back = dot3(split(grad_logits), feats, NN)
        back = back - jnp.sum(grad_logits, axis=1, keepdims=True) * (SCALE * all_ref[b, Q])
        res_ref[b, GQ] = back * SCALE
        stores[b].start()
    bt_ref[...] = jnp.zeros_like(bt_ref)

    def two(c, carry):
        total = jnp.zeros((rows, M), F32)
        for b in range(blocks):
            total = total + jnp.where(chains.mask(c, b), bt_rows[b], 0.0)
        bt_ref[pl.ds(c, 1), :] = jnp.sum(total, axis=0, keepdims=True)
        return carry

    lax.fori_loop(low, high + 1, two, 0)
    send_ref[0:M, :] = b_ref[low]
    send_ref[M : 2 * M, :] = b_ref[high] * (high != low).astype(F32)
    send_ref[2 * M :, :] = bt_ref[...]
    store = pltpu.make_async_copy(send_ref, send_hbm, send_sem)
    store.start()
    for one_store in stores:
        one_store.wait()
    store.wait()


def key_kernel(
    lens, place, all_ref, f_ref, er_ref, share_ref, b_ref, sent_ref,
    res_hbm, kr_ref, full_ref, sum_ref, dk_ref, res_ref, res_sem,
):
    blocks, _, rows, _ = all_ref.shape
    chains = Chains(lens, place[0], blocks, rows)
    share = share_ref[0:1, :]
    for b in range(blocks):
        kr_ref[b] = er_ref[b] * share
    full_ref[...] = b_ref[...]
    for r in range(sent_ref.shape[0]):
        low, high = chains.ends_of(r)

        @pl.when(chains.me != r)
        def _():
            full_ref[low] += sent_ref[r, :M, :]
            full_ref[high] += sent_ref[r, M : 2 * M, :]

    sum_ref[...] = jnp.sum(sent_ref[:, 2 * M :, :], axis=0)
    low, high = chains.ends_of(chains.me)

    def one(c, carry):
        back = split(full_ref[c])
        total = sum_ref[pl.ds(c, 1), :]
        for b in range(blocks):
            mask = chains.mask(c, b)
            dv = dot3(split(kr_ref[b] + EPS * RATIO), back, NN)
            res_ref[b, GV] = jnp.where(mask, dv, res_ref[b, GV])
            v = all_ref[b, V].astype(BF16)
            dk = dot(v, back[0], NT) + dot(v, back[1], NT) + total
            dk_ref[b] = jnp.where(mask, dk, dk_ref[b])
        return carry

    lax.fori_loop(low, high + 1, one, 0)
    feats = split(f_ref[...])
    stores = [pltpu.make_async_copy(res_ref.at[b], res_hbm.at[b], res_sem.at[b]) for b in range(blocks)]
    for b in range(blocks):
        grad_logits = dk_ref[b] * kr_ref[b]
        back = dot3(split(grad_logits), feats, NN)
        back = back - jnp.sum(grad_logits, axis=1, keepdims=True) * (SCALE * all_ref[b, K])
        res_ref[b, GK] = back * SCALE
        stores[b].start()
    for store in stores:
        store.wait()


def unpack_kernel(res_ref, *outs):
    for h in range(H):
        for i, out in enumerate(outs):
            out[:, head(h)] = res_ref[h, i].astype(BF16)


def is_hbm(shape):
    return getattr(shape, "memory_space", None) is pltpu.HBM


def call(kernel, shapes, args, scalars=0, scratch=(), anys=0):
    vmem = pl.BlockSpec(memory_space=pltpu.VMEM)
    smem = pl.BlockSpec(memory_space=pltpu.SMEM)
    hbm = pl.BlockSpec(memory_space=pltpu.HBM)
    return pl.pallas_call(
        kernel,
        out_shape=shapes,
        in_specs=[pl.BlockSpec(memory_space=pl.ANY)] * anys
        + [smem] * scalars
        + [vmem] * (len(args) - anys - scalars),
        out_specs=[hbm if is_hbm(a) else vmem for a in shapes],
        scratch_shapes=list(scratch),
        compiler_params=pltpu.CompilerParams(vmem_limit_bytes=40 * 2**20),
    )(*args)


def f32(*shape):
    return jax.ShapeDtypeStruct(shape, F32)


def on_device(queries, keys, values, grad_attended, features, chain_lengths):
    rows, width = queries.shape[1:]
    q, k, v, g = (a.reshape(rows, width) for a in (queries, keys, values, grad_attended))
    place = jnp.stack([lax.axis_index("row"), lax.axis_index("col")]).astype(jnp.int32)
    where = (chain_lengths, place)
    groups, lines, blocks = (lax.axis_size(a) for a in ("grp", "row", "col"))
    wide = (blocks, rows, D)
    hbm = pl.BlockSpec(memory_space=pltpu.HBM)
    dma = pltpu.SemaphoreType.DMA
    pair = (blocks, 2, rows, D)

    def exchanged(*two):
        packed = pl.pallas_call(
            pack_kernel,
            out_shape=pltpu.HBM((H, 2, rows, D), F32),
            in_specs=[hbm] * 2,
            out_specs=hbm,
            scratch_shapes=[
                pltpu.VMEM((2, rows, width), BF16), pltpu.VMEM((H, 2, rows, D), F32), dma((2,)), dma((H,)),
            ],
            compiler_params=pltpu.CompilerParams(vmem_limit_bytes=60 * 2**20),
        )(*two)
        return lax.all_to_all(packed, "col", 0, 0, tiled=True)

    key_rows, query_rows = exchanged(k, v), exchanged(q, g)
    states = (CHAINS, M + 8, D)
    own_states, ends = call(
        state_kernel,
        [pltpu.VMEM(states, F32), pltpu.HBM((2, M + 8, D), F32)],
        (*where, key_rows, features),
        2,
        [pltpu.VMEM(wide, F32), pltpu.VMEM((2, M + 8, D), F32), dma],
    )
    ends = lax.all_gather(ends, "row")
    peers = (groups, 8, M)
    peaks = pl.pallas_call(
        peak_kernel,
        out_shape=pltpu.HBM(peers, F32),
        in_specs=[pl.BlockSpec(memory_space=pl.ANY)] * 2,
        out_specs=hbm,
        scratch_shapes=[pltpu.VMEM((lines, 8, D), F32), pltpu.VMEM(peers, F32), dma((2,))],
    )(ends, query_rows)
    peaks = lax.all_to_all(peaks, "grp", 0, 0, tiled=True)
    held = pltpu.VMEM(wide, F32)
    full_states, *query_parts, key_raised = call(
        ahead_kernel,
        [pltpu.VMEM(states, F32)] + [held] * 6,
        (ends, *where, key_rows, query_rows, features, own_states),
        2,
        [pltpu.VMEM((lines, 2, M + 8, D), F32), dma],
        anys=1,
    )
    back = (2 * M + 2 * CHAINS, D)
    small = (2 * CHAINS, M)
    first, back_ends, backs, share = call(
        query_kernel,
        [pltpu.HBM(pair, F32), pltpu.HBM(back, F32), pltpu.VMEM((CHAINS, M, D), F32), f32(*small)],
        (*where, query_rows, features, peaks, full_states, *query_parts),
        2,
        [pltpu.VMEM(wide, F32)] * 3
        + [pltpu.VMEM(small, F32)] * 2
        + [pltpu.VMEM(pair, F32), pltpu.VMEM(back, F32), dma((blocks,)), dma],
    )
    first = lax.all_to_all(first, "col", 0, 0, tiled=True)
    back_ends = lax.all_gather(back_ends, "row")
    (second,) = call(
        key_kernel,
        [pltpu.HBM(pair, F32)],
        (*where, key_rows, features, key_raised, share, backs, back_ends),
        2,
        [pltpu.VMEM(wide, F32), pltpu.VMEM((CHAINS, M, D), F32), pltpu.VMEM(small, F32)]
        + [pltpu.VMEM(wide, F32), pltpu.VMEM(pair, F32), dma((blocks,))],
    )
    second = lax.all_to_all(second, "col", 0, 0, tiled=True)
    narrow = [jax.ShapeDtypeStruct((rows, width), BF16)] * 2
    outs = (*call(unpack_kernel, narrow, (first,)), *call(unpack_kernel, narrow, (second,)))
    return tuple(a.reshape(1, rows, width) for a in outs)


def solution(mesh):
    groups, seq = mesh.devices.shape
    fine = Mesh(mesh.devices.reshape(groups, seq // H, H), ("grp", "row", "col"))
    rows = P("grp", ("row", "col"), None)
    return jax.shard_map(
        on_device,
        mesh=fine,
        in_specs=(rows, rows, rows, rows, P(), P("grp", None)),
        out_specs=(rows, rows, rows, rows),
        check_vma=False,
    )
```

```python
import jax
import jax.numpy as jnp
from jax import lax
from jax.experimental import pallas as pl
from jax.experimental.pallas import tpu as pltpu
from jax.sharding import Mesh
from jax.sharding import PartitionSpec as P

H = 8
D = 128
M = 128
CHAINS = 4
EPS = 1e-06
SCALE = D ** (-0.25)
RATIO = M ** (-0.5)
F32 = jnp.float32
BF16 = jnp.bfloat16
NN = (((1,), (0,)), ((), ()))
NT = (((1,), (1,)), ((), ()))
TN = (((0,), (0,)), ((), ()))
K, V = range(2)
Q, G = range(2)
OUT, GQ = range(2)
GK, GV = range(2)
VALUES, TOTALS, PEAK = M, M + 1, M + 2


def dot(a, b, dims):
    return lax.dot_general(a, b, dims, preferred_element_type=F32)


def split(x):
    hi = x.astype(BF16)
    return hi, (x - hi.astype(F32)).astype(BF16)


def split3(x):
    hi = x.astype(BF16)
    rest = x - hi.astype(F32)
    mid = rest.astype(BF16)
    return hi, mid, (rest - mid.astype(F32)).astype(BF16)


def dot3(a, b, dims):
    (ah, al), (bh, bl) = a, b
    return dot(ah, bh, dims) + (dot(ah, bl, dims) + dot(al, bh, dims))


def head(h):
    return slice(h * D, (h + 1) * D)


def logits_of(x, parts):
    f1, f2, f3 = parts
    y = x.astype(BF16)
    z = dot(y, f1, NT) + (dot(y, f2, NT) + dot(y, f3, NT))
    return SCALE * z - (0.5 * SCALE * SCALE) * jnp.sum(x * x, axis=1, keepdims=True)


class Chains:
    def __init__(self, lens, me, blocks, rows):
        self.rows = rows
        self.span = blocks * rows
        self.me = me
        l0, l1, l2 = lens[0, 0], lens[0, 1], lens[0, 2]
        self.starts = (jnp.int32(0), l0, l0 + l1, l0 + l1 + l2)
        self.lens = lens

    def count_ended(self, position):
        c = jnp.int32(0)
        for s in self.starts[1:]:
            c = c + (position >= s).astype(jnp.int32)
        return c

    def ends_of(self, which):
        return self.count_ended(which * self.span), self.count_ended((which + 1) * self.span - 1)

    def start_of(self, c):
        s = self.starts
        return jnp.where(c == 0, s[0], jnp.where(c == 1, s[1], jnp.where(c == 2, s[2], s[3])))

    def mask(self, c, block):
        low = self.start_of(c) - (self.me * self.span + block * self.rows)
        at = lax.broadcasted_iota(jnp.int32, (self.rows, D), 0)
        return (at >= low) & (at < low + self.lens[0, c])


def pack_kernel(first_hbm, second_hbm, out_hbm, rows_ref, wide_ref, in_sem, out_sem):
    sources = (first_hbm, second_hbm)
    loads = [pltpu.make_async_copy(r, rows_ref.at[i], in_sem.at[i]) for i, r in enumerate(sources)]
    for load in loads:
        load.start()
    for load in loads:
        load.wait()
    stores = [pltpu.make_async_copy(wide_ref.at[h], out_hbm.at[h], out_sem.at[h]) for h in range(H)]
    for h in range(H):
        for i in range(2):
            wide_ref[h, i] = rows_ref[i, :, head(h)].astype(F32)
        stores[h].start()
    for store in stores:
        store.wait()


def state_kernel(lens, place, all_ref, f_ref, s_ref, send_hbm, er_ref, send_ref, sem):
    blocks, _, rows, _ = all_ref.shape
    chains = Chains(lens, place[0], blocks, rows)
    parts = split3(f_ref[...])
    peak = jnp.full((1, 1), -jnp.inf, F32)
    for b in range(blocks):
        logits = logits_of(all_ref[b, K], parts)
        er_ref[b] = logits
        peak = jnp.maximum(peak, jnp.max(logits, axis=(0, 1), keepdims=True))
    for b in range(blocks):
        er_ref[b] = jnp.exp(er_ref[b] - peak)
    s_ref[...] = jnp.zeros_like(s_ref)
    for c in range(CHAINS):
        s_ref[c, PEAK : PEAK + 1, :] = jnp.broadcast_to(peak, (1, D))
    low, high = chains.ends_of(chains.me)

    def one(c, carry):
        state = jnp.zeros((M, D), F32)
        values = jnp.zeros((rows, D), F32)
        totals = jnp.zeros((rows, M), F32)
        for b in range(blocks):
            mask = chains.mask(c, b)
            raised = jnp.where(mask, er_ref[b], 0.0)
            totals = totals + raised
            hi, lo = split(raised)
            v = all_ref[b, V]
            values = values + jnp.where(mask, v, 0.0)
            v = v.astype(BF16)
            state = state + (dot(hi, v, TN) + dot(lo, v, TN))
        s_ref[c, :M, :] = state
        s_ref[c, VALUES : VALUES + 1, :] = jnp.sum(values, axis=0, keepdims=True)
        s_ref[c, TOTALS : TOTALS + 1, :] = jnp.sum(totals, axis=0, keepdims=True)
        return carry

    lax.fori_loop(low, high + 1, one, 0)
    send_ref[0] = s_ref[low]
    send_ref[1] = s_ref[high] * (high != low).astype(F32)
    store = pltpu.make_async_copy(send_ref, send_hbm, sem)
    store.start()
    store.wait()


def peak_kernel(sent_hbm, wait_ref, z_hbm, tile_ref, z_ref, sems):
    load = pltpu.make_async_copy(sent_hbm.at[:, 0, pl.ds(M, 8), :], tile_ref, sems.at[0])
    load.start()
    load.wait()
    peak = jnp.max(tile_ref[:, PEAK - M : PEAK - M + 1, :], axis=0)
    for i in range(z_ref.shape[0]):
        z_ref[i] = jnp.broadcast_to(peak, z_ref.shape[1:])
    store = pltpu.make_async_copy(z_ref, z_hbm, sems.at[1])
    store.start()
    store.wait()


def raised_kernel(key_ref, f_ref, s_ref, er_ref):
    parts = split3(f_ref[...])
    peak = s_ref[0, PEAK : PEAK + 1, :]
    for b in range(key_ref.shape[0]):
        er_ref[b] = jnp.exp(logits_of(key_ref[b, K], parts) - peak)


def query_kernel(
    lens, place, all_ref, f_ref, z_ref, s_ref, sent_ref,
    res_hbm, send_hbm, b_ref, share_ref,
    qr_ref, full_ref, num_ref, gs_ref, inv_ref, tr_ref, t_ref, bt_ref, res_ref, send_ref, res_sem, send_sem,
):
    blocks, _, rows, _ = all_ref.shape
    chains = Chains(lens, place[0], blocks, rows)
    parts = split3(f_ref[...])
    for b in range(blocks):
        ql = logits_of(all_ref[b, Q], parts)
        qr_ref[b] = jnp.exp(ql - jnp.max(ql, axis=1, keepdims=True)) * RATIO
    peak = jnp.max(jnp.max(z_ref[...], axis=0), axis=0, keepdims=True)
    own_share = RATIO * jnp.exp(s_ref[0, PEAK : PEAK + 1, :] - peak)
    share_ref[...] = jnp.broadcast_to(own_share, share_ref.shape)
    row = lax.broadcasted_iota(jnp.int32, (M + 8, D), 0)
    share = jnp.where(row == VALUES, 1.0, jnp.exp(s_ref[0, PEAK : PEAK + 1, :] - peak))
    for c in range(CHAINS):
        full_ref[c] = s_ref[c] * share
    for r in range(sent_ref.shape[0]):
        ends = chains.ends_of(r)

        @pl.when(chains.me != r)
        def _():
            share = jnp.where(row == VALUES, 1.0, jnp.exp(sent_ref[r, 0, PEAK : PEAK + 1, :] - peak))
            for i, c in enumerate(ends):
                full_ref[c] += sent_ref[r, i] * share

    for c in range(CHAINS):
        count = lens[0, c].astype(F32)
        t_ref[c : c + 1, :] = RATIO * (full_ref[c, TOTALS : TOTALS + 1, :] + EPS * count)
    b_ref[...] = jnp.zeros_like(b_ref)
    low, high = chains.ends_of(chains.me)

    def one(c, carry):
        state = RATIO * (full_ref[c, :M, :] + EPS * full_ref[c, VALUES : VALUES + 1, :])
        state = split(state)
        weights = t_ref[pl.ds(c, 1), :]
        back = jnp.zeros((M, D), F32)
        for b in range(blocks):
            mask = chains.mask(c, b)
            qf = qr_ref[b] + EPS * RATIO
            inv = 1.0 / jnp.sum(qf * weights, axis=1, keepdims=True)
            inv_ref[b] = jnp.where(mask, inv, inv_ref[b])
            tr_ref[b] = jnp.where(mask, weights, tr_ref[b])
            num = dot3(split(qf), state, NN)
            num_ref[b] = jnp.where(mask, num, num_ref[b])
            g = all_ref[b, G].astype(BF16)
            gs = dot(g, state[0], NT) + dot(g, state[1], NT)
            gs_ref[b] = jnp.where(mask, gs, gs_ref[b])
            hi, lo = split(jnp.where(mask, qf * inv, 0.0))
            back = back + (dot(hi, g, TN) + dot(lo, g, TN))
        b_ref[c] = back
        return carry

    lax.fori_loop(low, high + 1, one, 0)
    feats = parts[:2]
    stores = [pltpu.make_async_copy(res_ref.at[b], res_hbm.at[b], res_sem.at[b]) for b in range(blocks)]
    for b in range(blocks):
        inv = inv_ref[b]
        exact = num_ref[b] * inv
        res_ref[b, OUT] = exact
        grad_denom = -jnp.sum(all_ref[b, G] * exact, axis=1, keepdims=True) * inv
        raised = qr_ref[b]
        num_ref[b] = (raised + EPS * RATIO) * grad_denom
        grad_logits = (gs_ref[b] * inv + grad_denom * tr_ref[b]) * raised
        back = dot3(split(grad_logits), feats, NN)
        back = back - jnp.sum(grad_logits, axis=1, keepdims=True) * (SCALE * all_ref[b, Q])
        res_ref[b, GQ] = back * SCALE
        stores[b].start()
    bt_ref[...] = jnp.zeros_like(bt_ref)

    def two(c, carry):
        total = jnp.zeros((rows, M), F32)
        for b in range(blocks):
            total = total + jnp.where(chains.mask(c, b), num_ref[b], 0.0)
        bt_ref[pl.ds(c, 1), :] = jnp.sum(total, axis=0, keepdims=True)
        return carry

    lax.fori_loop(low, high + 1, two, 0)
    send_ref[0:M, :] = b_ref[low]
    send_ref[M : 2 * M, :] = b_ref[high] * (high != low).astype(F32)
    send_ref[2 * M :, :] = bt_ref[...]
    store = pltpu.make_async_copy(send_ref, send_hbm, send_sem)
    store.start()
    for one_store in stores:
        one_store.wait()
    store.wait()


def key_kernel(
    lens, place, all_ref, f_ref, er_ref, share_ref, b_ref, sent_ref,
    res_hbm, kr_ref, full_ref, sum_ref, dk_ref, res_ref, res_sem,
):
    blocks, _, rows, _ = all_ref.shape
    chains = Chains(lens, place[0], blocks, rows)
    share = share_ref[0:1, :]
    for b in range(blocks):
        kr_ref[b] = er_ref[b] * share
    full_ref[...] = b_ref[...]
    for r in range(sent_ref.shape[0]):
        low, high = chains.ends_of(r)

        @pl.when(chains.me != r)
        def _():
            full_ref[low] += sent_ref[r, :M, :]
            full_ref[high] += sent_ref[r, M : 2 * M, :]

    sum_ref[...] = jnp.sum(sent_ref[:, 2 * M :, :], axis=0)
    low, high = chains.ends_of(chains.me)

    def one(c, carry):
        back = split(full_ref[c])
        total = sum_ref[pl.ds(c, 1), :]
        for b in range(blocks):
            mask = chains.mask(c, b)
            dv = dot3(split(kr_ref[b] + EPS * RATIO), back, NN)
            res_ref[b, GV] = jnp.where(mask, dv, res_ref[b, GV])
            v = all_ref[b, V].astype(BF16)
            dk = dot(v, back[0], NT) + dot(v, back[1], NT) + total
            dk_ref[b] = jnp.where(mask, dk, dk_ref[b])
        return carry

    lax.fori_loop(low, high + 1, one, 0)
    feats = split(f_ref[...])
    stores = [pltpu.make_async_copy(res_ref.at[b], res_hbm.at[b], res_sem.at[b]) for b in range(blocks)]
    for b in range(blocks):
        grad_logits = dk_ref[b] * kr_ref[b]
        back = dot3(split(grad_logits), feats, NN)
        back = back - jnp.sum(grad_logits, axis=1, keepdims=True) * (SCALE * all_ref[b, K])
        res_ref[b, GK] = back * SCALE
        stores[b].start()
    for store in stores:
        store.wait()


def unpack_kernel(res_ref, *outs):
    for h in range(H):
        for i, out in enumerate(outs):
            out[:, head(h)] = res_ref[h, i].astype(BF16)


def is_hbm(shape):
    return getattr(shape, "memory_space", None) is pltpu.HBM


def call(kernel, shapes, args, scalars=0, scratch=()):
    vmem = pl.BlockSpec(memory_space=pltpu.VMEM)
    smem = pl.BlockSpec(memory_space=pltpu.SMEM)
    hbm = pl.BlockSpec(memory_space=pltpu.HBM)
    return pl.pallas_call(
        kernel,
        out_shape=shapes,
        in_specs=[smem] * scalars + [vmem] * (len(args) - scalars),
        out_specs=[hbm if is_hbm(a) else vmem for a in shapes],
        scratch_shapes=list(scratch),
        compiler_params=pltpu.CompilerParams(vmem_limit_bytes=40 * 2**20),
    )(*args)


def f32(*shape):
    return jax.ShapeDtypeStruct(shape, F32)


def on_device(queries, keys, values, grad_attended, features, chain_lengths):
    rows, width = queries.shape[1:]
    q, k, v, g = (a.reshape(rows, width) for a in (queries, keys, values, grad_attended))
    place = jnp.stack([lax.axis_index("row"), lax.axis_index("col")]).astype(jnp.int32)
    where = (chain_lengths, place)
    groups, lines, blocks = (lax.axis_size(a) for a in ("grp", "row", "col"))
    wide = (blocks, rows, D)
    hbm = pl.BlockSpec(memory_space=pltpu.HBM)
    dma = pltpu.SemaphoreType.DMA
    pair = (blocks, 2, rows, D)

    def exchanged(*two):
        packed = pl.pallas_call(
            pack_kernel,
            out_shape=pltpu.HBM((H, 2, rows, D), F32),
            in_specs=[hbm] * 2,
            out_specs=hbm,
            scratch_shapes=[
                pltpu.VMEM((2, rows, width), BF16), pltpu.VMEM((H, 2, rows, D), F32), dma((2,)), dma((H,)),
            ],
            compiler_params=pltpu.CompilerParams(vmem_limit_bytes=60 * 2**20),
        )(*two)
        return lax.all_to_all(packed, "col", 0, 0, tiled=True)

    key_rows, query_rows = exchanged(k, v), exchanged(q, g)
    states = (CHAINS, M + 8, D)
    own_states, ends = call(
        state_kernel,
        [pltpu.VMEM(states, F32), pltpu.HBM((2, M + 8, D), F32)],
        (*where, key_rows, features),
        2,
        [pltpu.VMEM(wide, F32), pltpu.VMEM((2, M + 8, D), F32), dma],
    )
    ends = lax.all_gather(ends, "row")
    peers = (groups, 8, M)
    peaks = pl.pallas_call(
        peak_kernel,
        out_shape=pltpu.HBM(peers, F32),
        in_specs=[pl.BlockSpec(memory_space=pl.ANY)] * 2,
        out_specs=hbm,
        scratch_shapes=[pltpu.VMEM((lines, 8, D), F32), pltpu.VMEM(peers, F32), dma((2,))],
    )(ends, query_rows)
    peaks = lax.all_to_all(peaks, "grp", 0, 0, tiled=True)
    (key_raised,) = call(raised_kernel, [f32(*wide)], (key_rows, features, own_states))
    back = (2 * M + 2 * CHAINS, D)
    small = (2 * CHAINS, M)
    first, back_ends, backs, share = call(
        query_kernel,
        [pltpu.HBM(pair, F32), pltpu.HBM(back, F32), pltpu.VMEM((CHAINS, M, D), F32), f32(*small)],
        (*where, query_rows, features, peaks, own_states, ends),
        2,
        [pltpu.VMEM(wide, F32), pltpu.VMEM(states, F32)]
        + [pltpu.VMEM(wide, F32)] * 4
        + [pltpu.VMEM(small, F32)] * 2
        + [pltpu.VMEM(pair, F32), pltpu.VMEM(back, F32), dma((blocks,)), dma],
    )
    first = lax.all_to_all(first, "col", 0, 0, tiled=True)
    back_ends = lax.all_gather(back_ends, "row")
    (second,) = call(
        key_kernel,
        [pltpu.HBM(pair, F32)],
        (*where, key_rows, features, key_raised, share, backs, back_ends),
        2,
        [pltpu.VMEM(wide, F32), pltpu.VMEM((CHAINS, M, D), F32), pltpu.VMEM(small, F32)]
        + [pltpu.VMEM(wide, F32), pltpu.VMEM(pair, F32), dma((blocks,))],
    )
    second = lax.all_to_all(second, "col", 0, 0, tiled=True)
    narrow = [jax.ShapeDtypeStruct((rows, width), BF16)] * 2
    outs = (*call(unpack_kernel, narrow, (first,)), *call(unpack_kernel, narrow, (second,)))
    return tuple(a.reshape(1, rows, width) for a in outs)


def solution(mesh):
    groups, seq = mesh.devices.shape
    fine = Mesh(mesh.devices.reshape(groups, seq // H, H), ("grp", "row", "col"))
    rows = P("grp", ("row", "col"), None)
    return jax.shard_map(
        on_device,
        mesh=fine,
        in_specs=(rows, rows, rows, rows, P(), P("grp", None)),
        out_specs=(rows, rows, rows, rows),
        check_vma=False,
    )
```

```python
import jax
import jax.numpy as jnp
from jax import lax
from jax.experimental import pallas as pl
from jax.experimental.pallas import tpu as pltpu
from jax.sharding import Mesh
from jax.sharding import PartitionSpec as P

H = 8
D = 128
M = 128
CHAINS = 4
EPS = 1e-06
SCALE = D ** (-0.25)
RATIO = M ** (-0.5)
F32 = jnp.float32
BF16 = jnp.bfloat16
NN = (((1,), (0,)), ((), ()))
NT = (((1,), (1,)), ((), ()))
TN = (((0,), (0,)), ((), ()))
K, V, Q, G = range(4)
OUT, GQ = range(2)
GK, GV = range(2)
VALUES, TOTALS, PEAK = M, M + 1, M + 2


def dot(a, b, dims):
    return lax.dot_general(a, b, dims, preferred_element_type=F32)


def split(x):
    hi = x.astype(BF16)
    return hi, (x - hi.astype(F32)).astype(BF16)


def split3(x):
    hi = x.astype(BF16)
    rest = x - hi.astype(F32)
    mid = rest.astype(BF16)
    return hi, mid, (rest - mid.astype(F32)).astype(BF16)


def dot3(a, b, dims):
    (ah, al), (bh, bl) = a, b
    return dot(ah, bh, dims) + (dot(ah, bl, dims) + dot(al, bh, dims))


def head(h):
    return slice(h * D, (h + 1) * D)


def logits_of(x, parts):
    f1, f2, f3 = parts
    y = x.astype(BF16)
    z = dot(y, f1, NT) + (dot(y, f2, NT) + dot(y, f3, NT))
    return SCALE * z - (0.5 * SCALE * SCALE) * jnp.sum(x * x, axis=1, keepdims=True)


class Chains:
    def __init__(self, lens, me, blocks, rows):
        self.rows = rows
        self.span = blocks * rows
        self.me = me
        l0, l1, l2 = lens[0, 0], lens[0, 1], lens[0, 2]
        self.starts = (jnp.int32(0), l0, l0 + l1, l0 + l1 + l2)
        self.lens = lens

    def count_ended(self, position):
        c = jnp.int32(0)
        for s in self.starts[1:]:
            c = c + (position >= s).astype(jnp.int32)
        return c

    def ends_of(self, which):
        return self.count_ended(which * self.span), self.count_ended((which + 1) * self.span - 1)

    def start_of(self, c):
        s = self.starts
        return jnp.where(c == 0, s[0], jnp.where(c == 1, s[1], jnp.where(c == 2, s[2], s[3])))

    def mask(self, c, block):
        low = self.start_of(c) - (self.me * self.span + block * self.rows)
        at = lax.broadcasted_iota(jnp.int32, (self.rows, D), 0)
        return (at >= low) & (at < low + self.lens[0, c])


def pack_kernel(k_hbm, v_hbm, q_hbm, g_hbm, out_hbm, rows_ref, wide_ref, in_sem, out_sem):
    sources = (k_hbm, v_hbm, q_hbm, g_hbm)
    loads = [pltpu.make_async_copy(r, rows_ref.at[i], in_sem.at[i]) for i, r in enumerate(sources)]
    for load in loads:
        load.start()
    for load in loads:
        load.wait()
    stores = [pltpu.make_async_copy(wide_ref.at[h], out_hbm.at[h], out_sem.at[h]) for h in range(H)]
    for h in range(H):
        for i in range(4):
            wide_ref[h, i] = rows_ref[i, :, head(h)].astype(F32)
        stores[h].start()
    for store in stores:
        store.wait()


def state_kernel(
    lens, place, all_ref, f_ref, z_hbm, s_ref, send_hbm, er_ref, send_ref, z_ref, sem, z_sem
):
    blocks, _, rows, _ = all_ref.shape
    chains = Chains(lens, place[0], blocks, rows)
    parts = split3(f_ref[...])
    peak = jnp.full((1, 1), -jnp.inf, F32)
    for b in range(blocks):
        logits = logits_of(all_ref[b, K], parts)
        er_ref[b] = logits
        peak = jnp.maximum(peak, jnp.max(logits, axis=(0, 1), keepdims=True))
    for b in range(blocks):
        er_ref[b] = jnp.exp(er_ref[b] - peak)
    for i in range(z_ref.shape[0]):
        z_ref[i] = jnp.broadcast_to(peak, z_ref.shape[1:])
    z_store = pltpu.make_async_copy(z_ref, z_hbm, z_sem)
    z_store.start()
    s_ref[...] = jnp.zeros_like(s_ref)
    for c in range(CHAINS):
        s_ref[c, PEAK : PEAK + 1, :] = jnp.broadcast_to(peak, (1, D))
    low, high = chains.ends_of(chains.me)

    def one(c, carry):
        state = jnp.zeros((M, D), F32)
        values = jnp.zeros((rows, D), F32)
        totals = jnp.zeros((rows, M), F32)
        for b in range(blocks):
            mask = chains.mask(c, b)
            raised = jnp.where(mask, er_ref[b], 0.0)
            totals = totals + raised
            hi, lo = split(raised)
            v = all_ref[b, V]
            values = values + jnp.where(mask, v, 0.0)
            v = v.astype(BF16)
            state = state + (dot(hi, v, TN) + dot(lo, v, TN))
        s_ref[c, :M, :] = state
        s_ref[c, VALUES : VALUES + 1, :] = jnp.sum(values, axis=0, keepdims=True)
        s_ref[c, TOTALS : TOTALS + 1, :] = jnp.sum(totals, axis=0, keepdims=True)
        return carry

    lax.fori_loop(low, high + 1, one, 0)
    send_ref[0] = s_ref[low]
    send_ref[1] = s_ref[high] * (high != low).astype(F32)
    store = pltpu.make_async_copy(send_ref, send_hbm, sem)
    store.start()
    z_store.wait()
    store.wait()


def query_kernel(
    lens, place, all_ref, f_ref, z_ref, s_ref, sent_ref,
    res_hbm, send_hbm, b_ref, peak_ref,
    qr_ref, full_ref, num_ref, gs_ref, inv_ref, tr_ref, t_ref, bt_ref, res_ref, send_ref, res_sem, send_sem,
):
    blocks, _, rows, _ = all_ref.shape
    chains = Chains(lens, place[0], blocks, rows)
    parts = split3(f_ref[...])
    for b in range(blocks):
        ql = logits_of(all_ref[b, Q], parts)
        qr_ref[b] = jnp.exp(ql - jnp.max(ql, axis=1, keepdims=True)) * RATIO
    peak = jnp.max(jnp.max(z_ref[...], axis=0), axis=0, keepdims=True)
    peak_ref[...] = jnp.broadcast_to(peak, peak_ref.shape)
    row = lax.broadcasted_iota(jnp.int32, (M + 8, D), 0)
    share = jnp.where(row == VALUES, 1.0, jnp.exp(s_ref[0, PEAK : PEAK + 1, :] - peak))
    for c in range(CHAINS):
        full_ref[c] = s_ref[c] * share
    for r in range(sent_ref.shape[0]):
        ends = chains.ends_of(r)

        @pl.when(chains.me != r)
        def _():
            share = jnp.where(row == VALUES, 1.0, jnp.exp(sent_ref[r, 0, PEAK : PEAK + 1, :] - peak))
            for i, c in enumerate(ends):
                full_ref[c] += sent_ref[r, i] * share

    for c in range(CHAINS):
        count = lens[0, c].astype(F32)
        t_ref[c : c + 1, :] = RATIO * (full_ref[c, TOTALS : TOTALS + 1, :] + EPS * count)
    b_ref[...] = jnp.zeros_like(b_ref)
    low, high = chains.ends_of(chains.me)

    def one(c, carry):
        state = RATIO * (full_ref[c, :M, :] + EPS * full_ref[c, VALUES : VALUES + 1, :])
        state = split(state)
        weights = t_ref[pl.ds(c, 1), :]
        back = jnp.zeros((M, D), F32)
        for b in range(blocks):
            mask = chains.mask(c, b)
            qf = qr_ref[b] + EPS * RATIO
            inv = 1.0 / jnp.sum(qf * weights, axis=1, keepdims=True)
            inv_ref[b] = jnp.where(mask, inv, inv_ref[b])
            tr_ref[b] = jnp.where(mask, weights, tr_ref[b])
            num = dot3(split(qf), state, NN)
            num_ref[b] = jnp.where(mask, num, num_ref[b])
            g = all_ref[b, G].astype(BF16)
            gs = dot(g, state[0], NT) + dot(g, state[1], NT)
            gs_ref[b] = jnp.where(mask, gs, gs_ref[b])
            hi, lo = split(jnp.where(mask, qf * inv, 0.0))
            back = back + (dot(hi, g, TN) + dot(lo, g, TN))
        b_ref[c] = back
        return carry

    lax.fori_loop(low, high + 1, one, 0)
    feats = parts[:2]
    stores = [pltpu.make_async_copy(res_ref.at[b], res_hbm.at[b], res_sem.at[b]) for b in range(blocks)]
    for b in range(blocks):
        inv = inv_ref[b]
        exact = num_ref[b] * inv
        res_ref[b, OUT] = exact
        grad_denom = -jnp.sum(all_ref[b, G] * exact, axis=1, keepdims=True) * inv
        raised = qr_ref[b]
        num_ref[b] = (raised + EPS * RATIO) * grad_denom
        grad_logits = (gs_ref[b] * inv + grad_denom * tr_ref[b]) * raised
        back = dot3(split(grad_logits), feats, NN)
        back = back - jnp.sum(grad_logits, axis=1, keepdims=True) * (SCALE * all_ref[b, Q])
        res_ref[b, GQ] = back * SCALE
        stores[b].start()
    bt_ref[...] = jnp.zeros_like(bt_ref)

    def two(c, carry):
        total = jnp.zeros((rows, M), F32)
        for b in range(blocks):
            total = total + jnp.where(chains.mask(c, b), num_ref[b], 0.0)
        bt_ref[pl.ds(c, 1), :] = jnp.sum(total, axis=0, keepdims=True)
        return carry

    lax.fori_loop(low, high + 1, two, 0)
    send_ref[0:M, :] = b_ref[low]
    send_ref[M : 2 * M, :] = b_ref[high] * (high != low).astype(F32)
    send_ref[2 * M :, :] = bt_ref[...]
    store = pltpu.make_async_copy(send_ref, send_hbm, send_sem)
    store.start()
    for one_store in stores:
        one_store.wait()
    store.wait()


def key_kernel(
    lens, place, all_ref, f_ref, peak_ref, b_ref, sent_ref,
    res_hbm, kr_ref, full_ref, sum_ref, dk_ref, res_ref, res_sem,
):
    blocks, _, rows, _ = all_ref.shape
    chains = Chains(lens, place[0], blocks, rows)
    parts = split3(f_ref[...])
    peak = peak_ref[0:1, :]
    for b in range(blocks):
        kr_ref[b] = jnp.exp(logits_of(all_ref[b, K], parts) - peak) * RATIO
    full_ref[...] = b_ref[...]
    for r in range(sent_ref.shape[0]):
        low, high = chains.ends_of(r)

        @pl.when(chains.me != r)
        def _():
            full_ref[low] += sent_ref[r, :M, :]
            full_ref[high] += sent_ref[r, M : 2 * M, :]

    sum_ref[...] = jnp.sum(sent_ref[:, 2 * M :, :], axis=0)
    low, high = chains.ends_of(chains.me)

    def one(c, carry):
        back = split(full_ref[c])
        total = sum_ref[pl.ds(c, 1), :]
        for b in range(blocks):
            mask = chains.mask(c, b)
            dv = dot3(split(kr_ref[b] + EPS * RATIO), back, NN)
            res_ref[b, GV] = jnp.where(mask, dv, res_ref[b, GV])
            v = all_ref[b, V].astype(BF16)
            dk = dot(v, back[0], NT) + dot(v, back[1], NT) + total
            dk_ref[b] = jnp.where(mask, dk, dk_ref[b])
        return carry

    lax.fori_loop(low, high + 1, one, 0)
    feats = parts[:2]
    stores = [pltpu.make_async_copy(res_ref.at[b], res_hbm.at[b], res_sem.at[b]) for b in range(blocks)]
    for b in range(blocks):
        grad_logits = dk_ref[b] * kr_ref[b]
        back = dot3(split(grad_logits), feats, NN)
        back = back - jnp.sum(grad_logits, axis=1, keepdims=True) * (SCALE * all_ref[b, K])
        res_ref[b, GK] = back * SCALE
        stores[b].start()
    for store in stores:
        store.wait()


def unpack_kernel(res_ref, *outs):
    for h in range(H):
        for i, out in enumerate(outs):
            out[:, head(h)] = res_ref[h, i].astype(BF16)


def is_hbm(shape):
    return getattr(shape, "memory_space", None) is pltpu.HBM


def call(kernel, shapes, args, scalars=0, scratch=()):
    vmem = pl.BlockSpec(memory_space=pltpu.VMEM)
    smem = pl.BlockSpec(memory_space=pltpu.SMEM)
    hbm = pl.BlockSpec(memory_space=pltpu.HBM)
    return pl.pallas_call(
        kernel,
        out_shape=shapes,
        in_specs=[smem] * scalars + [vmem] * (len(args) - scalars),
        out_specs=[hbm if is_hbm(a) else vmem for a in shapes],
        scratch_shapes=list(scratch),
        compiler_params=pltpu.CompilerParams(vmem_limit_bytes=40 * 2**20),
    )(*args)


def f32(*shape):
    return jax.ShapeDtypeStruct(shape, F32)


def on_device(queries, keys, values, grad_attended, features, chain_lengths):
    rows, width = queries.shape[1:]
    q, k, v, g = (a.reshape(rows, width) for a in (queries, keys, values, grad_attended))
    place = jnp.stack([lax.axis_index("row"), lax.axis_index("col")]).astype(jnp.int32)
    where = (chain_lengths, place)
    groups, lines, blocks = (lax.axis_size(a) for a in ("grp", "row", "col"))
    wide = (blocks, rows, D)
    hbm = pl.BlockSpec(memory_space=pltpu.HBM)
    packed = pl.pallas_call(
        pack_kernel,
        out_shape=f32(H, 4, rows, D),
        in_specs=[hbm] * 4,
        out_specs=hbm,
        scratch_shapes=[
            pltpu.VMEM((4, rows, width), BF16),
            pltpu.VMEM((H, 4, rows, D), F32),
            pltpu.SemaphoreType.DMA((4,)),
            pltpu.SemaphoreType.DMA((H,)),
        ],
        compiler_params=pltpu.CompilerParams(vmem_limit_bytes=60 * 2**20),
    )(k, v, q, g)
    own = lax.all_to_all(packed, "col", 0, 0, tiled=True)
    states = (CHAINS, M + 8, D)
    peers = (groups * lines, 1, M)
    dma = pltpu.SemaphoreType.DMA
    peaks, own_states, ends = call(
        state_kernel,
        [pltpu.HBM(peers, F32), f32(*states), pltpu.HBM((2, M + 8, D), F32)],
        (*where, own, features),
        2,
        [pltpu.VMEM(wide, F32), pltpu.VMEM((2, M + 8, D), F32), pltpu.VMEM(peers, F32), dma, dma],
    )
    peaks = lax.all_to_all(peaks, ("grp", "row"), 0, 0, tiled=True)
    ends = lax.all_gather(ends, "row")
    pair = (blocks, 2, rows, D)
    back = (2 * M + 2 * CHAINS, D)
    small = (2 * CHAINS, M)
    first, back_ends, backs, peak = call(
        query_kernel,
        [pltpu.HBM(pair, F32), pltpu.HBM(back, F32), f32(CHAINS, M, D), f32(*small)],
        (*where, own, features, peaks, own_states, ends),
        2,
        [pltpu.VMEM(wide, F32), pltpu.VMEM(states, F32)]
        + [pltpu.VMEM(wide, F32)] * 4
        + [pltpu.VMEM(small, F32)] * 2
        + [pltpu.VMEM(pair, F32), pltpu.VMEM(back, F32), dma((blocks,)), dma],
    )
    first = lax.all_to_all(first, "col", 0, 0, tiled=True)
    back_ends = lax.all_gather(back_ends, "row")
    (second,) = call(
        key_kernel,
        [pltpu.HBM(pair, F32)],
        (*where, own, features, peak, backs, back_ends),
        2,
        [pltpu.VMEM(wide, F32), pltpu.VMEM((CHAINS, M, D), F32), pltpu.VMEM(small, F32)]
        + [pltpu.VMEM(wide, F32), pltpu.VMEM(pair, F32), dma((blocks,))],
    )
    second = lax.all_to_all(second, "col", 0, 0, tiled=True)
    narrow = [jax.ShapeDtypeStruct((rows, width), BF16)] * 2
    outs = (*call(unpack_kernel, narrow, (first,)), *call(unpack_kernel, narrow, (second,)))
    return tuple(a.reshape(1, rows, width) for a in outs)


def solution(mesh):
    groups, seq = mesh.devices.shape
    fine = Mesh(mesh.devices.reshape(groups, seq // H, H), ("grp", "row", "col"))
    rows = P("grp", ("row", "col"), None)
    return jax.shard_map(
        on_device,
        mesh=fine,
        in_specs=(rows, rows, rows, rows, P(), P("grp", None)),
        out_specs=(rows, rows, rows, rows),
        check_vma=False,
    )
```

```python
import jax
import jax.numpy as jnp
from jax import lax
from jax.experimental import pallas as pl
from jax.experimental.pallas import tpu as pltpu
from jax.sharding import Mesh
from jax.sharding import PartitionSpec as P

H = 8
D = 128
M = 128
CHAINS = 4
EPS = 1e-06
SCALE = D ** (-0.25)
RATIO = M ** (-0.5)
F32 = jnp.float32
BF16 = jnp.bfloat16
NN = (((1,), (0,)), ((), ()))
NT = (((1,), (1,)), ((), ()))
TN = (((0,), (0,)), ((), ()))
K, V, Q, G = range(4)
OUT, GQ = range(2)
GK, GV = range(2)
VALUES, TOTALS, PEAK = M, M + 1, M + 2


def dot(a, b, dims):
    return lax.dot_general(a, b, dims, preferred_element_type=F32)


def split(x):
    hi = x.astype(BF16)
    return hi, (x - hi.astype(F32)).astype(BF16)


def split3(x):
    hi = x.astype(BF16)
    rest = x - hi.astype(F32)
    mid = rest.astype(BF16)
    return hi, mid, (rest - mid.astype(F32)).astype(BF16)


def dot3(a, b, dims):
    (ah, al), (bh, bl) = a, b
    return dot(ah, bh, dims) + (dot(ah, bl, dims) + dot(al, bh, dims))


def head(h):
    return slice(h * D, (h + 1) * D)


def logits_of(x, parts):
    f1, f2, f3 = parts
    y = x.astype(BF16)
    z = dot(y, f1, NT) + (dot(y, f2, NT) + dot(y, f3, NT))
    return SCALE * z - (0.5 * SCALE * SCALE) * jnp.sum(x * x, axis=1, keepdims=True)


class Chains:
    def __init__(self, lens, me, blocks, rows):
        self.rows = rows
        self.span = blocks * rows
        self.me = me
        l0, l1, l2 = lens[0, 0], lens[0, 1], lens[0, 2]
        self.starts = (jnp.int32(0), l0, l0 + l1, l0 + l1 + l2)
        self.lens = lens

    def count_ended(self, position):
        c = jnp.int32(0)
        for s in self.starts[1:]:
            c = c + (position >= s).astype(jnp.int32)
        return c

    def ends_of(self, which):
        return self.count_ended(which * self.span), self.count_ended((which + 1) * self.span - 1)

    def start_of(self, c):
        s = self.starts
        return jnp.where(c == 0, s[0], jnp.where(c == 1, s[1], jnp.where(c == 2, s[2], s[3])))

    def mask(self, c, block):
        low = self.start_of(c) - (self.me * self.span + block * self.rows)
        at = lax.broadcasted_iota(jnp.int32, (self.rows, D), 0)
        return (at >= low) & (at < low + self.lens[0, c])


def pack_kernel(k_hbm, v_hbm, q_hbm, g_hbm, out_hbm, rows_ref, wide_ref, in_sem, out_sem):
    sources = (k_hbm, v_hbm, q_hbm, g_hbm)
    loads = [pltpu.make_async_copy(r, rows_ref.at[i], in_sem.at[i]) for i, r in enumerate(sources)]
    for load in loads:
        load.start()
    for load in loads:
        load.wait()
    stores = [pltpu.make_async_copy(wide_ref.at[h], out_hbm.at[h], out_sem.at[h]) for h in range(H)]
    for h in range(H):
        for i in range(4):
            wide_ref[h, i] = rows_ref[i, :, head(h)].astype(F32)
        stores[h].start()
    for store in stores:
        store.wait()


def state_kernel(
    lens, place, all_ref, f_ref, z_hbm, s_ref, send_hbm, er_ref, send_ref, z_ref, sem, z_sem
):
    blocks, _, rows, _ = all_ref.shape
    chains = Chains(lens, place[0], blocks, rows)
    parts = split3(f_ref[...])
    peak = jnp.full((1, 1), -jnp.inf, F32)
    for b in range(blocks):
        logits = logits_of(all_ref[b, K], parts)
        er_ref[b] = logits
        peak = jnp.maximum(peak, jnp.max(logits, axis=(0, 1), keepdims=True))
    for b in range(blocks):
        er_ref[b] = jnp.exp(er_ref[b] - peak)
    for i in range(z_ref.shape[0]):
        z_ref[i] = jnp.broadcast_to(peak, z_ref.shape[1:])
    z_store = pltpu.make_async_copy(z_ref, z_hbm, z_sem)
    z_store.start()
    s_ref[...] = jnp.zeros_like(s_ref)
    for c in range(CHAINS):
        s_ref[c, PEAK : PEAK + 1, :] = jnp.broadcast_to(peak, (1, D))
    low, high = chains.ends_of(chains.me)

    def one(c, carry):
        state = jnp.zeros((M, D), F32)
        values = jnp.zeros((rows, D), F32)
        totals = jnp.zeros((rows, M), F32)
        for b in range(blocks):
            mask = chains.mask(c, b)
            raised = jnp.where(mask, er_ref[b], 0.0)
            totals = totals + raised
            hi, lo = split(raised)
            v = all_ref[b, V]
            values = values + jnp.where(mask, v, 0.0)
            v = v.astype(BF16)
            state = state + (dot(hi, v, TN) + dot(lo, v, TN))
        s_ref[c, :M, :] = state
        s_ref[c, VALUES : VALUES + 1, :] = jnp.sum(values, axis=0, keepdims=True)
        s_ref[c, TOTALS : TOTALS + 1, :] = jnp.sum(totals, axis=0, keepdims=True)
        return carry

    lax.fori_loop(low, high + 1, one, 0)
    send_ref[0] = s_ref[low]
    send_ref[1] = s_ref[high] * (high != low).astype(F32)
    store = pltpu.make_async_copy(send_ref, send_hbm, sem)
    store.start()
    z_store.wait()
    store.wait()


def query_kernel(
    lens, place, all_ref, f_ref, z_ref, s_ref, sent_ref,
    res_hbm, send_hbm, b_ref, peak_ref,
    qr_ref, full_ref, num_ref, gs_ref, inv_ref, tr_ref, t_ref, bt_ref, res_ref, send_ref, res_sem, send_sem,
):
    blocks, _, rows, _ = all_ref.shape
    chains = Chains(lens, place[0], blocks, rows)
    parts = split3(f_ref[...])
    for b in range(blocks):
        ql = logits_of(all_ref[b, Q], parts)
        qr_ref[b] = jnp.exp(ql - jnp.max(ql, axis=1, keepdims=True)) * RATIO
    peak = jnp.max(jnp.max(z_ref[...], axis=0), axis=0, keepdims=True)
    peak_ref[...] = jnp.broadcast_to(peak, peak_ref.shape)
    row = lax.broadcasted_iota(jnp.int32, (M + 8, D), 0)
    share = jnp.where(row == VALUES, 1.0, jnp.exp(s_ref[0, PEAK : PEAK + 1, :] - peak))
    for c in range(CHAINS):
        full_ref[c] = s_ref[c] * share
    for r in range(sent_ref.shape[0]):
        ends = chains.ends_of(r)

        @pl.when(chains.me != r)
        def _():
            share = jnp.where(row == VALUES, 1.0, jnp.exp(sent_ref[r, 0, PEAK : PEAK + 1, :] - peak))
            for i, c in enumerate(ends):
                full_ref[c] += sent_ref[r, i] * share

    for c in range(CHAINS):
        count = lens[0, c].astype(F32)
        t_ref[c : c + 1, :] = RATIO * (full_ref[c, TOTALS : TOTALS + 1, :] + EPS * count)
    b_ref[...] = jnp.zeros_like(b_ref)
    low, high = chains.ends_of(chains.me)

    def one(c, carry):
        state = RATIO * (full_ref[c, :M, :] + EPS * full_ref[c, VALUES : VALUES + 1, :])
        state = split(state)
        weights = t_ref[pl.ds(c, 1), :]
        back = jnp.zeros((M, D), F32)
        for b in range(blocks):
            mask = chains.mask(c, b)
            qf = qr_ref[b] + EPS * RATIO
            inv = 1.0 / jnp.sum(qf * weights, axis=1, keepdims=True)
            inv_ref[b] = jnp.where(mask, inv, inv_ref[b])
            tr_ref[b] = jnp.where(mask, weights, tr_ref[b])
            num = dot3(split(qf), state, NN)
            num_ref[b] = jnp.where(mask, num, num_ref[b])
            g = all_ref[b, G].astype(BF16)
            gs = dot(g, state[0], NT) + dot(g, state[1], NT)
            gs_ref[b] = jnp.where(mask, gs, gs_ref[b])
            hi, lo = split(jnp.where(mask, qf * inv, 0.0))
            back = back + (dot(hi, g, TN) + dot(lo, g, TN))
        b_ref[c] = back
        return carry

    lax.fori_loop(low, high + 1, one, 0)
    feats = parts[:2]
    stores = [pltpu.make_async_copy(res_ref.at[b], res_hbm.at[b], res_sem.at[b]) for b in range(blocks)]
    for b in range(blocks):
        inv = inv_ref[b]
        exact = num_ref[b] * inv
        res_ref[b, OUT] = exact
        grad_denom = -jnp.sum(all_ref[b, G] * exact, axis=1, keepdims=True) * inv
        raised = qr_ref[b]
        num_ref[b] = (raised + EPS * RATIO) * grad_denom
        grad_logits = (gs_ref[b] * inv + grad_denom * tr_ref[b]) * raised
        back = dot3(split(grad_logits), feats, NN)
        back = back - jnp.sum(grad_logits, axis=1, keepdims=True) * (SCALE * all_ref[b, Q])
        res_ref[b, GQ] = back * SCALE
        stores[b].start()
    bt_ref[...] = jnp.zeros_like(bt_ref)

    def two(c, carry):
        total = jnp.zeros((rows, M), F32)
        for b in range(blocks):
            total = total + jnp.where(chains.mask(c, b), num_ref[b], 0.0)
        bt_ref[pl.ds(c, 1), :] = jnp.sum(total, axis=0, keepdims=True)
        return carry

    lax.fori_loop(low, high + 1, two, 0)
    send_ref[0:M, :] = b_ref[low]
    send_ref[M : 2 * M, :] = b_ref[high] * (high != low).astype(F32)
    send_ref[2 * M :, :] = bt_ref[...]
    store = pltpu.make_async_copy(send_ref, send_hbm, send_sem)
    store.start()
    for one_store in stores:
        one_store.wait()
    store.wait()


def key_kernel(
    lens, place, all_ref, f_ref, peak_ref, b_ref, sent_ref,
    res_hbm, kr_ref, full_ref, sum_ref, dk_ref, res_ref, res_sem,
):
    blocks, _, rows, _ = all_ref.shape
    chains = Chains(lens, place[0], blocks, rows)
    parts = split3(f_ref[...])
    peak = peak_ref[0:1, :]
    for b in range(blocks):
        kr_ref[b] = jnp.exp(logits_of(all_ref[b, K], parts) - peak) * RATIO
    full_ref[...] = b_ref[...]
    for r in range(sent_ref.shape[0]):
        low, high = chains.ends_of(r)

        @pl.when(chains.me != r)
        def _():
            full_ref[low] += sent_ref[r, :M, :]
            full_ref[high] += sent_ref[r, M : 2 * M, :]

    sum_ref[...] = jnp.sum(sent_ref[:, 2 * M :, :], axis=0)
    low, high = chains.ends_of(chains.me)

    def one(c, carry):
        back = split(full_ref[c])
        total = sum_ref[pl.ds(c, 1), :]
        for b in range(blocks):
            mask = chains.mask(c, b)
            dv = dot3(split(kr_ref[b] + EPS * RATIO), back, NN)
            res_ref[b, GV] = jnp.where(mask, dv, res_ref[b, GV])
            v = all_ref[b, V].astype(BF16)
            dk = dot(v, back[0], NT) + dot(v, back[1], NT) + total
            dk_ref[b] = jnp.where(mask, dk, dk_ref[b])
        return carry

    lax.fori_loop(low, high + 1, one, 0)
    feats = parts[:2]
    stores = [pltpu.make_async_copy(res_ref.at[b], res_hbm.at[b], res_sem.at[b]) for b in range(blocks)]
    for b in range(blocks):
        grad_logits = dk_ref[b] * kr_ref[b]
        back = dot3(split(grad_logits), feats, NN)
        back = back - jnp.sum(grad_logits, axis=1, keepdims=True) * (SCALE * all_ref[b, K])
        res_ref[b, GK] = back * SCALE
        stores[b].start()
    for store in stores:
        store.wait()


def unpack_kernel(res_ref, *outs):
    for h in range(H):
        for i, out in enumerate(outs):
            out[:, head(h)] = res_ref[h, i].astype(BF16)


def is_hbm(shape):
    return getattr(shape, "memory_space", None) is pltpu.HBM


def call(kernel, shapes, args, scalars=0, scratch=()):
    vmem = pl.BlockSpec(memory_space=pltpu.VMEM)
    smem = pl.BlockSpec(memory_space=pltpu.SMEM)
    hbm = pl.BlockSpec(memory_space=pltpu.HBM)
    return pl.pallas_call(
        kernel,
        out_shape=shapes,
        in_specs=[smem] * scalars + [vmem] * (len(args) - scalars),
        out_specs=[hbm if is_hbm(a) else vmem for a in shapes],
        scratch_shapes=list(scratch),
        compiler_params=pltpu.CompilerParams(vmem_limit_bytes=40 * 2**20),
    )(*args)


def f32(*shape):
    return jax.ShapeDtypeStruct(shape, F32)


def on_device(queries, keys, values, grad_attended, features, chain_lengths):
    rows, width = queries.shape[1:]
    q, k, v, g = (a.reshape(rows, width) for a in (queries, keys, values, grad_attended))
    place = jnp.stack([lax.axis_index("row"), lax.axis_index("col")]).astype(jnp.int32)
    where = (chain_lengths, place)
    groups, lines, blocks = (lax.axis_size(a) for a in ("grp", "row", "col"))
    wide = (blocks, rows, D)
    hbm = pl.BlockSpec(memory_space=pltpu.HBM)
    packed = pl.pallas_call(
        pack_kernel,
        out_shape=f32(H, 4, rows, D),
        in_specs=[hbm] * 4,
        out_specs=hbm,
        scratch_shapes=[
            pltpu.VMEM((4, rows, width), BF16),
            pltpu.VMEM((H, 4, rows, D), F32),
            pltpu.SemaphoreType.DMA((4,)),
            pltpu.SemaphoreType.DMA((H,)),
        ],
        compiler_params=pltpu.CompilerParams(vmem_limit_bytes=60 * 2**20),
    )(k, v, q, g)
    own = lax.all_to_all(packed, "col", 0, 0, tiled=True)
    states = (CHAINS, M + 8, D)
    peers = (groups * lines, 1, M)
    dma = pltpu.SemaphoreType.DMA
    peaks, own_states, ends = call(
        state_kernel,
        [pltpu.HBM(peers, F32), pltpu.VMEM(states, F32), pltpu.HBM((2, M + 8, D), F32)],
        (*where, own, features),
        2,
        [pltpu.VMEM(wide, F32), pltpu.VMEM((2, M + 8, D), F32), pltpu.VMEM(peers, F32), dma, dma],
    )
    peaks = lax.all_to_all(peaks, ("grp", "row"), 0, 0, tiled=True)
    ends = lax.all_gather(ends, "row")
    pair = (blocks, 2, rows, D)
    back = (2 * M + 2 * CHAINS, D)
    small = (2 * CHAINS, M)
    first, back_ends, backs, peak = call(
        query_kernel,
        [pltpu.HBM(pair, F32), pltpu.HBM(back, F32), pltpu.VMEM((CHAINS, M, D), F32), f32(*small)],
        (*where, own, features, peaks, own_states, ends),
        2,
        [pltpu.VMEM(wide, F32), pltpu.VMEM(states, F32)]
        + [pltpu.VMEM(wide, F32)] * 4
        + [pltpu.VMEM(small, F32)] * 2
        + [pltpu.VMEM(pair, F32), pltpu.VMEM(back, F32), dma((blocks,)), dma],
    )
    first = lax.all_to_all(first, "col", 0, 0, tiled=True)
    back_ends = lax.all_gather(back_ends, "row")
    (second,) = call(
        key_kernel,
        [pltpu.HBM(pair, F32)],
        (*where, own, features, peak, backs, back_ends),
        2,
        [pltpu.VMEM(wide, F32), pltpu.VMEM((CHAINS, M, D), F32), pltpu.VMEM(small, F32)]
        + [pltpu.VMEM(wide, F32), pltpu.VMEM(pair, F32), dma((blocks,))],
    )
    second = lax.all_to_all(second, "col", 0, 0, tiled=True)
    narrow = [jax.ShapeDtypeStruct((rows, width), BF16)] * 2
    outs = (*call(unpack_kernel, narrow, (first,)), *call(unpack_kernel, narrow, (second,)))
    return tuple(a.reshape(1, rows, width) for a in outs)


def solution(mesh):
    groups, seq = mesh.devices.shape
    fine = Mesh(mesh.devices.reshape(groups, seq // H, H), ("grp", "row", "col"))
    rows = P("grp", ("row", "col"), None)
    return jax.shard_map(
        on_device,
        mesh=fine,
        in_specs=(rows, rows, rows, rows, P(), P("grp", None)),
        out_specs=(rows, rows, rows, rows),
        check_vma=False,
    )
```
